32 devices in a mesh: tm: 8 (over z, x), seq: 2 (over y), mp: 2 (over core).
Axes of the slice: x: 2, y: 2, z: 4, core: 2. Of those that a mesh axis runs over, the one named last changes fastest.
Arguments:
- student_q: bfloat16 [2, 1024, 5120], P('seq', 'tm', 'mp'), may hold values from -110 to 110
- student_k: bfloat16 [2, 1024, 5120], P('seq', 'tm', 'mp'), may hold values from -6 to 6
- student_v: bfloat16 [2, 1024, 5120], P('seq', 'tm', 'mp'), may hold values from -6 to 6
- teacher_q: bfloat16 [2, 1024, 5120], P('seq', 'tm', 'mp'), may hold values from -110 to 110
- teacher_k: bfloat16 [2, 1024, 5120], P('seq', 'tm', 'mp'), may hold values from -6 to 6
- stagger: int32 [2], P('seq'), may hold values from 0 to 4, as said below
- clip_lengths: int32 [2, 3], P('seq'), may hold values from 1 to 5, 8 in all within a row
Outputs:
- generated: bfloat16 [2, 1024, 5120], P('seq', 'tm', 'mp')
- score_rows: bfloat16 [2, 1024, 5120], P('seq', 'tm', 'mp')
The draws below stay inside these ranges and needn't reach their ends.
Inputs may be any that keep to these rules, and one draw needn't show every extreme that they name: `clip_lengths`: the lengths of each video sum to 8, and some clip has 5 blocks. `stagger`: some video has the value 8 // 2.
All inputs are finite; a program needn't handle non-finite values.
Results may differ from the reference program's by a relative error of at most 0.007.
Values may be sent and summed in bfloat16 or wider, within the bound.
No kernel may reach another device: no remote copies, remote signals or barrier semaphores. Data moves between devices by JAX's collectives and lax.ppermute only.
A program may use at most 64 MiB of HBM per device.

```python
import math
import jax
import jax.numpy as jnp
import numpy as np
from jax import lax

HEADS = 40
HD = 128
TOK = 128
CLIPS = 3
BLOCKS = 8
VIDEOS = 2
F = 5120


def pair_draw(key, salt):
    base = jax.random.fold_in(key, salt)
    query_key, key_key = jax.random.split(base)
    shape = (VIDEOS, BLOCKS * TOK, HEADS * HD)
    queries = jnp.clip(jax.random.normal(query_key, shape, jnp.float32), -6.0, 6.0)
    keys = jnp.clip(jax.random.normal(key_key, shape, jnp.float32), -6.0, 6.0)
    return (queries, keys)


def draw_student_q(key, part):
    return pair_draw(key, 11)[0].astype(jnp.bfloat16)


def draw_student_k(key, part):
    return pair_draw(key, 11)[1].astype(jnp.bfloat16)


def draw_teacher_q(key, part):
    return pair_draw(key, 23)[0].astype(jnp.bfloat16)


def draw_teacher_k(key, part):
    return pair_draw(key, 23)[1].astype(jnp.bfloat16)


def draw_stagger(key, part):
    value_key, place_key = jax.random.split(jax.random.fold_in(key, 37))
    values = jax.random.randint(value_key, (VIDEOS,), 0, BLOCKS // 2 + 1).astype(jnp.int32)
    place = jax.random.randint(place_key, (), 0, VIDEOS).astype(jnp.int32)
    return jnp.where(jnp.arange(VIDEOS, dtype=jnp.int32) == place, jnp.int32(BLOCKS // 2), values).astype(jnp.int32)


def steps_of(stream_key, extent, cuts, low, largest):
    level = 1.0
    for axis_at, parts in cuts:
        steps = jax.random.uniform(jax.random.fold_in(jax.random.fold_in(stream_key, 6), axis_at), (parts,), jnp.float32, low / len(cuts), largest / len(cuts))
        level = level * jnp.repeat(jnp.exp(steps), extent[axis_at] // parts).reshape((-1,) + (1,) * (len(extent) - 1 - axis_at))
    return level


def split_up(number_of, total, reach, lean):
    portions = [(1 << 20) // math.isqrt(rank ** lean) + 1 for rank in range(2, number_of + 1)]
    surplus, counts = total - reach - (number_of - 1), [1] * (number_of - 1)
    while surplus > 0:
        free = [i for i in range(number_of - 1) if counts[i] < reach]
        whole, budget = sum([portions[i] for i in free]), surplus
        for i in free:
            more = min(reach - counts[i], max(1, budget * portions[i] // whole), surplus)
            counts[i] = counts[i] + more
            surplus = surplus - more
    return np.array([reach] + counts)


def ragged_sizes(stream_key, count, total, limit, skew):
    if count == 2:
        one = jax.random.randint(stream_key, (), max(1, total - limit), min(limit, total - 1) + 1)
        return jnp.stack([one, total - one])
    lengths = jnp.asarray(split_up(count, total, limit, skew), jnp.int32)
    couples = (count - 1) // 2
    giver, sink = lengths[1:1 + 2 * couples:2], lengths[2:2 + 2 * couples:2]
    margin = jnp.minimum(giver - 1, limit - sink)
    moved = jax.random.randint(jax.random.fold_in(stream_key, 1), (couples,), 0, 1 << 20) % (margin + 1)
    lengths = lengths.at[1:1 + 2 * couples:2].set(giver - moved).at[2:2 + 2 * couples:2].set(sink + moved)
    return lengths[jax.random.permutation(jax.random.fold_in(stream_key, 2), count)]


def centred(rng, shape, deviation, limit, pieces=(), kind=jnp.bfloat16):
    entries = jax.random.normal(rng, shape, jnp.float32) * deviation
    if len(pieces) > 0:
        entries = steps_of(rng, shape, pieces, -0.22, 0.18) * entries
    return jnp.clip(entries, min=-limit, max=limit).astype(kind)


def setup_inputs(seed: int = 0) -> dict:
    key_list = jax.random.split(jax.random.key(seed), 8)
    return {
        "student_q": draw_student_q(jax.random.fold_in(key_list[7], 71), 0),
        "student_k": draw_student_k(jax.random.fold_in(key_list[7], 71), 0),
        "student_v": centred(key_list[2], (VIDEOS, BLOCKS * TOK, F), 1.0, 6.0, ((0, 2), (1, 8), (2, 2))),
        "teacher_q": draw_teacher_q(jax.random.fold_in(key_list[7], 71), 0),
        "teacher_k": draw_teacher_k(jax.random.fold_in(key_list[7], 71), 0),
        "stagger": draw_stagger(jax.random.fold_in(key_list[7], 71), 0),
        "clip_lengths": jax.vmap(lambda own: ragged_sizes(own, CLIPS, BLOCKS, BLOCKS // 2 + 1, 0))(jax.random.split(key_list[6], VIDEOS)).reshape((VIDEOS, CLIPS)).astype(jnp.int32),
    }


negative = -1e+30

def attend_rule(queries, keys, values, allowed):
    rows = queries.shape[0]
    qh = queries.astype(jnp.float32).reshape(rows, HEADS, HD)
    kh = keys.astype(jnp.float32).reshape(rows, HEADS, HD)
    vh = values.astype(jnp.float32).reshape(rows, HEADS, HD)
    scores = jnp.einsum('qhd,khd->hqk', qh, kh) / math.sqrt(HD)
    scores = jnp.where(allowed[None], scores, negative)
    top = lax.optimization_barrier(jnp.max(scores, axis=-1))
    weights = jnp.where(allowed[None], jnp.exp(scores - top[..., None]), 0.0)
    total = lax.optimization_barrier(jnp.sum(weights, axis=-1))
    rounded = weights.astype(jnp.bfloat16).astype(jnp.float32)
    mixed = jnp.einsum('hqk,khd->qhd', rounded, vh)
    mixed = mixed / jnp.transpose(total)[..., None]
    return mixed.reshape(rows, HEADS * HD)

def one_video(packed_tokens):
    student_query_rows, student_key_rows, student_value_rows, teacher_query_rows, teacher_key_rows, opening_block, clip_length_list = packed_tokens
    block = (jnp.arange(BLOCKS * TOK) // TOK).astype(jnp.int32)
    student_block_mask = (block[None, :] == block[:, None]) | (block[None, :] >= opening_block) & (block[None, :] < block[:, None])
    generated = attend_rule(student_query_rows, student_key_rows, student_value_rows, student_block_mask).astype(jnp.bfloat16)
    running = jnp.cumsum(clip_length_list)
    clip = lax.optimization_barrier(jnp.sum((running[None, :] <= block[:, None]).astype(jnp.int32), axis=1))
    teacher_mask = clip[:, None] == clip[None, :]
    teacher_out = attend_rule(teacher_query_rows, teacher_key_rows, generated, teacher_mask)
    score_rows = (teacher_out - generated.astype(jnp.float32)).astype(jnp.bfloat16)
    return (generated, score_rows)

def reference(student_q, student_k, student_v, teacher_q, teacher_k, stagger, clip_lengths):
    return lax.map(one_video, (student_q, student_k, student_v, teacher_q, teacher_k, stagger, clip_lengths))
```

```python
import functools
import math

import jax
import jax.numpy as jnp
from jax import lax
from jax.experimental import pallas as pl
from jax.experimental.pallas import tpu as pltpu
from jax.sharding import PartitionSpec as P

HD = 128
TOK = 128
NEG = -1e30
RATE = math.log2(math.e) / math.sqrt(HD)


def head_table(peers, heads):
    slots = -(-heads // peers)
    full = heads // peers
    rest = heads - full * peers
    table = [[s * peers + p for s in range(full)] for p in range(peers)]
    if rest:
        for p in range(peers):
            table[p].append(full * peers + p * rest // peers)
    return table, slots


def soft(scores, bias):
    scores = scores + bias
    top = jnp.max(scores, axis=-1, keepdims=True)
    weights = jnp.exp2((scores - top) * RATE)
    total = jnp.sum(weights, axis=-1, keepdims=True)
    return weights.astype(jnp.bfloat16), total


def attend(q, k, v, bias):
    scores = lax.dot_general(q, k, (((1,), (1,)), ((), ())), preferred_element_type=jnp.float32)
    weights, total = soft(scores, bias)
    mixed = jnp.dot(weights, v, preferred_element_type=jnp.float32)
    return mixed / total


def kernel(blocks, reach, first_ref, clip_ref, x_ref, o_ref):
    first = first_ref[0]
    for i in range(blocks):
        width = (i + 1) * TOK
        block = lax.broadcasted_iota(jnp.int32, (1, width), 1) // TOK
        bias = jnp.where((block >= first) | (block == i), 0.0, NEG)
        k = x_ref[0 : i + 1, 0, 1].reshape(width, HD)
        v = x_ref[0 : i + 1, 0, 2].reshape(width, HD)
        o_ref[i, 0, 0] = attend(x_ref[i, 0, 0], k, v, bias).astype(jnp.bfloat16)
    width = reach * TOK
    offset = lax.broadcasted_iota(jnp.int32, (1, width), 1) // TOK

    def teacher(i, carry):
        low = clip_ref[0, i]
        high = clip_ref[1, i]
        start = jnp.minimum(low, blocks - reach)
        block = offset + start
        bias = jnp.where((block >= low) & (block < high), 0.0, NEG)
        k = x_ref[pl.ds(start, reach), 0, 4].reshape(width, HD)
        v = o_ref[pl.ds(start, reach), 0, 0].reshape(width, HD)
        out = attend(x_ref[i, 0, 3], k, v, bias)
        o_ref[i, 0, 1] = (out - o_ref[i, 0, 0].astype(jnp.float32)).astype(jnp.bfloat16)
        return carry

    lax.fori_loop(0, blocks, teacher, 0)


def both_attentions(first, clips, arrived):
    blocks, slots = arrived.shape[:2]
    reach = blocks // 2 + 1
    return pl.pallas_call(
        functools.partial(kernel, blocks, reach),
        grid_spec=pltpu.PrefetchScalarGridSpec(
            num_scalar_prefetch=2,
            grid=(slots,),
            in_specs=[pl.BlockSpec((blocks, 1, 5, TOK, HD), lambda s, *_: (0, s, 0, 0, 0))],
            out_specs=pl.BlockSpec((blocks, 1, 2, TOK, HD), lambda s, *_: (0, s, 0, 0, 0)),
        ),
        out_shape=jax.ShapeDtypeStruct((blocks, slots, 2, TOK, HD), jnp.bfloat16),
        compiler_params=pltpu.CompilerParams(vmem_limit_bytes=32 * 2**20),
        cost_estimate=pl.CostEstimate(
            flops=slots * blocks * blocks * 4 * TOK * TOK * HD,
            bytes_accessed=slots * blocks * 7 * TOK * HD * 2,
            transcendentals=slots * blocks * blocks * TOK * TOK,
        ),
    )(first, clips, arrived)


def per_device(student_q, student_k, student_v, teacher_q, teacher_k, stagger, clip_lengths):
    heads = student_q.shape[2] // HD
    peers = lax.axis_size("tm")
    table, slots = head_table(peers, heads)
    running = jnp.cumsum(clip_lengths[0])
    block = jnp.arange(peers, dtype=jnp.int32)
    before = running[None, :] <= block[:, None]
    low = jnp.max(jnp.where(before, running[None, :], 0), axis=1)
    high = jnp.min(jnp.where(before, peers, running[None, :]), axis=1)
    clips = jnp.stack([low, high]).astype(jnp.int32)

    def by_head(x):
        return x[0].reshape(TOK, heads, HD)

    tensors = [by_head(x) for x in (student_q, student_k, student_v, teacher_q, teacher_k)]
    flat = [h for row in table for h in row]
    packed = jnp.stack(
        [jnp.stack([t[:, h] for t in tensors]) for h in flat]
    ).reshape(peers, slots, 5, TOK, HD)
    arrived = lax.all_to_all(packed, "tm", 0, 0)
    done = both_attentions(stagger, clips, arrived)
    back = lax.all_to_all(done, "tm", 0, 0)
    place = {}
    for p, row in enumerate(table):
        for s, h in enumerate(row):
            place.setdefault(h, (p, s))
    result = [
        jnp.concatenate([back[place[h][0], place[h][1], t] for h in range(heads)], axis=1)[None]
        for t in range(2)
    ]
    return tuple(result)


def solution(mesh):
    spec = P("seq", "tm", "mp")
    return jax.shard_map(
        per_device,
        mesh=mesh,
        in_specs=(spec,) * 5 + (P("seq"), P("seq", None)),
        out_specs=(spec, spec),
        check_vma=False,
    )
```

```python
import functools
import math

import jax
import jax.numpy as jnp
from jax import lax
from jax.experimental import pallas as pl
from jax.experimental.pallas import tpu as pltpu
from jax.sharding import PartitionSpec as P

HD = 128
TOK = 128
NEG = -1e30
RATE = math.log2(math.e) / math.sqrt(HD)
MIB = 2**20


def attend(q, k, v, bias):
    g = q.shape[0]
    scores = lax.dot_general(
        q.reshape(g * TOK, HD), k, (((1,), (1,)), ((), ())), preferred_element_type=jnp.float32
    )
    scores = scores.reshape(g, TOK, -1) + bias
    top = jnp.max(scores, axis=-1, keepdims=True)
    weights = jnp.exp2((scores - top) * RATE)
    total = jnp.sum(weights, axis=-1, keepdims=True)
    weights = weights.astype(jnp.bfloat16).reshape(g * TOK, -1)
    mixed = jnp.dot(weights, v, preferred_element_type=jnp.float32)
    return mixed.reshape(g, TOK, HD) / total


def student_head(blocks, first, x_ref, o_ref):
    for i in range(0, blocks, 2):
        width = (i + 2) * TOK
        block = lax.broadcasted_iota(jnp.int32, (2, 1, width), 2) // TOK
        own = lax.broadcasted_iota(jnp.int32, (2, 1, width), 0) + i
        bias = jnp.where((block == own) | (block >= first) & (block < own), 0.0, NEG)
        k = x_ref[0 : i + 2, 1].reshape(width, HD)
        v = x_ref[0 : i + 2, 2].reshape(width, HD)
        o_ref[i : i + 2, 0] = attend(x_ref[i : i + 2, 0], k, v, bias).astype(jnp.bfloat16)


def teacher_head(blocks, clip_ref, x_ref, gen, o_ref):
    reach = blocks // 2 + 1
    width = reach * TOK
    offset = lax.broadcasted_iota(jnp.int32, (1, 1, width), 2) // TOK
    for i in range(blocks):
        low = clip_ref[0, i]
        high = clip_ref[1, i]
        start = jnp.minimum(low, blocks - reach)
        block = offset + start
        bias = jnp.where((block >= low) & (block < high), 0.0, NEG)
        k = x_ref[pl.ds(start, reach), 1].reshape(width, HD)
        v = gen(pl.ds(start, reach)).reshape(width, HD)
        out = attend(x_ref[pl.ds(i, 1), 0], k, v, bias)
        o_ref[i, 0] = (out[0] - gen(i).astype(jnp.float32)).astype(jnp.bfloat16)


def cost(heads, blocks, units):
    return pl.CostEstimate(
        flops=heads * blocks * blocks * 4 * TOK * TOK * HD,
        bytes_accessed=units * blocks * TOK * HD * 2,
        transcendentals=heads * blocks * blocks * TOK * TOK,
    )


def pack(plans, tensors):
    plans = [plan for plan in plans if plan[0]]

    def body(*refs):
        for o_ref, plan in zip(refs[len(tensors) :], plans):
            for p, row in enumerate(plan):
                for u, (t, h) in enumerate(row):
                    o_ref[p, u] = refs[t][0, :, h * HD : (h + 1) * HD]

    return pl.pallas_call(
        body,
        out_shape=[
            jax.ShapeDtypeStruct((len(plan), len(plan[0]), TOK, HD), jnp.bfloat16)
            for plan in plans
        ],
        compiler_params=pltpu.CompilerParams(vmem_limit_bytes=16 * MIB),
        cost_estimate=cost(0, len(plans[0]), 2 * sum(len(plan[0]) for plan in plans)),
    )(*tensors)


def unpack(places, back):
    def body(x_ref, o_ref):
        for h, (p, u) in enumerate(places):
            o_ref[0, :, h * HD : (h + 1) * HD] = x_ref[p, u]

    return pl.pallas_call(
        body,
        out_shape=jax.ShapeDtypeStruct((1, TOK, len(places) * HD), jnp.bfloat16),
        compiler_params=pltpu.CompilerParams(vmem_limit_bytes=16 * MIB),
        cost_estimate=cost(0, 1, 2 * len(places)),
    )(back)


def student_kernel(full, blocks, first, role, arrived):
    def body(first_ref, role_ref, x_ref, o_ref):
        @pl.when((pl.program_id(0) < full) | (role_ref[0] == 1))
        def _():
            student_head(blocks, first_ref[0], x_ref, o_ref)

    steps = arrived.shape[1] // 3
    return pl.pallas_call(
        body,
        grid_spec=pltpu.PrefetchScalarGridSpec(
            num_scalar_prefetch=2,
            grid=(steps,),
            in_specs=[pl.BlockSpec((blocks, 3, TOK, HD), lambda s, *_: (0, s, 0, 0))],
            out_specs=pl.BlockSpec((blocks, 1, TOK, HD), lambda s, *_: (0, s, 0, 0)),
        ),
        out_shape=jax.ShapeDtypeStruct((blocks, steps, TOK, HD), jnp.bfloat16),
        compiler_params=pltpu.CompilerParams(vmem_limit_bytes=24 * MIB),
        cost_estimate=cost(steps, blocks, 4 * steps),
    )(first, role, arrived)


def teacher_kernel(full, blocks, clips, role, arrived, later, gen, shared):
    def body(clip_ref, role_ref, *refs):
        o_ref = refs[-1]
        step = pl.program_id(0)
        if full:

            @pl.when(step < full)
            def _():
                gen_ref = refs[1]
                teacher_head(blocks, clip_ref, refs[0], lambda at: gen_ref[at, 0], o_ref)

        if shared is not None:

            @pl.when((step == full) & (role_ref[0] == 2))
            def _():
                gen_ref = refs[-2]
                teacher_head(blocks, clip_ref, refs[-3], lambda at: gen_ref[at], o_ref)

    steps = full
    operands, specs = [], []
    if full:
        operands += [later, gen]
        specs += [
            pl.BlockSpec((blocks, 2, TOK, HD), lambda s, *_: (0, jnp.minimum(s, full - 1), 0, 0)),
            pl.BlockSpec((blocks, 1, TOK, HD), lambda s, *_: (0, jnp.minimum(s, full - 1), 0, 0)),
        ]
    if shared is not None:
        steps += 1
        operands += [arrived, shared]
        specs += [
            pl.BlockSpec((blocks, 3, TOK, HD), lambda s, *_: (0, full, 0, 0)),
            pl.BlockSpec((blocks, TOK, HD), lambda s, *_: (0, 0, 0)),
        ]
    return pl.pallas_call(
        body,
        grid_spec=pltpu.PrefetchScalarGridSpec(
            num_scalar_prefetch=2,
            grid=(steps,),
            in_specs=specs,
            out_specs=pl.BlockSpec((blocks, 1, TOK, HD), lambda s, *_: (0, s, 0, 0)),
        ),
        out_shape=jax.ShapeDtypeStruct((blocks, steps, TOK, HD), jnp.bfloat16),
        compiler_params=pltpu.CompilerParams(vmem_limit_bytes=24 * MIB),
        cost_estimate=cost(steps, blocks, 4 * steps),
    )(clips, role, *operands)


def per_device(student_q, student_k, student_v, teacher_q, teacher_k, stagger, clip_lengths):
    heads = student_q.shape[2] // HD
    peers = lax.axis_size("tm")
    full, rest = divmod(heads, peers)
    assert 2 * rest <= peers
    base = full * peers
    here = lax.axis_index("tm")
    role = jnp.where(here < 2 * rest, 1 + here % 2, 0).astype(jnp.int32)[None]
    running = jnp.cumsum(clip_lengths[0])
    block = jnp.arange(peers, dtype=jnp.int32)
    before = running[None, :] <= block[:, None]
    low = jnp.max(jnp.where(before, running[None, :], 0), axis=1)
    high = jnp.min(jnp.where(before, peers, running[None, :]), axis=1)
    clips = jnp.stack([low, high]).astype(jnp.int32)

    tensors = (student_q, student_k, student_v, teacher_q, teacher_k)
    plan, plan_later = [], []
    for p in range(peers):
        row = [(t, s * peers + p) for s in range(full) for t in (0, 1, 2)]
        if rest:
            h = base + min(p // 2, rest - 1)
            row += [(t, h) for t in ((3, 4, 4) if p % 2 else (0, 1, 2))]
        plan.append(row)
        plan_later.append([(t, s * peers + p) for s in range(full) for t in (3, 4)])

    packed = pack((plan, plan_later), tensors)
    arrived = lax.all_to_all(packed[0], "tm", 0, 0)
    later = lax.all_to_all(packed[1], "tm", 0, 0) if full else None
    gen = student_kernel(full, peers, stagger, role, arrived)
    shared = None
    if rest:
        shared = lax.ppermute(gen[:, full], "tm", [(2 * r, 2 * r + 1) for r in range(rest)])
    gen_back = lax.all_to_all(gen, "tm", 0, 0)
    score = teacher_kernel(full, peers, clips, role, arrived, later, gen, shared)
    score_back = lax.all_to_all(score, "tm", 0, 0)

    places = [
        [(h % peers, h // peers) for h in range(base)] + [(2 * r + which, full) for r in range(rest)]
        for which in (0, 1)
    ]
    return (unpack(places[0], gen_back), unpack(places[1], score_back))


def solution(mesh):
    spec = P("seq", "tm", "mp")
    return jax.shard_map(
        per_device,
        mesh=mesh,
        in_specs=(spec,) * 5 + (P("seq"), P("seq", None)),
        out_specs=(spec, spec),
        check_vma=False,
    )
```

```python
import functools
import math

import jax
import jax.numpy as jnp
from jax import lax
from jax.experimental import pallas as pl
from jax.experimental.pallas import tpu as pltpu
from jax.sharding import PartitionSpec as P

HD = 128
TOK = 128
NEG = -1e30
RATE = math.log2(math.e) / math.sqrt(HD)
MIB = 2**20


def attend(q, k, v, bias):
    g = q.shape[0]
    scores = lax.dot_general(
        q.reshape(g * TOK, HD), k, (((1,), (1,)), ((), ())), preferred_element_type=jnp.float32
    )
    scores = scores.reshape(g, TOK, -1) + bias
    top = jnp.max(scores, axis=-1, keepdims=True)
    weights = jnp.exp2((scores - top) * RATE)
    total = jnp.sum(weights, axis=-1, keepdims=True)
    weights = weights.astype(jnp.bfloat16).reshape(g * TOK, -1)
    mixed = jnp.dot(weights, v, preferred_element_type=jnp.float32)
    return mixed.reshape(g, TOK, HD) / total


def student_head(blocks, first, sources, o_ref):
    (q_ref, q_at), (k_ref, k_at), (v_ref, v_at) = sources
    for i in range(0, blocks, 2):
        width = (i + 2) * TOK
        block = lax.broadcasted_iota(jnp.int32, (2, 1, width), 2) // TOK
        own = lax.broadcasted_iota(jnp.int32, (2, 1, width), 0) + i
        bias = jnp.where((block == own) | (block >= first) & (block < own), 0.0, NEG)
        k = k_ref[0 : i + 2, k_at].reshape(width, HD)
        v = v_ref[0 : i + 2, v_at].reshape(width, HD)
        o_ref[i : i + 2, 0] = attend(q_ref[i : i + 2, q_at], k, v, bias).astype(jnp.bfloat16)


def teacher_head(blocks, clip_ref, sources, gen, o_ref, o_at):
    (q_ref, q_at), (k_ref, k_at) = sources
    reach = blocks // 2 + 1
    width = reach * TOK
    offset = lax.broadcasted_iota(jnp.int32, (1, 1, width), 2) // TOK
    for i in range(blocks):
        low = clip_ref[0, i]
        high = clip_ref[1, i]
        start = jnp.minimum(low, blocks - reach)
        block = offset + start
        bias = jnp.where((block >= low) & (block < high), 0.0, NEG)
        k = k_ref[pl.ds(start, reach), k_at].reshape(width, HD)
        v = gen(pl.ds(start, reach)).reshape(width, HD)
        out = attend(q_ref[pl.ds(i, 1), q_at], k, v, bias)
        o_ref[i, o_at] = (out[0] - gen(i).astype(jnp.float32)).astype(jnp.bfloat16)


def cost(heads, blocks, units):
    return pl.CostEstimate(
        flops=heads * blocks * blocks * 4 * TOK * TOK * HD,
        bytes_accessed=units * blocks * TOK * HD * 2,
        transcendentals=heads * blocks * blocks * TOK * TOK,
    )


def pack(plan, tensors):
    peers, units = len(plan), len(plan[0])

    def body(*refs):
        o_ref, sems = refs[-2:]
        copies = []
        for u in range(units):
            for p in range(peers):
                t, h = plan[p][u]
                source = refs[t].at[0, :, pl.ds(h * HD, HD)]
                copies.append(pltpu.make_async_copy(source, o_ref.at[p, u], sems.at[u, p]))
                copies[-1].start()
        for copy in copies:
            copy.wait()

    return pl.pallas_call(
        body,
        in_specs=[pl.BlockSpec(memory_space=pl.ANY)] * len(tensors),
        out_specs=pl.BlockSpec(memory_space=pl.ANY),
        out_shape=jax.ShapeDtypeStruct((peers, units, TOK, HD), jnp.bfloat16),
        scratch_shapes=[pltpu.SemaphoreType.DMA((units, peers))],
        compiler_params=pltpu.CompilerParams(vmem_limit_bytes=60 * MIB),
        cost_estimate=cost(0, peers, 2 * units),
    )(*tensors)


def unpack(places, back):
    def body(x_ref, *o_refs):
        for o_ref, place in zip(o_refs, places):
            for h, (p, u) in enumerate(place):
                o_ref[0, :, h * HD : (h + 1) * HD] = x_ref[p, u]

    width = len(places[0]) * HD
    return pl.pallas_call(
        body,
        out_shape=[jax.ShapeDtypeStruct((1, TOK, width), jnp.bfloat16) for _ in places],
        cost_estimate=cost(0, 1, 4 * len(places[0])),
    )(back)


def rest_student(blocks, first, role, arrived):
    def body(first_ref, role_ref, x_ref, o_ref):
        @pl.when(role_ref[0] == 1)
        def _():
            student_head(blocks, first_ref[0], [(x_ref, u) for u in range(3)], o_ref)

    return pl.pallas_call(
        body,
        grid_spec=pltpu.PrefetchScalarGridSpec(
            num_scalar_prefetch=2,
            grid=(1,),
            in_specs=[pl.BlockSpec((blocks, 3, TOK, HD), lambda s, *_: (0, 0, 0, 0))],
            out_specs=pl.BlockSpec((blocks, 1, TOK, HD), lambda s, *_: (0, 0, 0, 0)),
        ),
        out_shape=jax.ShapeDtypeStruct((blocks, 1, TOK, HD), jnp.bfloat16),
        cost_estimate=cost(1, blocks, 4),
    )(first, role, arrived)


def rest_teacher(blocks, unit, clips, role, arrived, gen, shared, results):
    def body(clip_ref, role_ref, x_ref, gen_ref, shared_ref, *refs):
        o_ref = refs[-1]

        @pl.when(role_ref[0] == 1)
        def _():
            o_ref[...] = gen_ref[...]

        @pl.when(role_ref[0] == 2)
        def _():
            sources = [(x_ref, u) for u in range(2)]
            teacher_head(blocks, clip_ref, sources, lambda at: shared_ref[at, 0], o_ref, 0)

    block = pl.BlockSpec((blocks, 1, TOK, HD), lambda s, *_: (0, 0, 0, 0))
    units = unit + 1
    operands = [arrived, gen, shared]
    specs = [pl.BlockSpec((blocks, 3, TOK, HD), lambda s, *_: (0, 0, 0, 0)), block, block]
    aliases = {}
    if results is not None:
        operands.append(results)
        specs.append(pl.BlockSpec(memory_space=pl.ANY))
        aliases = {5: 0}
    return pl.pallas_call(
        body,
        grid_spec=pltpu.PrefetchScalarGridSpec(
            num_scalar_prefetch=2,
            grid=(1,),
            in_specs=specs,
            out_specs=pl.BlockSpec((blocks, 1, TOK, HD), lambda s, *_: (0, unit, 0, 0)),
        ),
        out_shape=jax.ShapeDtypeStruct((blocks, units, TOK, HD), jnp.bfloat16),
        input_output_aliases=aliases,
        cost_estimate=cost(1, blocks, 5),
    )(clips, role, *operands)


def slot_kernel(blocks, slots, units, first, clips, arrived, offset, results):
    def body(first_ref, clip_ref, q_ref, k_ref, v_ref, tq_ref, tk_ref, *refs):
        o_ref = refs[-1]
        student_head(blocks, first_ref[0], [(r, 0) for r in (q_ref, k_ref, v_ref)], o_ref)
        sources = [(r, 0) for r in (tq_ref, tk_ref)]
        teacher_head(blocks, clip_ref, sources, lambda at: o_ref[at, 0], o_ref, 1)

    def at(t):
        return pl.BlockSpec((blocks, 1, TOK, HD), lambda s, *_: (0, offset + 5 * s + t, 0, 0))

    operands = [arrived] * 5
    specs = [at(t) for t in range(5)]
    aliases = {}
    if results is not None:
        operands.append(results)
        specs.append(pl.BlockSpec(memory_space=pl.ANY))
        aliases = {7: 0}
    return pl.pallas_call(
        body,
        grid_spec=pltpu.PrefetchScalarGridSpec(
            num_scalar_prefetch=2,
            grid=(len(slots),),
            in_specs=specs,
            out_specs=pl.BlockSpec(
                (blocks, 2, TOK, HD), lambda s, *_: (0, slots[0] + s, 0, 0)
            ),
        ),
        out_shape=jax.ShapeDtypeStruct((blocks, units, TOK, HD), jnp.bfloat16),
        input_output_aliases=aliases,
        cost_estimate=cost(2 * len(slots), blocks, 7 * len(slots)),
    )(first, clips, *operands)


def per_device(student_q, student_k, student_v, teacher_q, teacher_k, stagger, clip_lengths):
    heads = student_q.shape[2] // HD
    peers = lax.axis_size("tm")
    full, rest = divmod(heads, peers)
    assert rest and 2 * rest <= peers
    base = full * peers
    here = lax.axis_index("tm")
    role = jnp.where(here < 2 * rest, 1 + here % 2, 0).astype(jnp.int32)[None]
    running = jnp.cumsum(clip_lengths[0])
    block = jnp.arange(peers, dtype=jnp.int32)
    before = running[None, :] <= block[:, None]
    low = jnp.max(jnp.where(before, running[None, :], 0), axis=1)
    high = jnp.min(jnp.where(before, peers, running[None, :]), axis=1)
    clips = jnp.stack([low, high]).astype(jnp.int32)

    tensors = (student_q, student_k, student_v, teacher_q, teacher_k)
    early, late = tuple(range(full))[:-1], tuple(range(full))[-1:]
    plan, plan_late = [], []
    for p in range(peers):
        h = base + min(p // 2, rest - 1)
        row = [(t, h) for t in ((3, 4, 4) if p % 2 else (0, 1, 2))]
        plan.append(row + [(t, s * peers + p) for s in early for t in range(5)])
        plan_late.append([(t, s * peers + p) for s in late for t in range(5)])
    units = 2 * full + 1

    arrived = lax.all_to_all(pack(plan, tensors), "tm", 0, 0)
    arrived_late = None
    if late:
        arrived, packed_late = lax.optimization_barrier((arrived, pack(plan_late, tensors)))
        arrived_late = lax.all_to_all(packed_late, "tm", 0, 0)
    gen = rest_student(peers, stagger, role, arrived)
    shared = lax.ppermute(gen, "tm", [(2 * r, 2 * r + 1) for r in range(rest)])
    results = None
    if early:
        results = slot_kernel(peers, early, units, stagger, clips, arrived, 3, None)
    results = rest_teacher(peers, 2 * full, clips, role, arrived, gen, shared, results)
    if late:
        results = slot_kernel(peers, late, units, stagger, clips, arrived_late, 0, results)
    back = lax.all_to_all(results, "tm", 0, 0)
    return tuple(
        unpack(
            [
                [(h % peers, 2 * (h // peers) + which) for h in range(base)]
                + [(2 * r + which, 2 * full) for r in range(rest)]
                for which in (0, 1)
            ],
            back,
        )
    )


def solution(mesh):
    spec = P("seq", "tm", "mp")
    return jax.shard_map(
        per_device,
        mesh=mesh,
        in_specs=(spec,) * 5 + (P("seq"), P("seq", None)),
        out_specs=(spec, spec),
        check_vma=False,
    )
```

```python
import functools
import math

import jax
import jax.numpy as jnp
from jax import lax
from jax.experimental import pallas as pl
from jax.experimental.pallas import tpu as pltpu
from jax.sharding import PartitionSpec as P

HD = 128
TOK = 128
NEG = -1e30
RATE = math.log2(math.e) / math.sqrt(HD)
MIB = 2**20


def attend(q, k, v, bias):
    g = q.shape[0]
    scores = lax.dot_general(
        q.reshape(g * TOK, HD), k, (((1,), (1,)), ((), ())), preferred_element_type=jnp.float32
    )
    scores = scores.reshape(g, TOK, -1) + bias
    top = jnp.max(scores, axis=-1, keepdims=True)
    weights = jnp.exp2((scores - top) * RATE)
    total = jnp.sum(weights, axis=-1, keepdims=True)
    weights = weights.astype(jnp.bfloat16).reshape(g * TOK, -1)
    mixed = jnp.dot(weights, v, preferred_element_type=jnp.float32)
    return mixed.reshape(g, TOK, HD) / total


def student_head(pairs, first, sources, o_ref):
    (q_ref, q_at), (k_ref, k_at), (v_ref, v_at) = sources
    for i in pairs:
        width = (i + 2) * TOK
        block = lax.broadcasted_iota(jnp.int32, (2, 1, width), 2) // TOK
        own = lax.broadcasted_iota(jnp.int32, (2, 1, width), 0) + i
        bias = jnp.where((block == own) | (block >= first) & (block < own), 0.0, NEG)
        k = k_ref[0 : i + 2, k_at].reshape(width, HD)
        v = v_ref[0 : i + 2, v_at].reshape(width, HD)
        o_ref[i : i + 2, 0] = attend(q_ref[i : i + 2, q_at], k, v, bias).astype(jnp.bfloat16)


def teacher_head(blocks, rows, clip_ref, sources, gen, o_ref, o_at):
    (q_ref, q_at), (k_ref, k_at) = sources
    reach = blocks // 2 + 1
    width = reach * TOK
    offset = lax.broadcasted_iota(jnp.int32, (1, 1, width), 2) // TOK
    for i in rows:
        low = clip_ref[0, i]
        high = clip_ref[1, i]
        start = jnp.minimum(low, blocks - reach)
        block = offset + start
        bias = jnp.where((block >= low) & (block < high), 0.0, NEG)
        k = k_ref[pl.ds(start, reach), k_at].reshape(width, HD)
        v = gen(pl.ds(start, reach)).reshape(width, HD)
        out = attend(q_ref[pl.ds(i, 1), q_at], k, v, bias)
        o_ref[i, o_at] = (out[0] - gen(i).astype(jnp.float32)).astype(jnp.bfloat16)


def cost(heads, blocks, units):
    return pl.CostEstimate(
        flops=heads * blocks * blocks * 4 * TOK * TOK * HD,
        bytes_accessed=units * blocks * TOK * HD * 2,
        transcendentals=heads * blocks * blocks * TOK * TOK,
    )


def pack(plan, ranges, tensors):
    peers, units = len(plan), len(plan[0])
    widths = [count * HD for _, count in ranges]
    starts = [sum(widths[:r]) for r in range(len(ranges))]

    def place(h):
        for r, (head, count) in enumerate(ranges):
            if head <= h < head + count:
                return r, starts[r] + (h - head) * HD

    need = []
    for u in range(units):
        need.append(list(dict.fromkeys((plan[p][u][0], place(plan[p][u][1])[0]) for p in range(peers))))
    order = sorted(range(units), key=lambda u: (len(need[u]), u))
    fetch = list(dict.fromkeys(piece for u in order for piece in need[u]))

    def body(*refs):
        o_ref, rows, tiles, in_sem, out_sem = refs[len(tensors) :]
        copies = {}
        for n, (t, r) in enumerate(fetch):
            source = refs[t].at[0, :, pl.ds(ranges[r][0] * HD, widths[r])]
            target = rows.at[t, :, pl.ds(starts[r], widths[r])]
            copies[t, r] = pltpu.make_async_copy(source, target, in_sem.at[n])
            copies[t, r].start()
        sent = []
        for u in order:
            for piece in need[u]:
                if piece in copies:
                    copies.pop(piece).wait()
            for p in range(peers):
                t, h = plan[p][u]
                at = place(h)[1]
                tiles[p, u] = rows[t, :, at : at + HD]
            sent.append(pltpu.make_async_copy(tiles.at[:, u], o_ref.at[:, u], out_sem.at[u]))
            sent[-1].start()
        for copy in sent:
            copy.wait()

    return pl.pallas_call(
        body,
        in_specs=[pl.BlockSpec(memory_space=pl.ANY)] * len(tensors),
        out_specs=pl.BlockSpec(memory_space=pl.ANY),
        out_shape=jax.ShapeDtypeStruct((peers, units, TOK, HD), jnp.bfloat16),
        scratch_shapes=[
            pltpu.VMEM((len(tensors), TOK, sum(widths)), jnp.bfloat16),
            pltpu.VMEM((peers, units, TOK, HD), jnp.bfloat16),
            pltpu.SemaphoreType.DMA((len(fetch),)),
            pltpu.SemaphoreType.DMA((units,)),
        ],
        compiler_params=pltpu.CompilerParams(vmem_limit_bytes=60 * MIB),
        cost_estimate=cost(0, peers, 2 * units),
    )(*tensors)


def unpack(places, back):
    def body(x_ref, *o_refs):
        for o_ref, place in zip(o_refs, places):
            for h, (p, u) in enumerate(place):
                o_ref[0, :, h * HD : (h + 1) * HD] = x_ref[p, u]

    width = len(places[0]) * HD
    return pl.pallas_call(
        body,
        out_shape=[jax.ShapeDtypeStruct((1, TOK, width), jnp.bfloat16) for _ in places],
        compiler_params=pltpu.CompilerParams(vmem_limit_bytes=12 * MIB),
        cost_estimate=cost(0, 1, 4 * len(places[0])),
    )(back)


def rest_student(blocks, first, role, arrived):
    def body(first_ref, role_ref, x_ref, o_ref):
        @pl.when(role_ref[0] == 1)
        def _():
            student_head(range(0, blocks, 2), first_ref[0], [(x_ref, u) for u in range(3)], o_ref)

    return pl.pallas_call(
        body,
        grid_spec=pltpu.PrefetchScalarGridSpec(
            num_scalar_prefetch=2,
            grid=(1,),
            in_specs=[pl.BlockSpec((blocks, 3, TOK, HD), lambda s, *_: (0, 0, 0, 0))],
            out_specs=pl.BlockSpec((blocks, 1, TOK, HD), lambda s, *_: (0, 0, 0, 0)),
        ),
        out_shape=jax.ShapeDtypeStruct((blocks, 1, TOK, HD), jnp.bfloat16),
        compiler_params=pltpu.CompilerParams(vmem_limit_bytes=60 * MIB),
        cost_estimate=cost(1, blocks, 4),
    )(first, role, arrived)


def rest_teacher(blocks, unit, clips, role, arrived, gen, shared, results):
    def body(clip_ref, role_ref, x_ref, gen_ref, shared_ref, *refs):
        o_ref = refs[-1]

        @pl.when(role_ref[0] == 1)
        def _():
            o_ref[...] = gen_ref[...]

        @pl.when(role_ref[0] == 2)
        def _():
            sources = [(x_ref, u) for u in range(2)]
            teacher_head(blocks, range(blocks), clip_ref, sources, lambda at: shared_ref[at, 0], o_ref, 0)

    block = pl.BlockSpec((blocks, 1, TOK, HD), lambda s, *_: (0, 0, 0, 0))
    units = unit + 1
    operands = [arrived, gen, shared]
    specs = [pl.BlockSpec((blocks, 3, TOK, HD), lambda s, *_: (0, 0, 0, 0)), block, block]
    aliases = {}
    if results is not None:
        operands.append(results)
        specs.append(pl.BlockSpec(memory_space=pl.ANY))
        aliases = {5: 0}
    return pl.pallas_call(
        body,
        grid_spec=pltpu.PrefetchScalarGridSpec(
            num_scalar_prefetch=2,
            grid=(1,),
            in_specs=specs,
            out_specs=pl.BlockSpec((blocks, 1, TOK, HD), lambda s, *_: (0, unit, 0, 0)),
        ),
        out_shape=jax.ShapeDtypeStruct((blocks, units, TOK, HD), jnp.bfloat16),
        input_output_aliases=aliases,
        compiler_params=pltpu.CompilerParams(vmem_limit_bytes=60 * MIB),
        cost_estimate=cost(1, blocks, 5),
    )(clips, role, *operands)


def slot_kernel(blocks, slot, units, first, clips, arrived, offset, results):
    half = blocks // 2

    def body(first_ref, clip_ref, x_ref, *refs):
        o_ref, x, y, in_sem, out_sem = refs[-5:]

        def fetch(t, at, n):
            copy = pltpu.make_async_copy(
                x_ref.at[at, offset + t], x.at[at, t], in_sem.at[n]
            )
            copy.start()
            return copy

        def store(t, at, n):
            copy = pltpu.make_async_copy(
                y.at[at, t], o_ref.at[at, 2 * slot + t], out_sem.at[n]
            )
            copy.start()
            return copy

        lower, upper, whole = pl.ds(0, half), pl.ds(half, half), pl.ds(0, blocks)
        early = [fetch(t, lower, t) for t in range(3)]
        late = [fetch(t, upper, 3 + t) for t in range(3)]
        teacher = [fetch(t, whole, 3 + t) for t in (3, 4)]
        sources = [(x, t) for t in range(5)]
        for copy in early:
            copy.wait()
        student_head(range(0, half, 2), first_ref[0], sources[:3], y)
        for copy in late:
            copy.wait()
        student_head(range(half, blocks, 2), first_ref[0], sources[:3], y)
        sent = [store(0, whole, 0)]
        for copy in teacher:
            copy.wait()
        gen = lambda at: y[at, 0]
        teacher_head(blocks, range(half), clip_ref, sources[3:], gen, y, 1)
        sent.append(store(1, lower, 1))
        teacher_head(blocks, range(half, blocks), clip_ref, sources[3:], gen, y, 1)
        sent.append(store(1, upper, 2))
        for copy in sent:
            copy.wait()

    operands = [arrived]
    aliases = {}
    if results is not None:
        operands.append(results)
        aliases = {3: 0}
    return pl.pallas_call(
        body,
        in_specs=[pl.BlockSpec(memory_space=pltpu.SMEM)] * 2
        + [pl.BlockSpec(memory_space=pl.ANY)] * len(operands),
        out_specs=pl.BlockSpec(memory_space=pl.ANY),
        out_shape=jax.ShapeDtypeStruct((blocks, units, TOK, HD), jnp.bfloat16),
        scratch_shapes=[
            pltpu.VMEM((blocks, 5, TOK, HD), jnp.bfloat16),
            pltpu.VMEM((blocks, 2, TOK, HD), jnp.bfloat16),
            pltpu.SemaphoreType.DMA((8,)),
            pltpu.SemaphoreType.DMA((3,)),
        ],
        input_output_aliases=aliases,
        compiler_params=pltpu.CompilerParams(vmem_limit_bytes=60 * MIB),
        cost_estimate=cost(2, blocks, 7),
    )(first, clips, *operands)


def per_device(student_q, student_k, student_v, teacher_q, teacher_k, stagger, clip_lengths):
    heads = student_q.shape[2] // HD
    peers = lax.axis_size("tm")
    full, rest = divmod(heads, peers)
    assert rest and 2 * rest <= peers
    base = full * peers
    here = lax.axis_index("tm")
    role = jnp.where(here < 2 * rest, 1 + here % 2, 0).astype(jnp.int32)[None]
    running = jnp.cumsum(clip_lengths[0])
    block = jnp.arange(peers, dtype=jnp.int32)
    before = running[None, :] <= block[:, None]
    low = jnp.max(jnp.where(before, running[None, :], 0), axis=1)
    high = jnp.min(jnp.where(before, peers, running[None, :]), axis=1)
    clips = jnp.stack([low, high]).astype(jnp.int32)

    tensors = (student_q, student_k, student_v, teacher_q, teacher_k)
    early, late = tuple(range(full))[:-1], tuple(range(full))[-1:]
    plan, plan_late = [], []
    for p in range(peers):
        h = base + min(p // 2, rest - 1)
        row = [(t, h) for t in ((3, 4, 4) if p % 2 else (0, 1, 2))]
        plan.append(row + [(t, s * peers + p) for s in early for t in range(5)])
        plan_late.append([(t, s * peers + p) for s in late for t in range(5)])
    units = 2 * full + 1

    ranges = [(base, rest)] + [(s * peers, peers) for s in early]
    arrived = lax.all_to_all(pack(plan, ranges, tensors), "tm", 0, 0)
    arrived_late = None
    if late:
        ranges = [(s * peers, peers) for s in late]
        packed_late = pack(plan_late, ranges, tensors)
        arrived, packed_late = lax.optimization_barrier((arrived, packed_late))
        arrived_late = lax.all_to_all(packed_late, "tm", 0, 0)
    gen = rest_student(peers, stagger, role, arrived)
    shared = lax.ppermute(gen, "tm", [(2 * r, 2 * r + 1) for r in range(rest)])
    results = None
    for i, slot in enumerate(early):
        results = slot_kernel(peers, slot, units, stagger, clips, arrived, 3 + 5 * i, results)
    results = rest_teacher(peers, 2 * full, clips, role, arrived, gen, shared, results)
    for i, slot in enumerate(late):
        results = slot_kernel(peers, slot, units, stagger, clips, arrived_late, 5 * i, results)
    back = lax.all_to_all(results, "tm", 0, 0)
    return tuple(
        unpack(
            [
                [(h % peers, 2 * (h // peers) + which) for h in range(base)]
                + [(2 * r + which, 2 * full) for r in range(rest)]
                for which in (0, 1)
            ],
            back,
        )
    )


def solution(mesh):
    spec = P("seq", "tm", "mp")
    return jax.shard_map(
        per_device,
        mesh=mesh,
        in_specs=(spec,) * 5 + (P("seq"), P("seq", None)),
        out_specs=(spec, spec),
        check_vma=False,
    )
```

```python
import functools
import math

import jax
import jax.numpy as jnp
from jax import lax
from jax.experimental import pallas as pl
from jax.experimental.pallas import tpu as pltpu
from jax.sharding import PartitionSpec as P

HD = 128
TOK = 128
NEG = -1e30
RATE = math.log2(math.e) / math.sqrt(HD)
MIB = 2**20
VMEM = pl.BlockSpec(memory_space=pltpu.VMEM)
SMEM = pl.BlockSpec(memory_space=pltpu.SMEM)
LOCAL = pltpu.CompilerParams(vmem_limit_bytes=24 * MIB)


def attend(q, k, v, bias):
    g = q.shape[0]
    scores = lax.dot_general(
        q.reshape(g * TOK, HD), k, (((1,), (1,)), ((), ())), preferred_element_type=jnp.float32
    )
    scores = scores.reshape(g, TOK, -1) + bias
    top = jnp.max(scores, axis=-1, keepdims=True)
    weights = jnp.exp2((scores - top) * RATE)
    total = jnp.sum(weights, axis=-1, keepdims=True)
    weights = weights.astype(jnp.bfloat16).reshape(g * TOK, -1)
    mixed = jnp.dot(weights, v, preferred_element_type=jnp.float32)
    return mixed.reshape(g, TOK, HD) / total


def student_head(pairs, first, sources, o_ref, o_at):
    (q_ref, q_at), (k_ref, k_at), (v_ref, v_at) = sources
    for i in pairs:
        width = (i + 2) * TOK
        block = lax.broadcasted_iota(jnp.int32, (2, 1, width), 2) // TOK
        own = lax.broadcasted_iota(jnp.int32, (2, 1, width), 0) + i
        bias = jnp.where((block == own) | (block >= first) & (block < own), 0.0, NEG)
        k = k_ref[0 : i + 2, k_at].reshape(width, HD)
        v = v_ref[0 : i + 2, v_at].reshape(width, HD)
        o_ref[i : i + 2, o_at] = attend(q_ref[i : i + 2, q_at], k, v, bias).astype(jnp.bfloat16)


def teacher_head(blocks, rows, clip_ref, sources, gen, o_ref, o_at):
    (q_ref, q_at), (k_ref, k_at) = sources
    reach = blocks // 2 + 1
    width = reach * TOK
    offset = lax.broadcasted_iota(jnp.int32, (1, 1, width), 2) // TOK
    for i in rows:
        low = clip_ref[0, i]
        high = clip_ref[1, i]
        start = jnp.minimum(low, blocks - reach)
        block = offset + start
        bias = jnp.where((block >= low) & (block < high), 0.0, NEG)
        k = k_ref[pl.ds(start, reach), k_at].reshape(width, HD)
        v = gen(pl.ds(start, reach)).reshape(width, HD)
        out = attend(q_ref[pl.ds(i, 1), q_at], k, v, bias)
        o_ref[i, o_at] = (out[0] - gen(i).astype(jnp.float32)).astype(jnp.bfloat16)


def cost(heads, blocks, units):
    return pl.CostEstimate(
        flops=heads * blocks * blocks * 4 * TOK * TOK * HD,
        bytes_accessed=units * blocks * TOK * HD * 2,
        transcendentals=heads * blocks * blocks * TOK * TOK,
    )


def pack(plan, ranges, tensors):
    peers, units = len(plan), len(plan[0])
    widths = [count * HD for _, count in ranges]
    starts = [sum(widths[:r]) for r in range(len(ranges))]

    def place(h):
        for r, (head, count) in enumerate(ranges):
            if head <= h < head + count:
                return r, starts[r] + (h - head) * HD

    need = []
    for u in range(units):
        need.append(list(dict.fromkeys((plan[p][u][0], place(plan[p][u][1])[0]) for p in range(peers))))
    order = sorted(range(units), key=lambda u: (len(need[u]), u))
    fetch = list(dict.fromkeys(piece for u in order for piece in need[u]))

    def body(*refs):
        o_ref, rows, tiles, in_sem, out_sem = refs[len(tensors) :]
        copies = {}
        for n, (t, r) in enumerate(fetch):
            source = refs[t].at[0, :, pl.ds(ranges[r][0] * HD, widths[r])]
            target = rows.at[t, :, pl.ds(starts[r], widths[r])]
            copies[t, r] = pltpu.make_async_copy(source, target, in_sem.at[n])
            copies[t, r].start()
        sent = []
        for u in order:
            for piece in need[u]:
                if piece in copies:
                    copies.pop(piece).wait()
            for p in range(peers):
                t, h = plan[p][u]
                at = place(h)[1]
                tiles[p, u] = rows[t, :, at : at + HD]
            sent.append(pltpu.make_async_copy(tiles.at[:, u], o_ref.at[:, u], out_sem.at[u]))
            sent[-1].start()
        for copy in sent:
            copy.wait()

    return pl.pallas_call(
        body,
        in_specs=[pl.BlockSpec(memory_space=pl.ANY)] * len(tensors),
        out_specs=pl.BlockSpec(memory_space=pl.ANY),
        out_shape=jax.ShapeDtypeStruct((peers, units, TOK, HD), jnp.bfloat16),
        scratch_shapes=[
            pltpu.VMEM((len(tensors), TOK, sum(widths)), jnp.bfloat16),
            pltpu.VMEM((peers, units, TOK, HD), jnp.bfloat16),
            pltpu.SemaphoreType.DMA((len(fetch),)),
            pltpu.SemaphoreType.DMA((units,)),
        ],
        compiler_params=pltpu.CompilerParams(vmem_limit_bytes=60 * MIB),
        cost_estimate=cost(0, peers, 2 * units),
    )(*tensors)


def unpack(places, back):
    def body(x_ref, *o_refs):
        for o_ref, place in zip(o_refs, places):
            for h, (p, u) in enumerate(place):
                o_ref[0, :, h * HD : (h + 1) * HD] = x_ref[p, u]

    width = len(places[0]) * HD
    return pl.pallas_call(
        body,
        out_shape=[jax.ShapeDtypeStruct((1, TOK, width), jnp.bfloat16) for _ in places],
        compiler_params=LOCAL,
        cost_estimate=cost(0, 1, 4 * len(places[0])),
    )(back)


def student_kernel(full, blocks, first, role, arrived):
    def body(first_ref, role_ref, x_ref, *o_refs):
        def head(s, o_ref, to):
            sources = [(x_ref, 3 * s + t) for t in range(3)]
            student_head(range(0, blocks, 2), first_ref[0], sources, o_ref, to)

        if full:
            lax.fori_loop(0, full, lambda s, carry: head(s, o_refs[0], s), None)

        @pl.when(role_ref[0] == 1)
        def _():
            head(full, o_refs[-1], 0)

    shapes = [(blocks, full, TOK, HD)] if full else []
    shapes.append((blocks, 1, TOK, HD))
    return pl.pallas_call(
        body,
        in_specs=[SMEM, SMEM, VMEM],
        out_specs=[VMEM] * len(shapes),
        out_shape=[jax.ShapeDtypeStruct(shape, jnp.bfloat16) for shape in shapes],
        compiler_params=LOCAL,
        cost_estimate=cost(full + 1, blocks, 4 * (full + 1)),
    )(first, role, arrived)


def teacher_kernel(slots, blocks, clips, arrived, offset, gen):
    def body(clip_ref, x_ref, gen_ref, o_ref):
        def head(s, carry):
            sources = [(x_ref, offset + 2 * s + t) for t in range(2)]
            teacher_head(
                blocks, range(blocks), clip_ref, sources, lambda at: gen_ref[at, s], o_ref, s
            )

        lax.fori_loop(0, slots, head, None)

    return pl.pallas_call(
        body,
        in_specs=[SMEM, VMEM, VMEM],
        out_specs=VMEM,
        out_shape=jax.ShapeDtypeStruct((blocks, slots, TOK, HD), jnp.bfloat16),
        compiler_params=LOCAL,
        cost_estimate=cost(slots, blocks, 4 * slots),
    )(clips, arrived, gen)


def rest_teacher(blocks, clips, role, arrived, offset, gen, shared):
    def body(clip_ref, role_ref, x_ref, gen_ref, shared_ref, o_ref):
        @pl.when(role_ref[0] == 1)
        def _():
            o_ref[...] = gen_ref[...]

        @pl.when(role_ref[0] == 2)
        def _():
            sources = [(x_ref, offset + t) for t in range(2)]
            teacher_head(
                blocks, range(blocks), clip_ref, sources, lambda at: shared_ref[at, 0], o_ref, 0
            )

    return pl.pallas_call(
        body,
        in_specs=[SMEM, SMEM, VMEM, VMEM, VMEM],
        out_specs=VMEM,
        out_shape=jax.ShapeDtypeStruct((blocks, 1, TOK, HD), jnp.bfloat16),
        compiler_params=LOCAL,
        cost_estimate=cost(1, blocks, 5),
    )(clips, role, arrived, gen, shared)


def last_kernel(full, blocks, clips, arrived, gen, rest_unit, scores):
    def body(clip_ref, x_ref, gen_ref, rest_ref, *refs):
        o_ref = refs[-1]
        o_ref[:, 0:full] = gen_ref[...]
        o_ref[:, full : full + 1] = rest_ref[...]
        if scores is not None:
            o_ref[:, full + 1 : 2 * full] = refs[0][...]
        sources = [(x_ref, t) for t in range(2)]
        teacher_head(
            blocks,
            range(blocks),
            clip_ref,
            sources,
            lambda at: gen_ref[at, full - 1],
            o_ref,
            2 * full,
        )

    operands = [arrived, gen, rest_unit] + ([scores] if scores is not None else [])
    return pl.pallas_call(
        body,
        in_specs=[SMEM] + [VMEM] * len(operands),
        out_specs=VMEM,
        out_shape=jax.ShapeDtypeStruct((blocks, 2 * full + 1, TOK, HD), jnp.bfloat16),
        compiler_params=LOCAL,
        cost_estimate=cost(1, blocks, 4 * full + 4),
    )(clips, *operands)


def per_device(student_q, student_k, student_v, teacher_q, teacher_k, stagger, clip_lengths):
    heads = student_q.shape[2] // HD
    peers = lax.axis_size("tm")
    full, rest = divmod(heads, peers)
    assert rest and 2 * rest <= peers
    base = full * peers
    here = lax.axis_index("tm")
    role = jnp.where(here < 2 * rest, 1 + here % 2, 0).astype(jnp.int32)[None]
    running = jnp.cumsum(clip_lengths[0])
    block = jnp.arange(peers, dtype=jnp.int32)
    before = running[None, :] <= block[:, None]
    low = jnp.max(jnp.where(before, running[None, :], 0), axis=1)
    high = jnp.min(jnp.where(before, peers, running[None, :]), axis=1)
    clips = jnp.stack([low, high]).astype(jnp.int32)

    tensors = (student_q, student_k, student_v, teacher_q, teacher_k)
    plan, plan_late = [], []
    for p in range(peers):
        row = [(t, s * peers + p) for s in range(full) for t in (0, 1, 2)]
        h = base + min(p // 2, rest - 1)
        row += [(t, h) for t in ((3, 4, 4) if p % 2 else (0, 1, 2))]
        row += [(t, s * peers + p) for s in range(full - 1) for t in (3, 4)]
        plan.append(row)
        plan_late.append([(t, (full - 1) * peers + p) for t in (3, 4)])
    tail = 3 * full
    slots = [(s * peers, peers) for s in range(full)]

    arrived = lax.all_to_all(pack(plan, slots + [(base, rest)], tensors), "tm", 0, 0)
    if full:
        packed_late = pack(plan_late, slots[-1:], tensors)
        arrived, packed_late = lax.optimization_barrier((arrived, packed_late))
        arrived_late = lax.all_to_all(packed_late, "tm", 0, 0)
    *gen, rest_gen = student_kernel(full, peers, stagger, role, arrived)
    shared = lax.ppermute(rest_gen, "tm", [(2 * r, 2 * r + 1) for r in range(rest)])
    scores = None
    if full > 1:
        scores = teacher_kernel(full - 1, peers, clips, arrived, tail + 3, gen[0])
    results = rest_teacher(peers, clips, role, arrived, tail, rest_gen, shared)
    if full:
        results = last_kernel(full, peers, clips, arrived_late, gen[0], results, scores)
    back = lax.all_to_all(results, "tm", 0, 0)
    places = [
        [(h % peers, h // peers + which * (full + 1)) for h in range(base)]
        + [(2 * r + which, full) for r in range(rest)]
        for which in (0, 1)
    ]
    return tuple(unpack(places, back))


def solution(mesh):
    spec = P("seq", "tm", "mp")
    return jax.shard_map(
        per_device,
        mesh=mesh,
        in_specs=(spec,) * 5 + (P("seq"), P("seq", None)),
        out_specs=(spec, spec),
        check_vma=False,
    )
```

```python
import functools
import math

import jax
import jax.numpy as jnp
from jax import lax
from jax.experimental import pallas as pl
from jax.experimental.pallas import tpu as pltpu
from jax.sharding import PartitionSpec as P

HD = 128
TOK = 128
NEG = -1e30
RATE = math.log2(math.e) / math.sqrt(HD)
MIB = 2**20
VMEM = pl.BlockSpec(memory_space=pltpu.VMEM)
SMEM = pl.BlockSpec(memory_space=pltpu.SMEM)
WHOLE = pltpu.CompilerParams(vmem_limit_bytes=60 * MIB)
LOCAL = pltpu.CompilerParams(vmem_limit_bytes=24 * MIB)


def attend(q, k, v, bias):
    g = q.shape[0]
    scores = lax.dot_general(
        q.reshape(g * TOK, HD), k, (((1,), (1,)), ((), ())), preferred_element_type=jnp.float32
    )
    scores = scores.reshape(g, TOK, -1) + bias
    top = jnp.max(scores, axis=-1, keepdims=True)
    weights = jnp.exp2((scores - top) * RATE)
    total = jnp.sum(weights, axis=-1, keepdims=True)
    weights = weights.astype(jnp.bfloat16).reshape(g * TOK, -1)
    mixed = jnp.dot(weights, v, preferred_element_type=jnp.float32)
    return mixed.reshape(g, TOK, HD) / total


def student_head(pairs, first, sources, o_ref, o_at):
    (q_ref, q_at), (k_ref, k_at), (v_ref, v_at) = sources
    for i in pairs:
        width = (i + 2) * TOK
        block = lax.broadcasted_iota(jnp.int32, (2, 1, width), 2) // TOK
        own = lax.broadcasted_iota(jnp.int32, (2, 1, width), 0) + i
        bias = jnp.where((block == own) | (block >= first) & (block < own), 0.0, NEG)
        k = k_ref[0 : i + 2, k_at].reshape(width, HD)
        v = v_ref[0 : i + 2, v_at].reshape(width, HD)
        o_ref[i : i + 2, o_at] = attend(q_ref[i : i + 2, q_at], k, v, bias).astype(jnp.bfloat16)


def teacher_head(blocks, rows, clip_ref, sources, gen, o_ref, o_at):
    (q_ref, q_at), (k_ref, k_at) = sources
    reach = blocks // 2 + 1
    width = reach * TOK
    offset = lax.broadcasted_iota(jnp.int32, (1, 1, width), 2) // TOK
    for i in rows:
        low = clip_ref[0, i]
        high = clip_ref[1, i]
        start = jnp.minimum(low, blocks - reach)
        block = offset + start
        bias = jnp.where((block >= low) & (block < high), 0.0, NEG)
        k = k_ref[pl.ds(start, reach), k_at].reshape(width, HD)
        v = gen(pl.ds(start, reach)).reshape(width, HD)
        out = attend(q_ref[pl.ds(i, 1), q_at], k, v, bias)
        score = (out[0] - gen(i).astype(jnp.float32)).astype(jnp.bfloat16)
        if o_at is None:
            o_ref[1] = score
        else:
            o_ref[i, o_at] = score


def cost(heads, blocks, units):
    return pl.CostEstimate(
        flops=heads * blocks * blocks * 4 * TOK * TOK * HD,
        bytes_accessed=units * blocks * TOK * HD * 2,
        transcendentals=heads * blocks * blocks * TOK * TOK,
    )


def pack(plan, ranges, tensors):
    peers, units = len(plan), len(plan[0])
    widths = [count * HD for _, count in ranges]
    starts = [sum(widths[:r]) for r in range(len(ranges))]

    def place(h):
        for r, (head, count) in enumerate(ranges):
            if head <= h < head + count:
                return r, starts[r] + (h - head) * HD

    need = []
    for u in range(units):
        need.append(list(dict.fromkeys((plan[p][u][0], place(plan[p][u][1])[0]) for p in range(peers))))
    order = sorted(range(units), key=lambda u: (len(need[u]), u))
    fetch = list(dict.fromkeys(piece for u in order for piece in need[u]))

    def body(*refs):
        o_ref, rows, tiles, in_sem, out_sem = refs[len(tensors) :]
        copies = {}
        for n, (t, r) in enumerate(fetch):
            source = refs[t].at[0, :, pl.ds(ranges[r][0] * HD, widths[r])]
            target = rows.at[t, :, pl.ds(starts[r], widths[r])]
            copies[t, r] = pltpu.make_async_copy(source, target, in_sem.at[n])
            copies[t, r].start()
        sent = []
        for u in order:
            for piece in need[u]:
                if piece in copies:
                    copies.pop(piece).wait()
            for p in range(peers):
                t, h = plan[p][u]
                at = place(h)[1]
                tiles[p, u] = rows[t, :, at : at + HD]
            sent.append(pltpu.make_async_copy(tiles.at[:, u], o_ref.at[:, u], out_sem.at[u]))
            sent[-1].start()
        for copy in sent:
            copy.wait()

    return pl.pallas_call(
        body,
        in_specs=[pl.BlockSpec(memory_space=pl.ANY)] * len(tensors),
        out_specs=pl.BlockSpec(memory_space=pl.ANY),
        out_shape=jax.ShapeDtypeStruct((peers, units, TOK, HD), jnp.bfloat16),
        scratch_shapes=[
            pltpu.VMEM((len(tensors), TOK, sum(widths)), jnp.bfloat16),
            pltpu.VMEM((peers, units, TOK, HD), jnp.bfloat16),
            pltpu.SemaphoreType.DMA((len(fetch),)),
            pltpu.SemaphoreType.DMA((units,)),
        ],
        compiler_params=WHOLE,
        cost_estimate=cost(0, peers, 2 * units),
    )(*tensors)


def unpack(places, back):
    def body(x_ref, *o_refs):
        for o_ref, place in zip(o_refs, places):
            for h, (p, u) in enumerate(place):
                o_ref[0, :, h * HD : (h + 1) * HD] = x_ref[p, u]

    width = len(places[0]) * HD
    return pl.pallas_call(
        body,
        out_shape=[jax.ShapeDtypeStruct((1, TOK, width), jnp.bfloat16) for _ in places],
        compiler_params=LOCAL,
        cost_estimate=cost(0, 1, 4 * len(places[0])),
    )(back)


def student_kernel(blocks, first, role, arrived):
    def body(first_ref, role_ref, x_ref, o_ref):
        @pl.when(role_ref[0] == 1)
        def _():
            sources = [(x_ref, t) for t in range(3)]
            student_head(range(0, blocks, 2), first_ref[0], sources, o_ref, 0)

    return pl.pallas_call(
        body,
        in_specs=[SMEM, SMEM, VMEM],
        out_specs=VMEM,
        out_shape=jax.ShapeDtypeStruct((blocks, 1, TOK, HD), jnp.bfloat16),
        compiler_params=LOCAL,
        cost_estimate=cost(1, blocks, 4),
    )(first, role, arrived)


def rest_teacher(blocks, clips, role, arrived, offset, gen, shared):
    def body(clip_ref, role_ref, x_ref, gen_ref, shared_ref, o_ref):
        @pl.when(role_ref[0] == 1)
        def _():
            o_ref[...] = gen_ref[...]

        @pl.when(role_ref[0] == 2)
        def _():
            sources = [(x_ref, offset + t) for t in range(2)]
            teacher_head(
                blocks, range(blocks), clip_ref, sources, lambda at: shared_ref[at, 0], o_ref, 0
            )

    return pl.pallas_call(
        body,
        in_specs=[SMEM, SMEM, VMEM, VMEM, VMEM],
        out_specs=VMEM,
        out_shape=jax.ShapeDtypeStruct((blocks, 1, TOK, HD), jnp.bfloat16),
        compiler_params=LOCAL,
        cost_estimate=cost(1, blocks, 5),
    )(clips, role, arrived, gen, shared)


def slots_kernel(full, blocks, first, clips, arrived):
    def body(first_ref, clip_ref, x_ref, o_ref):
        def head(s, carry):
            sources = [(x_ref, 5 * s + t) for t in range(5)]
            student_head(range(0, blocks, 2), first_ref[0], sources[:3], o_ref, 2 * s)
            gen = lambda at: o_ref[at, 2 * s]
            teacher_head(blocks, range(blocks), clip_ref, sources[3:], gen, o_ref, 2 * s + 1)

        lax.fori_loop(0, full, head, None)

    return pl.pallas_call(
        body,
        in_specs=[SMEM, SMEM, VMEM],
        out_specs=VMEM,
        out_shape=jax.ShapeDtypeStruct((blocks, 2 * full, TOK, HD), jnp.bfloat16),
        compiler_params=LOCAL,
        cost_estimate=cost(2 * full, blocks, 7 * full),
    )(first, clips, arrived)


def rest_pack(base, columns, column, tensors):
    def body(column_ref, *refs):
        rows, sems = refs[-2:]
        copies = []
        for t in range(5):
            source = refs[t].at[0, :, pl.ds(base * HD, columns * HD)]
            copies.append(pltpu.make_async_copy(source, rows.at[t], sems.at[t]))
            copies[-1].start()
        for t in range(5):
            copies[t].wait()
            for s in range(columns):
                at = pl.multiple_of((column_ref[0] ^ s) * HD, HD)
                refs[5 + s][t] = rows[t, :, pl.ds(at, HD)]

    return pl.pallas_call(
        body,
        in_specs=[SMEM] + [pl.BlockSpec(memory_space=pl.ANY)] * 5,
        out_specs=[VMEM] * columns,
        out_shape=[jax.ShapeDtypeStruct((5, TOK, HD), jnp.bfloat16)] * columns,
        scratch_shapes=[
            pltpu.VMEM((5, TOK, columns * HD), jnp.bfloat16),
            pltpu.SemaphoreType.DMA((5,)),
        ],
        compiler_params=WHOLE,
        cost_estimate=cost(0, 1, 10 * columns),
    )(column, *tensors)


def rest_kernel(columns, first, clips, where, own, other):
    blocks = 2 * columns

    def body(first_ref, clip_ref, where_ref, *refs):
        x, gen = refs[-2:]
        column, side = where_ref[0], where_ref[1]
        mine = [2 * (column ^ s) + side for s in range(columns)]
        for s in range(columns):
            x[mine[s]] = refs[s][...]
            x[mine[s] ^ 1] = refs[columns + s][...]
        sources = [(x, t) for t in range(5)]
        student_head(range(0, blocks, 2), first_ref[0], sources[:3], gen, 0)
        at_gen = lambda at: gen[at, 0]
        for s in range(columns):
            o_ref = refs[2 * columns + s]
            o_ref[0:1] = gen[mine[s]]
            teacher_head(blocks, [mine[s]], clip_ref, sources[3:], at_gen, o_ref, None)

    return pl.pallas_call(
        body,
        in_specs=[SMEM] * 3 + [VMEM] * (2 * columns),
        out_specs=[VMEM] * columns,
        out_shape=[jax.ShapeDtypeStruct((2, TOK, HD), jnp.bfloat16)] * columns,
        scratch_shapes=[
            pltpu.VMEM((blocks, 5, TOK, HD), jnp.bfloat16),
            pltpu.VMEM((blocks, 1, TOK, HD), jnp.bfloat16),
        ],
        compiler_params=LOCAL,
        cost_estimate=cost(2, blocks, 7),
    )(first, clips, where, *own, *other)


def join(base, columns, places, column, back, pieces):
    def body(column_ref, x_ref, *refs):
        for i, o_ref in enumerate(refs[columns:]):
            for h, (p, u) in enumerate(places[i]):
                o_ref[0, :, h * HD : (h + 1) * HD] = x_ref[p, u]
            for s in range(columns):
                at = pl.multiple_of((base + (column_ref[0] ^ s)) * HD, HD)
                o_ref[0, :, pl.ds(at, HD)] = refs[s][i]

    width = (base + columns) * HD
    return pl.pallas_call(
        body,
        in_specs=[SMEM, VMEM] + [VMEM] * columns,
        out_specs=[VMEM] * 2,
        out_shape=[jax.ShapeDtypeStruct((1, TOK, width), jnp.bfloat16)] * 2,
        compiler_params=LOCAL,
        cost_estimate=cost(0, 1, 4 * (base + columns)),
    )(column, back, *pieces)


def by_slots_and_columns(tensors, peers, full, rest, first, clips):
    base = full * peers
    here = lax.axis_index("tm")
    column, side = here // 2, here % 2
    where = jnp.stack([column, side]).astype(jnp.int32)

    def swapped(x, by):
        return lax.ppermute(x, "tm", [(i, i ^ by) for i in range(peers)])

    plan = [[(t, s * peers + p) for s in range(full) for t in range(5)] for p in range(peers)]
    slots = [(s * peers, peers) for s in range(full)]
    arrived = lax.all_to_all(pack(plan, slots, tensors), "tm", 0, 0)
    pieces = rest_pack(base, rest, where[:1], tensors)
    near, far = pieces[:2], pieces[2:]
    arrived, far = lax.optimization_barrier((arrived, far))
    own = [pieces[0]] + [swapped(x, 2 * s) for s, x in enumerate(near) if s]
    own += [swapped(x, 2 * (s + len(near))) for s, x in enumerate(far)]
    other = [swapped(x, 1) for x in own]
    results = slots_kernel(full, peers, first, clips, arrived)
    back = lax.all_to_all(results, "tm", 0, 0)
    _, own, other = lax.optimization_barrier((results, own, other))
    pieces = rest_kernel(rest, first, clips, where, own, other)
    pieces = [swapped(x, 2 * s) if s else x for s, x in enumerate(pieces)]
    places = [[(h % peers, 2 * (h // peers) + i) for h in range(base)] for i in (0, 1)]
    return tuple(join(base, rest, places, where[:1], back, pieces))


def by_roles(tensors, peers, heads, first, clips):
    here = lax.axis_index("tm")
    role = jnp.where(here < 2 * heads, 1 + here % 2, 0).astype(jnp.int32)[None]
    plan = [
        [(t, min(p // 2, heads - 1)) for t in ((3, 4, 4) if p % 2 else (0, 1, 2))]
        for p in range(peers)
    ]
    arrived = lax.all_to_all(pack(plan, [(0, heads)], tensors), "tm", 0, 0)
    gen = student_kernel(peers, first, role, arrived)
    shared = lax.ppermute(gen, "tm", [(2 * r, 2 * r + 1) for r in range(heads)])
    results = rest_teacher(peers, clips, role, arrived, 0, gen, shared)
    back = lax.all_to_all(results, "tm", 0, 0)
    return tuple(unpack([[(2 * r + i, 0) for r in range(heads)] for i in (0, 1)], back))


def per_device(student_q, student_k, student_v, teacher_q, teacher_k, stagger, clip_lengths):
    heads = student_q.shape[2] // HD
    peers = lax.axis_size("tm")
    full, rest = divmod(heads, peers)
    running = jnp.cumsum(clip_lengths[0])
    block = jnp.arange(peers, dtype=jnp.int32)
    before = running[None, :] <= block[:, None]
    low = jnp.max(jnp.where(before, running[None, :], 0), axis=1)
    high = jnp.min(jnp.where(before, peers, running[None, :]), axis=1)
    clips = jnp.stack([low, high]).astype(jnp.int32)
    tensors = (student_q, student_k, student_v, teacher_q, teacher_k)
    if full == 0:
        assert 2 * rest <= peers
        return by_roles(tensors, peers, rest, stagger, clips)
    assert peers == 2 * rest and rest & (rest - 1) == 0
    return by_slots_and_columns(tensors, peers, full, rest, stagger, clips)


def solution(mesh):
    spec = P("seq", "tm", "mp")
    return jax.shard_map(
        per_device,
        mesh=mesh,
        in_specs=(spec,) * 5 + (P("seq"), P("seq", None)),
        out_specs=(spec, spec),
        check_vma=False,
    )
```

```python
import functools
import math

import jax
import jax.numpy as jnp
from jax import lax
from jax.experimental import pallas as pl
from jax.experimental.pallas import tpu as pltpu
from jax.sharding import PartitionSpec as P

HD = 128
TOK = 128
NEG = -1e30
RATE = math.log2(math.e) / math.sqrt(HD)
MIB = 2**20
VMEM = pl.BlockSpec(memory_space=pltpu.VMEM)
SMEM = pl.BlockSpec(memory_space=pltpu.SMEM)
WHOLE = pltpu.CompilerParams(vmem_limit_bytes=60 * MIB)
LOCAL = pltpu.CompilerParams(vmem_limit_bytes=24 * MIB)


def attend(q, k, v, bias):
    g = q.shape[0]
    scores = lax.dot_general(
        q.reshape(g * TOK, HD), k, (((1,), (1,)), ((), ())), preferred_element_type=jnp.float32
    )
    scores = scores.reshape(g, TOK, -1) + bias
    top = jnp.max(scores, axis=-1, keepdims=True)
    weights = jnp.exp2((scores - top) * RATE)
    total = jnp.sum(weights, axis=-1, keepdims=True)
    weights = weights.astype(jnp.bfloat16).reshape(g * TOK, -1)
    mixed = jnp.dot(weights, v, preferred_element_type=jnp.float32)
    return mixed.reshape(g, TOK, HD) / total


def student_head(pairs, first, sources, o_ref, o_at):
    (q_ref, q_at), (k_ref, k_at), (v_ref, v_at) = sources
    for i in pairs:
        width = (i + 2) * TOK
        block = lax.broadcasted_iota(jnp.int32, (2, 1, width), 2) // TOK
        own = lax.broadcasted_iota(jnp.int32, (2, 1, width), 0) + i
        bias = jnp.where((block == own) | (block >= first) & (block < own), 0.0, NEG)
        k = k_ref[0 : i + 2, k_at].reshape(width, HD)
        v = v_ref[0 : i + 2, v_at].reshape(width, HD)
        o_ref[i : i + 2, o_at] = attend(q_ref[i : i + 2, q_at], k, v, bias).astype(jnp.bfloat16)


def teacher_head(blocks, rows, clip_ref, sources, gen, o_ref, o_at):
    (q_ref, q_at), (k_ref, k_at) = sources
    reach = blocks // 2 + 1
    width = reach * TOK
    offset = lax.broadcasted_iota(jnp.int32, (1, 1, width), 2) // TOK
    for i in rows:
        low = clip_ref[0, i]
        high = clip_ref[1, i]
        start = jnp.minimum(low, blocks - reach)
        block = offset + start
        bias = jnp.where((block >= low) & (block < high), 0.0, NEG)
        k = k_ref[pl.ds(start, reach), k_at].reshape(width, HD)
        v = gen(pl.ds(start, reach)).reshape(width, HD)
        out = attend(q_ref[pl.ds(i, 1), q_at], k, v, bias)
        score = (out[0] - gen(i).astype(jnp.float32)).astype(jnp.bfloat16)
        if o_at is None:
            o_ref[1] = score
        else:
            o_ref[i, o_at] = score


def cost(heads, blocks, units):
    return pl.CostEstimate(
        flops=heads * blocks * blocks * 4 * TOK * TOK * HD,
        bytes_accessed=units * blocks * TOK * HD * 2,
        transcendentals=heads * blocks * blocks * TOK * TOK,
    )


def pack(plan, ranges, tensors):
    peers, units = len(plan), len(plan[0])
    widths = [count * HD for _, count in ranges]
    starts = [sum(widths[:r]) for r in range(len(ranges))]

    def place(h):
        for r, (head, count) in enumerate(ranges):
            if head <= h < head + count:
                return r, starts[r] + (h - head) * HD

    need = []
    for u in range(units):
        need.append(list(dict.fromkeys((plan[p][u][0], place(plan[p][u][1])[0]) for p in range(peers))))
    order = sorted(range(units), key=lambda u: (len(need[u]), u))
    fetch = list(dict.fromkeys(piece for u in order for piece in need[u]))

    def body(*refs):
        o_ref, rows, tiles, in_sem, out_sem = refs[len(tensors) :]
        copies = {}
        for n, (t, r) in enumerate(fetch):
            source = refs[t].at[0, :, pl.ds(ranges[r][0] * HD, widths[r])]
            target = rows.at[t, :, pl.ds(starts[r], widths[r])]
            copies[t, r] = pltpu.make_async_copy(source, target, in_sem.at[n])
            copies[t, r].start()
        sent = []
        for u in order:
            for piece in need[u]:
                if piece in copies:
                    copies.pop(piece).wait()
            for p in range(peers):
                t, h = plan[p][u]
                at = place(h)[1]
                tiles[p, u] = rows[t, :, at : at + HD]
            sent.append(pltpu.make_async_copy(tiles.at[:, u], o_ref.at[:, u], out_sem.at[u]))
            sent[-1].start()
        for copy in sent:
            copy.wait()

    return pl.pallas_call(
        body,
        in_specs=[pl.BlockSpec(memory_space=pl.ANY)] * len(tensors),
        out_specs=pl.BlockSpec(memory_space=pl.ANY),
        out_shape=jax.ShapeDtypeStruct((peers, units, TOK, HD), jnp.bfloat16),
        scratch_shapes=[
            pltpu.VMEM((len(tensors), TOK, sum(widths)), jnp.bfloat16),
            pltpu.VMEM((peers, units, TOK, HD), jnp.bfloat16),
            pltpu.SemaphoreType.DMA((len(fetch),)),
            pltpu.SemaphoreType.DMA((units,)),
        ],
        compiler_params=WHOLE,
        cost_estimate=cost(0, peers, 2 * units),
    )(*tensors)


def unpack(places, back):
    def body(x_ref, *o_refs):
        for o_ref, place in zip(o_refs, places):
            for h, (p, u) in enumerate(place):
                o_ref[0, :, h * HD : (h + 1) * HD] = x_ref[p, u]

    width = len(places[0]) * HD
    return pl.pallas_call(
        body,
        out_shape=[jax.ShapeDtypeStruct((1, TOK, width), jnp.bfloat16) for _ in places],
        compiler_params=LOCAL,
        cost_estimate=cost(0, 1, 4 * len(places[0])),
    )(back)


def student_kernel(blocks, first, role, arrived):
    def body(first_ref, role_ref, x_ref, o_ref):
        @pl.when(role_ref[0] == 1)
        def _():
            sources = [(x_ref, t) for t in range(3)]
            student_head(range(0, blocks, 2), first_ref[0], sources, o_ref, 0)

    return pl.pallas_call(
        body,
        in_specs=[SMEM, SMEM, VMEM],
        out_specs=VMEM,
        out_shape=jax.ShapeDtypeStruct((blocks, 1, TOK, HD), jnp.bfloat16),
        compiler_params=LOCAL,
        cost_estimate=cost(1, blocks, 4),
    )(first, role, arrived)


def rest_teacher(blocks, clips, role, arrived, offset, gen, shared):
    def body(clip_ref, role_ref, x_ref, gen_ref, shared_ref, o_ref):
        @pl.when(role_ref[0] == 1)
        def _():
            o_ref[...] = gen_ref[...]

        @pl.when(role_ref[0] == 2)
        def _():
            sources = [(x_ref, offset + t) for t in range(2)]
            teacher_head(
                blocks, range(blocks), clip_ref, sources, lambda at: shared_ref[at, 0], o_ref, 0
            )

    return pl.pallas_call(
        body,
        in_specs=[SMEM, SMEM, VMEM, VMEM, VMEM],
        out_specs=VMEM,
        out_shape=jax.ShapeDtypeStruct((blocks, 1, TOK, HD), jnp.bfloat16),
        compiler_params=LOCAL,
        cost_estimate=cost(1, blocks, 5),
    )(clips, role, arrived, gen, shared)


def slots_kernel(full, blocks, first, clips, arrived):
    def body(first_ref, clip_ref, x_ref, o_ref):
        def head(s, carry):
            sources = [(x_ref, 5 * s + t) for t in range(5)]
            student_head(range(0, blocks, 2), first_ref[0], sources[:3], o_ref, 2 * s)
            gen = lambda at: o_ref[at, 2 * s]
            teacher_head(blocks, range(blocks), clip_ref, sources[3:], gen, o_ref, 2 * s + 1)

        lax.fori_loop(0, full, head, None)

    return pl.pallas_call(
        body,
        in_specs=[SMEM, SMEM, VMEM],
        out_specs=VMEM,
        out_shape=jax.ShapeDtypeStruct((blocks, 2 * full, TOK, HD), jnp.bfloat16),
        compiler_params=LOCAL,
        cost_estimate=cost(2 * full, blocks, 7 * full),
    )(first, clips, arrived)


def rest_pack(base, columns, column, tensors):
    def body(column_ref, *refs):
        rows, sems = refs[-2:]
        copies = []
        for t in range(5):
            source = refs[t].at[0, :, pl.ds(base * HD, columns * HD)]
            copies.append(pltpu.make_async_copy(source, rows.at[t], sems.at[t]))
            copies[-1].start()
        for t in range(5):
            copies[t].wait()
            for s in range(columns):
                at = pl.multiple_of((column_ref[0] ^ s) * HD, HD)
                refs[5 + s][t] = rows[t, :, pl.ds(at, HD)]

    return pl.pallas_call(
        body,
        in_specs=[SMEM] + [pl.BlockSpec(memory_space=pl.ANY)] * 5,
        out_specs=[VMEM] * columns,
        out_shape=[jax.ShapeDtypeStruct((5, TOK, HD), jnp.bfloat16)] * columns,
        scratch_shapes=[
            pltpu.VMEM((5, TOK, columns * HD), jnp.bfloat16),
            pltpu.SemaphoreType.DMA((5,)),
        ],
        compiler_params=WHOLE,
        cost_estimate=cost(0, 1, 10 * columns),
    )(column, *tensors)


def rest_kernel(columns, first, clips, where, own, other):
    blocks = 2 * columns

    def body(first_ref, clip_ref, where_ref, *refs):
        x, gen = refs[-2:]
        column, side = where_ref[0], where_ref[1]
        mine = [2 * (column ^ s) + side for s in range(columns)]
        for s in range(columns):
            x[mine[s]] = refs[s][...]
            x[mine[s] ^ 1] = refs[columns + s][...]
        sources = [(x, t) for t in range(5)]
        student_head(range(0, blocks, 2), first_ref[0], sources[:3], gen, 0)
        at_gen = lambda at: gen[at, 0]
        for s in range(columns):
            o_ref = refs[2 * columns + s]
            o_ref[0:1] = gen[mine[s]]
            teacher_head(blocks, [mine[s]], clip_ref, sources[3:], at_gen, o_ref, None)

    return pl.pallas_call(
        body,
        in_specs=[SMEM] * 3 + [VMEM] * (2 * columns),
        out_specs=[VMEM] * columns,
        out_shape=[jax.ShapeDtypeStruct((2, TOK, HD), jnp.bfloat16)] * columns,
        scratch_shapes=[
            pltpu.VMEM((blocks, 5, TOK, HD), jnp.bfloat16),
            pltpu.VMEM((blocks, 1, TOK, HD), jnp.bfloat16),
        ],
        compiler_params=LOCAL,
        cost_estimate=cost(2, blocks, 7),
    )(first, clips, where, *own, *other)


def join(base, columns, places, column, back, pieces):
    def body(column_ref, x_ref, *refs):
        for i, o_ref in enumerate(refs[columns:]):
            for h, (p, u) in enumerate(places[i]):
                o_ref[0, :, h * HD : (h + 1) * HD] = x_ref[p, u]
            for s in range(columns):
                at = pl.multiple_of((base + (column_ref[0] ^ s)) * HD, HD)
                o_ref[0, :, pl.ds(at, HD)] = refs[s][i]

    width = (base + columns) * HD
    return pl.pallas_call(
        body,
        in_specs=[SMEM, VMEM] + [VMEM] * columns,
        out_specs=[VMEM] * 2,
        out_shape=[jax.ShapeDtypeStruct((1, TOK, width), jnp.bfloat16)] * 2,
        compiler_params=LOCAL,
        cost_estimate=cost(0, 1, 4 * (base + columns)),
    )(column, back, *pieces)


def by_slots_and_columns(tensors, peers, full, rest, first, clips):
    base = full * peers
    here = lax.axis_index("tm")
    column, side = here // 2, here % 2
    where = jnp.stack([column, side]).astype(jnp.int32)

    def swapped(x, by):
        return lax.ppermute(x, "tm", [(i, i ^ by) for i in range(peers)])

    plan = [[(t, s * peers + p) for s in range(full) for t in range(5)] for p in range(peers)]
    slots = [(s * peers, peers) for s in range(full)]
    arrived = lax.all_to_all(pack(plan, slots, tensors), "tm", 0, 0)
    pieces = rest_pack(base, rest, where[:1], tensors)
    own = [swapped(x, 2 * s) if s else x for s, x in enumerate(pieces)]
    other = [swapped(x, 1) for x in own]
    pieces = rest_kernel(rest, first, clips, where, own, other)
    arrived, _ = lax.optimization_barrier((arrived, pieces))
    results = slots_kernel(full, peers, first, clips, arrived)
    back = lax.all_to_all(results, "tm", 0, 0)
    pieces = [swapped(x, 2 * s) if s else x for s, x in enumerate(pieces)]
    places = [[(h % peers, 2 * (h // peers) + i) for h in range(base)] for i in (0, 1)]
    return tuple(join(base, rest, places, where[:1], back, pieces))


def by_roles(tensors, peers, heads, first, clips):
    here = lax.axis_index("tm")
    role = jnp.where(here < 2 * heads, 1 + here % 2, 0).astype(jnp.int32)[None]
    plan = [
        [(t, min(p // 2, heads - 1)) for t in ((3, 4, 4) if p % 2 else (0, 1, 2))]
        for p in range(peers)
    ]
    arrived = lax.all_to_all(pack(plan, [(0, heads)], tensors), "tm", 0, 0)
    gen = student_kernel(peers, first, role, arrived)
    shared = lax.ppermute(gen, "tm", [(2 * r, 2 * r + 1) for r in range(heads)])
    results = rest_teacher(peers, clips, role, arrived, 0, gen, shared)
    back = lax.all_to_all(results, "tm", 0, 0)
    return tuple(unpack([[(2 * r + i, 0) for r in range(heads)] for i in (0, 1)], back))


def per_device(student_q, student_k, student_v, teacher_q, teacher_k, stagger, clip_lengths):
    heads = student_q.shape[2] // HD
    peers = lax.axis_size("tm")
    full, rest = divmod(heads, peers)
    running = jnp.cumsum(clip_lengths[0])
    block = jnp.arange(peers, dtype=jnp.int32)
    before = running[None, :] <= block[:, None]
    low = jnp.max(jnp.where(before, running[None, :], 0), axis=1)
    high = jnp.min(jnp.where(before, peers, running[None, :]), axis=1)
    clips = jnp.stack([low, high]).astype(jnp.int32)
    tensors = (student_q, student_k, student_v, teacher_q, teacher_k)
    if full == 0:
        assert 2 * rest <= peers
        return by_roles(tensors, peers, rest, stagger, clips)
    assert peers == 2 * rest and rest & (rest - 1) == 0
    return by_slots_and_columns(tensors, peers, full, rest, stagger, clips)


def solution(mesh):
    spec = P("seq", "tm", "mp")
    return jax.shard_map(
        per_device,
        mesh=mesh,
        in_specs=(spec,) * 5 + (P("seq"), P("seq", None)),
        out_specs=(spec, spec),
        check_vma=False,
    )
```

```python
import functools
import math

import jax
import jax.numpy as jnp
from jax import lax
from jax.experimental import pallas as pl
from jax.experimental.pallas import tpu as pltpu
from jax.sharding import PartitionSpec as P

HD = 128
TOK = 128
NEG = -1e30
RATE = math.log2(math.e) / math.sqrt(HD)
MIB = 2**20
VMEM = pl.BlockSpec(memory_space=pltpu.VMEM)
SMEM = pl.BlockSpec(memory_space=pltpu.SMEM)
WHOLE = pltpu.CompilerParams(vmem_limit_bytes=60 * MIB)
LOCAL = pltpu.CompilerParams(vmem_limit_bytes=24 * MIB)


def attend(q, k, v, bias):
    g = q.shape[0]
    scores = lax.dot_general(
        q.reshape(g * TOK, HD), k, (((1,), (1,)), ((), ())), preferred_element_type=jnp.float32
    )
    scores = scores.reshape(g, TOK, -1) + bias
    top = jnp.max(scores, axis=-1, keepdims=True)
    weights = jnp.exp2((scores - top) * RATE)
    total = jnp.sum(weights, axis=-1, keepdims=True)
    weights = weights.astype(jnp.bfloat16).reshape(g * TOK, -1)
    mixed = jnp.dot(weights, v, preferred_element_type=jnp.float32)
    return mixed.reshape(g, TOK, HD) / total


def student_head(pairs, first, sources, o_ref, o_at):
    (q_ref, q_at), (k_ref, k_at), (v_ref, v_at) = sources
    for i in pairs:
        width = (i + 2) * TOK
        block = lax.broadcasted_iota(jnp.int32, (2, 1, width), 2) // TOK
        own = lax.broadcasted_iota(jnp.int32, (2, 1, width), 0) + i
        bias = jnp.where((block == own) | (block >= first) & (block < own), 0.0, NEG)
        k = k_ref[0 : i + 2, k_at].reshape(width, HD)
        v = v_ref[0 : i + 2, v_at].reshape(width, HD)
        o_ref[i : i + 2, o_at] = attend(q_ref[i : i + 2, q_at], k, v, bias).astype(jnp.bfloat16)


def teacher_head(blocks, rows, clip_ref, sources, gen, o_ref, o_at):
    (q_ref, q_at), (k_ref, k_at) = sources
    reach = blocks // 2 + 1
    width = reach * TOK
    offset = lax.broadcasted_iota(jnp.int32, (1, 1, width), 2) // TOK
    for i in rows:
        low = clip_ref[0, i]
        high = clip_ref[1, i]
        start = jnp.minimum(low, blocks - reach)
        block = offset + start
        bias = jnp.where((block >= low) & (block < high), 0.0, NEG)
        k = k_ref[pl.ds(start, reach), k_at].reshape(width, HD)
        v = gen(pl.ds(start, reach)).reshape(width, HD)
        out = attend(q_ref[pl.ds(i, 1), q_at], k, v, bias)
        score = (out[0] - gen(i).astype(jnp.float32)).astype(jnp.bfloat16)
        if o_at is None:
            o_ref[1] = score
        else:
            o_ref[i, o_at] = score


def cost(heads, blocks, units):
    return pl.CostEstimate(
        flops=heads * blocks * blocks * 4 * TOK * TOK * HD,
        bytes_accessed=units * blocks * TOK * HD * 2,
        transcendentals=heads * blocks * blocks * TOK * TOK,
    )


def pack(plan, ranges, tensors):
    peers, units = len(plan), len(plan[0])
    widths = [count * HD for _, count in ranges]
    starts = [sum(widths[:r]) for r in range(len(ranges))]

    def place(h):
        for r, (head, count) in enumerate(ranges):
            if head <= h < head + count:
                return r, starts[r] + (h - head) * HD

    need = []
    for u in range(units):
        need.append(list(dict.fromkeys((plan[p][u][0], place(plan[p][u][1])[0]) for p in range(peers))))
    order = sorted(range(units), key=lambda u: (len(need[u]), u))
    fetch = list(dict.fromkeys(piece for u in order for piece in need[u]))

    def body(*refs):
        o_ref, rows, tiles, in_sem, out_sem = refs[len(tensors) :]
        copies = {}
        for n, (t, r) in enumerate(fetch):
            source = refs[t].at[0, :, pl.ds(ranges[r][0] * HD, widths[r])]
            target = rows.at[t, :, pl.ds(starts[r], widths[r])]
            copies[t, r] = pltpu.make_async_copy(source, target, in_sem.at[n])
            copies[t, r].start()
        sent = []
        for u in order:
            for piece in need[u]:
                if piece in copies:
                    copies.pop(piece).wait()
            for p in range(peers):
                t, h = plan[p][u]
                at = place(h)[1]
                tiles[p, u] = rows[t, :, at : at + HD]
            sent.append(pltpu.make_async_copy(tiles.at[:, u], o_ref.at[:, u], out_sem.at[u]))
            sent[-1].start()
        for copy in sent:
            copy.wait()

    return pl.pallas_call(
        body,
        in_specs=[pl.BlockSpec(memory_space=pl.ANY)] * len(tensors),
        out_specs=pl.BlockSpec(memory_space=pl.ANY),
        out_shape=jax.ShapeDtypeStruct((peers, units, TOK, HD), jnp.bfloat16),
        scratch_shapes=[
            pltpu.VMEM((len(tensors), TOK, sum(widths)), jnp.bfloat16),
            pltpu.VMEM((peers, units, TOK, HD), jnp.bfloat16),
            pltpu.SemaphoreType.DMA((len(fetch),)),
            pltpu.SemaphoreType.DMA((units,)),
        ],
        compiler_params=WHOLE,
        cost_estimate=cost(0, peers, 2 * units),
    )(*tensors)


def unpack(places, back):
    def body(x_ref, *o_refs):
        for o_ref, place in zip(o_refs, places):
            for h, (p, u) in enumerate(place):
                o_ref[0, :, h * HD : (h + 1) * HD] = x_ref[p, u]

    width = len(places[0]) * HD
    return pl.pallas_call(
        body,
        out_shape=[jax.ShapeDtypeStruct((1, TOK, width), jnp.bfloat16) for _ in places],
        compiler_params=LOCAL,
        cost_estimate=cost(0, 1, 4 * len(places[0])),
    )(back)


def student_kernel(blocks, first, role, arrived):
    def body(first_ref, role_ref, x_ref, o_ref):
        @pl.when(role_ref[0] == 1)
        def _():
            sources = [(x_ref, t) for t in range(3)]
            student_head(range(0, blocks, 2), first_ref[0], sources, o_ref, 0)

    return pl.pallas_call(
        body,
        in_specs=[SMEM, SMEM, VMEM],
        out_specs=VMEM,
        out_shape=jax.ShapeDtypeStruct((blocks, 1, TOK, HD), jnp.bfloat16),
        compiler_params=LOCAL,
        cost_estimate=cost(1, blocks, 4),
    )(first, role, arrived)


def rest_teacher(blocks, clips, role, arrived, offset, gen, shared):
    def body(clip_ref, role_ref, x_ref, gen_ref, shared_ref, o_ref):
        @pl.when(role_ref[0] == 1)
        def _():
            o_ref[...] = gen_ref[...]

        @pl.when(role_ref[0] == 2)
        def _():
            sources = [(x_ref, offset + t) for t in range(2)]
            teacher_head(
                blocks, range(blocks), clip_ref, sources, lambda at: shared_ref[at, 0], o_ref, 0
            )

    return pl.pallas_call(
        body,
        in_specs=[SMEM, SMEM, VMEM, VMEM, VMEM],
        out_specs=VMEM,
        out_shape=jax.ShapeDtypeStruct((blocks, 1, TOK, HD), jnp.bfloat16),
        compiler_params=LOCAL,
        cost_estimate=cost(1, blocks, 5),
    )(clips, role, arrived, gen, shared)


def slots_kernel(full, blocks, first, clips, arrived):
    def body(first_ref, clip_ref, x_ref, o_ref):
        def head(s, carry):
            sources = [(x_ref, 5 * s + t) for t in range(5)]
            student_head(range(0, blocks, 2), first_ref[0], sources[:3], o_ref, 2 * s)
            gen = lambda at: o_ref[at, 2 * s]
            teacher_head(blocks, range(blocks), clip_ref, sources[3:], gen, o_ref, 2 * s + 1)

        lax.fori_loop(0, full, head, None)

    return pl.pallas_call(
        body,
        in_specs=[SMEM, SMEM, VMEM],
        out_specs=VMEM,
        out_shape=jax.ShapeDtypeStruct((blocks, 2 * full, TOK, HD), jnp.bfloat16),
        compiler_params=LOCAL,
        cost_estimate=cost(2 * full, blocks, 7 * full),
    )(first, clips, arrived)


def rest_pack(base, columns, column, tensors):
    def body(column_ref, *refs):
        rows, sems = refs[-2:]
        copies = []
        for t in range(5):
            source = refs[t].at[0, :, pl.ds(base * HD, columns * HD)]
            copies.append(pltpu.make_async_copy(source, rows.at[t], sems.at[t]))
            copies[-1].start()
        for t in range(5):
            copies[t].wait()
            for s in range(columns):
                at = pl.multiple_of((column_ref[0] ^ s) * HD, HD)
                refs[5 + s][t] = rows[t, :, pl.ds(at, HD)]

    return pl.pallas_call(
        body,
        in_specs=[SMEM] + [pl.BlockSpec(memory_space=pl.ANY)] * 5,
        out_specs=[VMEM] * columns,
        out_shape=[jax.ShapeDtypeStruct((5, TOK, HD), jnp.bfloat16)] * columns,
        scratch_shapes=[
            pltpu.VMEM((5, TOK, columns * HD), jnp.bfloat16),
            pltpu.SemaphoreType.DMA((5,)),
        ],
        compiler_params=WHOLE,
        cost_estimate=cost(0, 1, 10 * columns),
    )(column, *tensors)


def rest_kernel(columns, first, clips, where, own, other):
    blocks = 2 * columns

    def body(first_ref, clip_ref, where_ref, *refs):
        x, gen = refs[-2:]
        column, side = where_ref[0], where_ref[1]
        mine = [2 * (column ^ s) + side for s in range(columns)]
        for s in range(columns):
            x[mine[s]] = refs[s][...]
            x[mine[s] ^ 1] = refs[columns + s][...]
        sources = [(x, t) for t in range(5)]
        student_head(range(0, blocks, 2), first_ref[0], sources[:3], gen, 0)
        at_gen = lambda at: gen[at, 0]
        for s in range(columns):
            o_ref = refs[2 * columns + s]
            o_ref[0:1] = gen[mine[s]]
            teacher_head(blocks, [mine[s]], clip_ref, sources[3:], at_gen, o_ref, None)

    return pl.pallas_call(
        body,
        in_specs=[SMEM] * 3 + [VMEM] * (2 * columns),
        out_specs=[VMEM] * columns,
        out_shape=[jax.ShapeDtypeStruct((2, TOK, HD), jnp.bfloat16)] * columns,
        scratch_shapes=[
            pltpu.VMEM((blocks, 5, TOK, HD), jnp.bfloat16),
            pltpu.VMEM((blocks, 1, TOK, HD), jnp.bfloat16),
        ],
        compiler_params=LOCAL,
        cost_estimate=cost(2, blocks, 7),
    )(first, clips, where, *own, *other)


def join(base, columns, places, column, back, pieces):
    def body(column_ref, x_ref, *refs):
        for i, o_ref in enumerate(refs[columns:]):
            for h, (p, u) in enumerate(places[i]):
                o_ref[0, :, h * HD : (h + 1) * HD] = x_ref[p, u]
            for s in range(columns):
                at = pl.multiple_of((base + (column_ref[0] ^ s)) * HD, HD)
                o_ref[0, :, pl.ds(at, HD)] = refs[s][i]

    width = (base + columns) * HD
    return pl.pallas_call(
        body,
        in_specs=[SMEM, VMEM] + [VMEM] * columns,
        out_specs=[VMEM] * 2,
        out_shape=[jax.ShapeDtypeStruct((1, TOK, width), jnp.bfloat16)] * 2,
        compiler_params=LOCAL,
        cost_estimate=cost(0, 1, 4 * (base + columns)),
    )(column, back, *pieces)


def by_slots_and_columns(tensors, peers, full, rest, first, clips):
    base = full * peers
    here = lax.axis_index("tm")
    column, side = here // 2, here % 2
    where = jnp.stack([column, side]).astype(jnp.int32)

    def swapped(x, by):
        return lax.ppermute(x, "tm", [(i, i ^ by) for i in range(peers)])

    plan = [[(t, s * peers + p) for s in range(full) for t in range(5)] for p in range(peers)]
    slots = [(s * peers, peers) for s in range(full)]
    pieces = rest_pack(base, rest, where[:1], tensors)
    own = [swapped(x, 2 * s) if s else x for s, x in enumerate(pieces)]
    other = [swapped(x, 1) for x in own]
    packed, _ = lax.optimization_barrier((pack(plan, slots, tensors), own))
    arrived = lax.all_to_all(packed, "tm", 0, 0)
    pieces = rest_kernel(rest, first, clips, where, own, other)
    pieces = [swapped(x, 2 * s) if s else x for s, x in enumerate(pieces)]
    arrived, _ = lax.optimization_barrier((arrived, pieces))
    back = lax.all_to_all(slots_kernel(full, peers, first, clips, arrived), "tm", 0, 0)
    places = [[(h % peers, 2 * (h // peers) + i) for h in range(base)] for i in (0, 1)]
    return tuple(join(base, rest, places, where[:1], back, pieces))


def by_roles(tensors, peers, heads, first, clips):
    here = lax.axis_index("tm")
    role = jnp.where(here < 2 * heads, 1 + here % 2, 0).astype(jnp.int32)[None]
    plan = [
        [(t, min(p // 2, heads - 1)) for t in ((3, 4, 4) if p % 2 else (0, 1, 2))]
        for p in range(peers)
    ]
    arrived = lax.all_to_all(pack(plan, [(0, heads)], tensors), "tm", 0, 0)
    gen = student_kernel(peers, first, role, arrived)
    shared = lax.ppermute(gen, "tm", [(2 * r, 2 * r + 1) for r in range(heads)])
    results = rest_teacher(peers, clips, role, arrived, 0, gen, shared)
    back = lax.all_to_all(results, "tm", 0, 0)
    return tuple(unpack([[(2 * r + i, 0) for r in range(heads)] for i in (0, 1)], back))


def per_device(student_q, student_k, student_v, teacher_q, teacher_k, stagger, clip_lengths):
    heads = student_q.shape[2] // HD
    peers = lax.axis_size("tm")
    full, rest = divmod(heads, peers)
    running = jnp.cumsum(clip_lengths[0])
    block = jnp.arange(peers, dtype=jnp.int32)
    before = running[None, :] <= block[:, None]
    low = jnp.max(jnp.where(before, running[None, :], 0), axis=1)
    high = jnp.min(jnp.where(before, peers, running[None, :]), axis=1)
    clips = jnp.stack([low, high]).astype(jnp.int32)
    tensors = (student_q, student_k, student_v, teacher_q, teacher_k)
    if full == 0:
        assert 2 * rest <= peers
        return by_roles(tensors, peers, rest, stagger, clips)
    assert peers == 2 * rest and rest & (rest - 1) == 0
    return by_slots_and_columns(tensors, peers, full, rest, stagger, clips)


def solution(mesh):
    spec = P("seq", "tm", "mp")
    return jax.shard_map(
        per_device,
        mesh=mesh,
        in_specs=(spec,) * 5 + (P("seq"), P("seq", None)),
        out_specs=(spec, spec),
        check_vma=False,
    )
```

```python
import functools
import math

import jax
import jax.numpy as jnp
from jax import lax
from jax.experimental import pallas as pl
from jax.experimental.pallas import tpu as pltpu
from jax.sharding import PartitionSpec as P

HD = 128
TOK = 128
NEG = -1e30
RATE = math.log2(math.e) / math.sqrt(HD)
MIB = 2**20
VMEM = pl.BlockSpec(memory_space=pltpu.VMEM)
SMEM = pl.BlockSpec(memory_space=pltpu.SMEM)
WHOLE = pltpu.CompilerParams(vmem_limit_bytes=60 * MIB)
LOCAL = pltpu.CompilerParams(vmem_limit_bytes=24 * MIB)


def attend(q, k, v, bias):
    g = q.shape[0]
    scores = lax.dot_general(
        q.reshape(g * TOK, HD), k, (((1,), (1,)), ((), ())), preferred_element_type=jnp.float32
    )
    scores = scores.reshape(g, TOK, -1) + bias
    top = jnp.max(scores, axis=-1, keepdims=True)
    weights = jnp.exp2((scores - top) * RATE)
    total = jnp.sum(weights, axis=-1, keepdims=True)
    weights = weights.astype(jnp.bfloat16).reshape(g * TOK, -1)
    mixed = jnp.dot(weights, v, preferred_element_type=jnp.float32)
    return mixed.reshape(g, TOK, HD) / total


def student_head(pairs, first, sources, o_ref, o_at):
    (q_ref, q_at), (k_ref, k_at), (v_ref, v_at) = sources
    for i in pairs:
        width = (i + 2) * TOK
        block = lax.broadcasted_iota(jnp.int32, (2, 1, width), 2) // TOK
        own = lax.broadcasted_iota(jnp.int32, (2, 1, width), 0) + i
        bias = jnp.where((block == own) | (block >= first) & (block < own), 0.0, NEG)
        k = k_ref[0 : i + 2, k_at].reshape(width, HD)
        v = v_ref[0 : i + 2, v_at].reshape(width, HD)
        o_ref[i : i + 2, o_at] = attend(q_ref[i : i + 2, q_at], k, v, bias).astype(jnp.bfloat16)


def teacher_head(blocks, rows, clip_ref, sources, gen, o_ref, o_at):
    (q_ref, q_at), (k_ref, k_at) = sources
    reach = blocks // 2 + 1
    width = reach * TOK
    offset = lax.broadcasted_iota(jnp.int32, (1, 1, width), 2) // TOK
    for i in rows:
        low = clip_ref[0, i]
        high = clip_ref[1, i]
        start = jnp.minimum(low, blocks - reach)
        block = offset + start
        bias = jnp.where((block >= low) & (block < high), 0.0, NEG)
        k = k_ref[pl.ds(start, reach), k_at].reshape(width, HD)
        v = gen(pl.ds(start, reach)).reshape(width, HD)
        out = attend(q_ref[pl.ds(i, 1), q_at], k, v, bias)
        score = (out[0] - gen(i).astype(jnp.float32)).astype(jnp.bfloat16)
        o_ref[i, o_at] = score


def cost(heads, blocks, units):
    return pl.CostEstimate(
        flops=heads * blocks * blocks * 4 * TOK * TOK * HD,
        bytes_accessed=units * blocks * TOK * HD * 2,
        transcendentals=heads * blocks * blocks * TOK * TOK,
    )


def pack(plan, ranges, tensors):
    peers, units = len(plan), len(plan[0])
    widths = [count * HD for _, count in ranges]
    starts = [sum(widths[:r]) for r in range(len(ranges))]

    def place(h):
        for r, (head, count) in enumerate(ranges):
            if head <= h < head + count:
                return r, starts[r] + (h - head) * HD

    need = []
    for u in range(units):
        need.append(list(dict.fromkeys((plan[p][u][0], place(plan[p][u][1])[0]) for p in range(peers))))
    order = sorted(range(units), key=lambda u: (len(need[u]), u))
    fetch = list(dict.fromkeys(piece for u in order for piece in need[u]))

    def body(*refs):
        o_ref, rows, tiles, in_sem, out_sem = refs[len(tensors) :]
        copies = {}
        for n, (t, r) in enumerate(fetch):
            source = refs[t].at[0, :, pl.ds(ranges[r][0] * HD, widths[r])]
            target = rows.at[t, :, pl.ds(starts[r], widths[r])]
            copies[t, r] = pltpu.make_async_copy(source, target, in_sem.at[n])
            copies[t, r].start()
        sent = []
        for u in order:
            for piece in need[u]:
                if piece in copies:
                    copies.pop(piece).wait()
            for p in range(peers):
                t, h = plan[p][u]
                at = place(h)[1]
                tiles[p, u] = rows[t, :, at : at + HD]
            sent.append(pltpu.make_async_copy(tiles.at[:, u], o_ref.at[:, u], out_sem.at[u]))
            sent[-1].start()
        for copy in sent:
            copy.wait()

    return pl.pallas_call(
        body,
        in_specs=[pl.BlockSpec(memory_space=pl.ANY)] * len(tensors),
        out_specs=pl.BlockSpec(memory_space=pl.ANY),
        out_shape=jax.ShapeDtypeStruct((peers, units, TOK, HD), jnp.bfloat16),
        scratch_shapes=[
            pltpu.VMEM((len(tensors), TOK, sum(widths)), jnp.bfloat16),
            pltpu.VMEM((peers, units, TOK, HD), jnp.bfloat16),
            pltpu.SemaphoreType.DMA((len(fetch),)),
            pltpu.SemaphoreType.DMA((units,)),
        ],
        compiler_params=WHOLE,
        cost_estimate=cost(0, peers, 2 * units),
    )(*tensors)


def unpack(places, back):
    def body(x_ref, *o_refs):
        for o_ref, place in zip(o_refs, places):
            for h, (p, u) in enumerate(place):
                o_ref[0, :, h * HD : (h + 1) * HD] = x_ref[p, u]

    width = len(places[0]) * HD
    return pl.pallas_call(
        body,
        out_shape=[jax.ShapeDtypeStruct((1, TOK, width), jnp.bfloat16) for _ in places],
        compiler_params=LOCAL,
        cost_estimate=cost(0, 1, 4 * len(places[0])),
    )(back)


def student_kernel(blocks, first, role, arrived):
    def body(first_ref, role_ref, x_ref, o_ref):
        @pl.when(role_ref[0] == 1)
        def _():
            sources = [(x_ref, t) for t in range(3)]
            student_head(range(0, blocks, 2), first_ref[0], sources, o_ref, 0)

    return pl.pallas_call(
        body,
        in_specs=[SMEM, SMEM, VMEM],
        out_specs=VMEM,
        out_shape=jax.ShapeDtypeStruct((blocks, 1, TOK, HD), jnp.bfloat16),
        compiler_params=LOCAL,
        cost_estimate=cost(1, blocks, 4),
    )(first, role, arrived)


def rest_teacher(blocks, clips, role, arrived, offset, gen, shared):
    def body(clip_ref, role_ref, x_ref, gen_ref, shared_ref, o_ref):
        @pl.when(role_ref[0] == 1)
        def _():
            o_ref[...] = gen_ref[...]

        @pl.when(role_ref[0] == 2)
        def _():
            sources = [(x_ref, offset + t) for t in range(2)]
            teacher_head(
                blocks, range(blocks), clip_ref, sources, lambda at: shared_ref[at, 0], o_ref, 0
            )

    return pl.pallas_call(
        body,
        in_specs=[SMEM, SMEM, VMEM, VMEM, VMEM],
        out_specs=VMEM,
        out_shape=jax.ShapeDtypeStruct((blocks, 1, TOK, HD), jnp.bfloat16),
        compiler_params=LOCAL,
        cost_estimate=cost(1, blocks, 5),
    )(clips, role, arrived, gen, shared)


def slots_kernel(full, blocks, first, clips, arrived):
    def body(first_ref, clip_ref, x_ref, o_ref):
        def head(s, carry):
            sources = [(x_ref, 5 * s + t) for t in range(5)]
            student_head(range(0, blocks, 2), first_ref[0], sources[:3], o_ref, 2 * s)
            gen = lambda at: o_ref[at, 2 * s]
            teacher_head(blocks, range(blocks), clip_ref, sources[3:], gen, o_ref, 2 * s + 1)

        lax.fori_loop(0, full, head, None)

    return pl.pallas_call(
        body,
        in_specs=[SMEM, SMEM, VMEM],
        out_specs=VMEM,
        out_shape=jax.ShapeDtypeStruct((blocks, 2 * full, TOK, HD), jnp.bfloat16),
        compiler_params=LOCAL,
        cost_estimate=cost(2 * full, blocks, 7 * full),
    )(first, clips, arrived)


def rest_pack(base, columns, column, tensors):
    def body(column_ref, *refs):
        rows, sems = refs[-2:]
        copies = []
        for t in range(5):
            source = refs[t].at[0, :, pl.ds(base * HD, columns * HD)]
            copies.append(pltpu.make_async_copy(source, rows.at[t], sems.at[t]))
            copies[-1].start()
        for t in range(5):
            copies[t].wait()
            for s in range(columns):
                at = pl.multiple_of((column_ref[0] ^ s) * HD, HD)
                refs[5 + s][t] = rows[t, :, pl.ds(at, HD)]

    return pl.pallas_call(
        body,
        in_specs=[SMEM] + [pl.BlockSpec(memory_space=pl.ANY)] * 5,
        out_specs=[VMEM] * columns,
        out_shape=[jax.ShapeDtypeStruct((5, TOK, HD), jnp.bfloat16)] * columns,
        scratch_shapes=[
            pltpu.VMEM((5, TOK, columns * HD), jnp.bfloat16),
            pltpu.SemaphoreType.DMA((5,)),
        ],
        compiler_params=WHOLE,
        cost_estimate=cost(0, 1, 10 * columns),
    )(column, *tensors)


def rest_kernel(blocks, first, clips, where, arrived):
    def body(first_ref, clip_ref, where_ref, *refs):
        x_refs, o_refs, (x, y) = refs[:blocks], refs[blocks : 2 * blocks], refs[2 * blocks :]

        @pl.when(where_ref[1] == 0)
        def _():
            at = [2 * where_ref[0] ^ d for d in range(blocks)]
            for d in range(blocks):
                x[at[d]] = x_refs[d][...]
            sources = [(x, t) for t in range(5)]
            student_head(range(0, blocks, 2), first_ref[0], sources[:3], y, 0)
            gen = lambda at: y[at, 0]
            teacher_head(blocks, range(blocks), clip_ref, sources[3:], gen, y, 1)
            for d in range(blocks):
                o_refs[d][...] = y[at[d]]

    return pl.pallas_call(
        body,
        in_specs=[SMEM] * 3 + [VMEM] * blocks,
        out_specs=[VMEM] * blocks,
        out_shape=[jax.ShapeDtypeStruct((2, TOK, HD), jnp.bfloat16)] * blocks,
        scratch_shapes=[
            pltpu.VMEM((blocks, 5, TOK, HD), jnp.bfloat16),
            pltpu.VMEM((blocks, 2, TOK, HD), jnp.bfloat16),
        ],
        compiler_params=LOCAL,
        cost_estimate=cost(2, blocks, 7),
    )(first, clips, where, *arrived)


def join(base, columns, places, where, back, pieces):
    def body(where_ref, x_ref, *refs):
        column, side = where_ref[0], where_ref[1]
        for i, o_ref in enumerate(refs[2 * columns :]):
            for h, (p, u) in enumerate(places[i]):
                o_ref[0, :, h * HD : (h + 1) * HD] = x_ref[p, u]
            for s in range(columns):
                at = pl.ds(pl.multiple_of((base + (column ^ s)) * HD, HD), HD)
                o_ref[0, :, at] = jnp.where(side == 0, refs[2 * s][i], refs[2 * s + 1][i])

    width = (base + columns) * HD
    return pl.pallas_call(
        body,
        in_specs=[SMEM, VMEM] + [VMEM] * (2 * columns),
        out_specs=[VMEM] * 2,
        out_shape=[jax.ShapeDtypeStruct((1, TOK, width), jnp.bfloat16)] * 2,
        compiler_params=LOCAL,
        cost_estimate=cost(0, 1, 4 * (base + columns)),
    )(where, back, *pieces)


def by_slots_and_columns(tensors, peers, full, rest, first, clips):
    base = full * peers
    here = lax.axis_index("tm")
    where = jnp.stack([here // 2, here % 2]).astype(jnp.int32)

    def sent(x, d, home):
        pairs = [(i, i ^ d) for i in range(peers) if (i if home else i ^ d) % 2 == 0]
        return lax.ppermute(x, "tm", pairs) if d else x

    plan = [[(t, s * peers + p) for s in range(full) for t in range(5)] for p in range(peers)]
    slots = [(s * peers, peers) for s in range(full)]
    arrived = lax.all_to_all(pack(plan, slots, tensors), "tm", 0, 0)
    pieces = rest_pack(base, rest, where[:1], tensors)
    middle = rest // 2
    near = [sent(pieces[d // 2], d, False) for d in range(2 * middle)]
    arrived, far = lax.optimization_barrier((arrived, pieces[middle:]))
    far = [sent(far[d // 2 - middle], d, False) for d in range(2 * middle, peers)]
    results = slots_kernel(full, peers, first, clips, arrived)
    results, near, far = lax.optimization_barrier((results, near, far))
    back = lax.all_to_all(results, "tm", 0, 0)
    pieces = rest_kernel(peers, first, clips, where, near + far)
    pieces = [sent(x, d, True) for d, x in enumerate(pieces)]
    places = [[(h % peers, 2 * (h // peers) + i) for h in range(base)] for i in (0, 1)]
    return tuple(join(base, rest, places, where, back, pieces))


def by_roles(tensors, peers, heads, first, clips):
    here = lax.axis_index("tm")
    role = jnp.where(here < 2 * heads, 1 + here % 2, 0).astype(jnp.int32)[None]
    plan = [
        [(t, min(p // 2, heads - 1)) for t in ((3, 4, 4) if p % 2 else (0, 1, 2))]
        for p in range(peers)
    ]
    arrived = lax.all_to_all(pack(plan, [(0, heads)], tensors), "tm", 0, 0)
    gen = student_kernel(peers, first, role, arrived)
    shared = lax.ppermute(gen, "tm", [(2 * r, 2 * r + 1) for r in range(heads)])
    results = rest_teacher(peers, clips, role, arrived, 0, gen, shared)
    back = lax.all_to_all(results, "tm", 0, 0)
    return tuple(unpack([[(2 * r + i, 0) for r in range(heads)] for i in (0, 1)], back))


def per_device(student_q, student_k, student_v, teacher_q, teacher_k, stagger, clip_lengths):
    heads = student_q.shape[2] // HD
    peers = lax.axis_size("tm")
    full, rest = divmod(heads, peers)
    running = jnp.cumsum(clip_lengths[0])
    block = jnp.arange(peers, dtype=jnp.int32)
    before = running[None, :] <= block[:, None]
    low = jnp.max(jnp.where(before, running[None, :], 0), axis=1)
    high = jnp.min(jnp.where(before, peers, running[None, :]), axis=1)
    clips = jnp.stack([low, high]).astype(jnp.int32)
    tensors = (student_q, student_k, student_v, teacher_q, teacher_k)
    if full == 0:
        assert 2 * rest <= peers
        return by_roles(tensors, peers, rest, stagger, clips)
    assert peers == 2 * rest and rest & (rest - 1) == 0
    return by_slots_and_columns(tensors, peers, full, rest, stagger, clips)


def solution(mesh):
    spec = P("seq", "tm", "mp")
    return jax.shard_map(
        per_device,
        mesh=mesh,
        in_specs=(spec,) * 5 + (P("seq"), P("seq", None)),
        out_specs=(spec, spec),
        check_vma=False,
    )
```

```python
import functools
import math

import jax
import jax.numpy as jnp
from jax import lax
from jax.experimental import pallas as pl
from jax.experimental.pallas import tpu as pltpu
from jax.sharding import PartitionSpec as P

HD = 128
TOK = 128
NEG = -1e30
RATE = math.log2(math.e) / math.sqrt(HD)
MIB = 2**20
VMEM = pl.BlockSpec(memory_space=pltpu.VMEM)
SMEM = pl.BlockSpec(memory_space=pltpu.SMEM)
WHOLE = pltpu.CompilerParams(vmem_limit_bytes=60 * MIB)
LOCAL = pltpu.CompilerParams(vmem_limit_bytes=24 * MIB)


def attend(q, k, v, bias):
    g = q.shape[0]
    scores = lax.dot_general(
        q.reshape(g * TOK, HD), k, (((1,), (1,)), ((), ())), preferred_element_type=jnp.float32
    )
    scores = scores.reshape(g, TOK, -1)
    if bias is not None:
        scores = scores + bias
    top = jnp.max(scores, axis=-1, keepdims=True)
    weights = jnp.exp2((scores - top) * RATE)
    total = jnp.sum(weights, axis=-1, keepdims=True)
    weights = weights.astype(jnp.bfloat16).reshape(g * TOK, -1)
    mixed = jnp.dot(weights, v, preferred_element_type=jnp.float32)
    return mixed.reshape(g, TOK, HD) / total


def student_head(pairs, first, sources, o_ref, o_at):
    (q_ref, q_at), (k_ref, k_at), (v_ref, v_at) = sources
    for i in pairs:
        width = (i + 2) * TOK
        block = lax.broadcasted_iota(jnp.int32, (2, 1, width), 2) // TOK
        own = lax.broadcasted_iota(jnp.int32, (2, 1, width), 0) + i
        bias = jnp.where((block == own) | (block >= first) & (block < own), 0.0, NEG)
        k = k_ref[0 : i + 2, k_at].reshape(width, HD)
        v = v_ref[0 : i + 2, v_at].reshape(width, HD)
        o_ref[i : i + 2, o_at] = attend(q_ref[i : i + 2, q_at], k, v, bias).astype(jnp.bfloat16)


def teacher_head(blocks, rows, clip_ref, sources, gen, o_ref, o_at):
    (q_ref, q_at), (k_ref, k_at) = sources
    reach = blocks // 2 + 1
    width = reach * TOK
    offset = lax.broadcasted_iota(jnp.int32, (1, 1, width), 2) // TOK
    for i in rows:
        low = clip_ref[0, i]
        high = clip_ref[1, i]
        start = jnp.minimum(low, blocks - reach)
        block = offset + start
        bias = jnp.where((block >= low) & (block < high), 0.0, NEG)
        k = k_ref[pl.ds(start, reach), k_at].reshape(width, HD)
        v = gen(pl.ds(start, reach)).reshape(width, HD)
        out = attend(q_ref[pl.ds(i, 1), q_at], k, v, bias)
        score = (out[0] - gen(i).astype(jnp.float32)).astype(jnp.bfloat16)
        if o_at is None:
            o_ref[1] = score
        else:
            o_ref[i, o_at] = score


def teacher_whole_head(blocks, clip_ref, sources, gen, o_ref, o_at):
    (q_ref, q_at), (k_ref, k_at) = sources
    reach = blocks // 2 + 1

    def put(at, out):
        score = out - gen(at).astype(jnp.float32)
        o_ref[at, o_at] = score.astype(jnp.bfloat16)

    large = clip_ref[2, 0]
    k = k_ref[pl.ds(large, reach), k_at].reshape(reach * TOK, HD)
    v = gen(pl.ds(large, reach)).reshape(reach * TOK, HD)
    for i in range(0, reach, 2):
        at = pl.ds(large + i, min(2, reach - i))
        put(at, attend(q_ref[at, q_at], k, v, None))
    span = blocks - reach - 1
    offset = lax.broadcasted_iota(jnp.int32, (1, 1, span * TOK), 2) // TOK
    for j in range(blocks - reach):
        i = jnp.where(j < large, j, j + reach)
        low, high = clip_ref[0, i], clip_ref[1, i]
        start = jnp.minimum(low, blocks - span)
        block = offset + start
        bias = jnp.where((block >= low) & (block < high), 0.0, NEG)
        k = k_ref[pl.ds(start, span), k_at].reshape(span * TOK, HD)
        v = gen(pl.ds(start, span)).reshape(span * TOK, HD)
        put(pl.ds(i, 1), attend(q_ref[pl.ds(i, 1), q_at], k, v, bias))


def cost(heads, blocks, units):
    return pl.CostEstimate(
        flops=heads * blocks * blocks * 4 * TOK * TOK * HD,
        bytes_accessed=units * blocks * TOK * HD * 2,
        transcendentals=heads * blocks * blocks * TOK * TOK,
    )


def pack(plan, ranges, tensors):
    peers, units = len(plan), len(plan[0])
    widths = [count * HD for _, count in ranges]
    starts = [sum(widths[:r]) for r in range(len(ranges))]

    def place(h):
        for r, (head, count) in enumerate(ranges):
            if head <= h < head + count:
                return r, starts[r] + (h - head) * HD

    need = []
    for u in range(units):
        need.append(list(dict.fromkeys((plan[p][u][0], place(plan[p][u][1])[0]) for p in range(peers))))
    order = sorted(range(units), key=lambda u: (len(need[u]), u))
    fetch = list(dict.fromkeys(piece for u in order for piece in need[u]))

    def body(*refs):
        o_ref, rows, tiles, in_sem, out_sem = refs[len(tensors) :]
        copies = {}
        for n, (t, r) in enumerate(fetch):
            source = refs[t].at[0, :, pl.ds(ranges[r][0] * HD, widths[r])]
            target = rows.at[t, :, pl.ds(starts[r], widths[r])]
            copies[t, r] = pltpu.make_async_copy(source, target, in_sem.at[n])
            copies[t, r].start()
        sent = []
        for u in order:
            for piece in need[u]:
                if piece in copies:
                    copies.pop(piece).wait()
            for p in range(peers):
                t, h = plan[p][u]
                at = place(h)[1]
                tiles[p, u] = rows[t, :, at : at + HD]
            sent.append(pltpu.make_async_copy(tiles.at[:, u], o_ref.at[:, u], out_sem.at[u]))
            sent[-1].start()
        for copy in sent:
            copy.wait()

    return pl.pallas_call(
        body,
        in_specs=[pl.BlockSpec(memory_space=pl.ANY)] * len(tensors),
        out_specs=pl.BlockSpec(memory_space=pl.ANY),
        out_shape=jax.ShapeDtypeStruct((peers, units, TOK, HD), jnp.bfloat16),
        scratch_shapes=[
            pltpu.VMEM((len(tensors), TOK, sum(widths)), jnp.bfloat16),
            pltpu.VMEM((peers, units, TOK, HD), jnp.bfloat16),
            pltpu.SemaphoreType.DMA((len(fetch),)),
            pltpu.SemaphoreType.DMA((units,)),
        ],
        compiler_params=WHOLE,
        cost_estimate=cost(0, peers, 2 * units),
    )(*tensors)


def unpack(places, back):
    def body(x_ref, *o_refs):
        for o_ref, place in zip(o_refs, places):
            for h, (p, u) in enumerate(place):
                o_ref[0, :, h * HD : (h + 1) * HD] = x_ref[p, u]

    width = len(places[0]) * HD
    return pl.pallas_call(
        body,
        out_shape=[jax.ShapeDtypeStruct((1, TOK, width), jnp.bfloat16) for _ in places],
        compiler_params=LOCAL,
        cost_estimate=cost(0, 1, 4 * len(places[0])),
    )(back)


def student_kernel(blocks, first, role, arrived):
    def body(first_ref, role_ref, x_ref, o_ref):
        @pl.when(role_ref[0] == 1)
        def _():
            sources = [(x_ref, t) for t in range(3)]
            student_head(range(0, blocks, 2), first_ref[0], sources, o_ref, 0)

    return pl.pallas_call(
        body,
        in_specs=[SMEM, SMEM, VMEM],
        out_specs=VMEM,
        out_shape=jax.ShapeDtypeStruct((blocks, 1, TOK, HD), jnp.bfloat16),
        compiler_params=LOCAL,
        cost_estimate=cost(1, blocks, 4),
    )(first, role, arrived)


def rest_teacher(blocks, clips, role, arrived, offset, gen, shared):
    def body(clip_ref, role_ref, x_ref, gen_ref, shared_ref, o_ref):
        @pl.when(role_ref[0] == 1)
        def _():
            o_ref[...] = gen_ref[...]

        @pl.when(role_ref[0] == 2)
        def _():
            sources = [(x_ref, offset + t) for t in range(2)]
            teacher_head(
                blocks, range(blocks), clip_ref, sources, lambda at: shared_ref[at, 0], o_ref, 0
            )

    return pl.pallas_call(
        body,
        in_specs=[SMEM, SMEM, VMEM, VMEM, VMEM],
        out_specs=VMEM,
        out_shape=jax.ShapeDtypeStruct((blocks, 1, TOK, HD), jnp.bfloat16),
        compiler_params=LOCAL,
        cost_estimate=cost(1, blocks, 5),
    )(clips, role, arrived, gen, shared)


def slots_kernel(full, blocks, first, clips, arrived):
    def body(first_ref, clip_ref, x_ref, o_ref):
        def head(s, carry):
            sources = [(x_ref, 5 * s + t) for t in range(5)]
            student_head(range(0, blocks, 2), first_ref[0], sources[:3], o_ref, 2 * s)
            gen = lambda at: o_ref[at, 2 * s]
            teacher_whole_head(blocks, clip_ref, sources[3:], gen, o_ref, 2 * s + 1)

        lax.fori_loop(0, full, head, None)

    return pl.pallas_call(
        body,
        in_specs=[SMEM, SMEM, VMEM],
        out_specs=VMEM,
        out_shape=jax.ShapeDtypeStruct((blocks, 2 * full, TOK, HD), jnp.bfloat16),
        compiler_params=LOCAL,
        cost_estimate=cost(2 * full, blocks, 7 * full),
    )(first, clips, arrived)


def rest_pack(base, columns, column, tensors):
    def body(column_ref, *refs):
        rows, sems = refs[-2:]
        copies = []
        for t in range(5):
            source = refs[t].at[0, :, pl.ds(base * HD, columns * HD)]
            copies.append(pltpu.make_async_copy(source, rows.at[t], sems.at[t]))
            copies[-1].start()
        for t in range(5):
            copies[t].wait()
            for s in range(columns):
                at = pl.multiple_of((column_ref[0] ^ s) * HD, HD)
                refs[5 + s][t] = rows[t, :, pl.ds(at, HD)]

    return pl.pallas_call(
        body,
        in_specs=[SMEM] + [pl.BlockSpec(memory_space=pl.ANY)] * 5,
        out_specs=[VMEM] * columns,
        out_shape=[jax.ShapeDtypeStruct((5, TOK, HD), jnp.bfloat16)] * columns,
        scratch_shapes=[
            pltpu.VMEM((5, TOK, columns * HD), jnp.bfloat16),
            pltpu.SemaphoreType.DMA((5,)),
        ],
        compiler_params=WHOLE,
        cost_estimate=cost(0, 1, 10 * columns),
    )(column, *tensors)


def rest_kernel(columns, first, clips, where, own, other):
    blocks = 2 * columns

    def body(first_ref, clip_ref, where_ref, *refs):
        x, gen = refs[-2:]
        column, side = where_ref[0], where_ref[1]
        mine = [2 * (column ^ s) + side for s in range(columns)]
        for s in range(columns):
            x[mine[s]] = refs[s][...]
            x[mine[s] ^ 1] = refs[columns + s][...]
        sources = [(x, t) for t in range(5)]
        student_head(range(0, blocks, 2), first_ref[0], sources[:3], gen, 0)
        at_gen = lambda at: gen[at, 0]
        for s in range(columns):
            o_ref = refs[2 * columns + s]
            o_ref[0:1] = gen[mine[s]]
            teacher_head(blocks, [mine[s]], clip_ref, sources[3:], at_gen, o_ref, None)

    return pl.pallas_call(
        body,
        in_specs=[SMEM] * 3 + [VMEM] * (2 * columns),
        out_specs=[VMEM] * columns,
        out_shape=[jax.ShapeDtypeStruct((2, TOK, HD), jnp.bfloat16)] * columns,
        scratch_shapes=[
            pltpu.VMEM((blocks, 5, TOK, HD), jnp.bfloat16),
            pltpu.VMEM((blocks, 1, TOK, HD), jnp.bfloat16),
        ],
        compiler_params=LOCAL,
        cost_estimate=cost(2, blocks, 7),
    )(first, clips, where, *own, *other)


def join(base, columns, places, column, back, pieces):
    def body(column_ref, x_ref, *refs):
        for i, o_ref in enumerate(refs[columns:]):
            for h, (p, u) in enumerate(places[i]):
                o_ref[0, :, h * HD : (h + 1) * HD] = x_ref[p, u]
            for s in range(columns):
                at = pl.multiple_of((base + (column_ref[0] ^ s)) * HD, HD)
                o_ref[0, :, pl.ds(at, HD)] = refs[s][i]

    width = (base + columns) * HD
    return pl.pallas_call(
        body,
        in_specs=[SMEM, VMEM] + [VMEM] * columns,
        out_specs=[VMEM] * 2,
        out_shape=[jax.ShapeDtypeStruct((1, TOK, width), jnp.bfloat16)] * 2,
        compiler_params=LOCAL,
        cost_estimate=cost(0, 1, 4 * (base + columns)),
    )(column, back, *pieces)


def by_slots_and_columns(tensors, peers, full, rest, first, clips):
    base = full * peers
    here = lax.axis_index("tm")
    column, side = here // 2, here % 2
    where = jnp.stack([column, side]).astype(jnp.int32)

    def swapped(x, by):
        return lax.ppermute(x, "tm", [(i, i ^ by) for i in range(peers)])

    plan = [[(t, s * peers + p) for s in range(full) for t in range(5)] for p in range(peers)]
    slots = [(s * peers, peers) for s in range(full)]
    pieces = rest_pack(base, rest, where[:1], tensors)
    own = [swapped(x, 2 * s) if s else x for s, x in enumerate(pieces)]
    other = [swapped(x, 1) for x in own]
    packed, _ = lax.optimization_barrier((pack(plan, slots, tensors), own))
    arrived = lax.all_to_all(packed, "tm", 0, 0)
    pieces = rest_kernel(rest, first, clips, where, own, other)
    arrived, _ = lax.optimization_barrier((arrived, pieces))
    results = slots_kernel(full, peers, first, clips, arrived)
    pieces = [swapped(x, 2 * s) if s else x for s, x in enumerate(pieces)]
    results, pieces = lax.optimization_barrier((results, pieces))
    back = lax.all_to_all(results, "tm", 0, 0)
    places = [[(h % peers, 2 * (h // peers) + i) for h in range(base)] for i in (0, 1)]
    return tuple(join(base, rest, places, where[:1], back, pieces))


def by_roles(tensors, peers, heads, first, clips):
    here = lax.axis_index("tm")
    role = jnp.where(here < 2 * heads, 1 + here % 2, 0).astype(jnp.int32)[None]
    plan = [
        [(t, min(p // 2, heads - 1)) for t in ((3, 4, 4) if p % 2 else (0, 1, 2))]
        for p in range(peers)
    ]
    arrived = lax.all_to_all(pack(plan, [(0, heads)], tensors), "tm", 0, 0)
    gen = student_kernel(peers, first, role, arrived)
    shared = lax.ppermute(gen, "tm", [(2 * r, 2 * r + 1) for r in range(heads)])
    results = rest_teacher(peers, clips, role, arrived, 0, gen, shared)
    back = lax.all_to_all(results, "tm", 0, 0)
    return tuple(unpack([[(2 * r + i, 0) for r in range(heads)] for i in (0, 1)], back))


def per_device(student_q, student_k, student_v, teacher_q, teacher_k, stagger, clip_lengths):
    heads = student_q.shape[2] // HD
    peers = lax.axis_size("tm")
    full, rest = divmod(heads, peers)
    running = jnp.cumsum(clip_lengths[0])
    block = jnp.arange(peers, dtype=jnp.int32)
    before = running[None, :] <= block[:, None]
    low = jnp.max(jnp.where(before, running[None, :], 0), axis=1)
    high = jnp.min(jnp.where(before, peers, running[None, :]), axis=1)
    large = jnp.where(clip_lengths[0] == peers // 2 + 1, running - clip_lengths[0], 0)
    large = jnp.broadcast_to(jnp.max(large), (peers,))
    clips = jnp.stack([low, high, large]).astype(jnp.int32)
    tensors = (student_q, student_k, student_v, teacher_q, teacher_k)
    if full == 0:
        assert 2 * rest <= peers
        return by_roles(tensors, peers, rest, stagger, clips)
    assert peers == 2 * rest and rest & (rest - 1) == 0
    return by_slots_and_columns(tensors, peers, full, rest, stagger, clips)


def solution(mesh):
    spec = P("seq", "tm", "mp")
    return jax.shard_map(
        per_device,
        mesh=mesh,
        in_specs=(spec,) * 5 + (P("seq"), P("seq", None)),
        out_specs=(spec, spec),
        check_vma=False,
    )
```

```python
import functools
import math

import jax
import jax.numpy as jnp
from jax import lax
from jax.experimental import pallas as pl
from jax.experimental.pallas import tpu as pltpu
from jax.sharding import PartitionSpec as P

HD = 128
TOK = 128
NEG = -1e30
RATE = math.log2(math.e) / math.sqrt(HD)
MIB = 2**20
VMEM = pl.BlockSpec(memory_space=pltpu.VMEM)
SMEM = pl.BlockSpec(memory_space=pltpu.SMEM)
WHOLE = pltpu.CompilerParams(vmem_limit_bytes=60 * MIB)
LOCAL = pltpu.CompilerParams(vmem_limit_bytes=24 * MIB)


def attend(q, k, v, bias):
    g = q.shape[0]
    scores = lax.dot_general(
        q.reshape(g * TOK, HD), k, (((1,), (1,)), ((), ())), preferred_element_type=jnp.float32
    )
    scores = scores.reshape(g, TOK, -1)
    if bias is not None:
        scores = scores + bias
    top = jnp.max(scores, axis=-1, keepdims=True)
    weights = jnp.exp2((scores - top) * RATE)
    total = jnp.sum(weights, axis=-1, keepdims=True)
    weights = weights.astype(jnp.bfloat16).reshape(g * TOK, -1)
    mixed = jnp.dot(weights, v, preferred_element_type=jnp.float32)
    return mixed.reshape(g, TOK, HD) / total


def student_head(pairs, first, sources, o_ref, o_at):
    (q_ref, q_at), (k_ref, k_at), (v_ref, v_at) = sources
    for i in pairs:
        width = (i + 2) * TOK
        block = lax.broadcasted_iota(jnp.int32, (2, 1, width), 2) // TOK
        own = lax.broadcasted_iota(jnp.int32, (2, 1, width), 0) + i
        bias = jnp.where((block == own) | (block >= first) & (block < own), 0.0, NEG)
        k = k_ref[0 : i + 2, k_at].reshape(width, HD)
        v = v_ref[0 : i + 2, v_at].reshape(width, HD)
        o_ref[i : i + 2, o_at] = attend(q_ref[i : i + 2, q_at], k, v, bias).astype(jnp.bfloat16)


def teacher_head(blocks, rows, clip_ref, sources, gen, o_ref, o_at):
    (q_ref, q_at), (k_ref, k_at) = sources
    reach = blocks // 2 + 1
    width = reach * TOK
    offset = lax.broadcasted_iota(jnp.int32, (1, 1, width), 2) // TOK
    for i in rows:
        low = clip_ref[0, i]
        high = clip_ref[1, i]
        start = jnp.minimum(low, blocks - reach)
        block = offset + start
        bias = jnp.where((block >= low) & (block < high), 0.0, NEG)
        k = k_ref[pl.ds(start, reach), k_at].reshape(width, HD)
        v = gen(pl.ds(start, reach)).reshape(width, HD)
        out = attend(q_ref[pl.ds(i, 1), q_at], k, v, bias)
        score = (out[0] - gen(i).astype(jnp.float32)).astype(jnp.bfloat16)
        if o_at is None:
            o_ref[1] = score
        else:
            o_ref[i, o_at] = score


def teacher_whole_head(blocks, clip_ref, sources, gen, o_ref, o_at):
    (q_ref, q_at), (k_ref, k_at) = sources
    reach = blocks // 2 + 1

    def put(at, out):
        score = out - gen(at).astype(jnp.float32)
        o_ref[at, o_at] = score.astype(jnp.bfloat16)

    large = clip_ref[2, 0]
    k = k_ref[pl.ds(large, reach), k_at].reshape(reach * TOK, HD)
    v = gen(pl.ds(large, reach)).reshape(reach * TOK, HD)
    for i in range(0, reach, 2):
        at = pl.ds(large + i, min(2, reach - i))
        put(at, attend(q_ref[at, q_at], k, v, None))
    span = blocks - reach - 1
    offset = lax.broadcasted_iota(jnp.int32, (1, 1, span * TOK), 2) // TOK
    for j in range(blocks - reach):
        i = jnp.where(j < large, j, j + reach)
        low, high = clip_ref[0, i], clip_ref[1, i]
        start = jnp.minimum(low, blocks - span)
        block = offset + start
        bias = jnp.where((block >= low) & (block < high), 0.0, NEG)
        k = k_ref[pl.ds(start, span), k_at].reshape(span * TOK, HD)
        v = gen(pl.ds(start, span)).reshape(span * TOK, HD)
        put(pl.ds(i, 1), attend(q_ref[pl.ds(i, 1), q_at], k, v, bias))


def cost(heads, blocks, units):
    return pl.CostEstimate(
        flops=heads * blocks * blocks * 4 * TOK * TOK * HD,
        bytes_accessed=units * blocks * TOK * HD * 2,
        transcendentals=heads * blocks * blocks * TOK * TOK,
    )


def pack(plan, ranges, tensors):
    peers, units = len(plan), len(plan[0])
    widths = [count * HD for _, count in ranges]
    starts = [sum(widths[:r]) for r in range(len(ranges))]

    def place(h):
        for r, (head, count) in enumerate(ranges):
            if head <= h < head + count:
                return r, starts[r] + (h - head) * HD

    need = []
    for u in range(units):
        need.append(list(dict.fromkeys((plan[p][u][0], place(plan[p][u][1])[0]) for p in range(peers))))
    order = sorted(range(units), key=lambda u: (len(need[u]), u))
    fetch = list(dict.fromkeys(piece for u in order for piece in need[u]))

    def body(*refs):
        o_ref, rows, tiles, in_sem, out_sem = refs[len(tensors) :]
        copies = {}
        for n, (t, r) in enumerate(fetch):
            source = refs[t].at[0, :, pl.ds(ranges[r][0] * HD, widths[r])]
            target = rows.at[t, :, pl.ds(starts[r], widths[r])]
            copies[t, r] = pltpu.make_async_copy(source, target, in_sem.at[n])
            copies[t, r].start()
        sent = []
        for u in order:
            for piece in need[u]:
                if piece in copies:
                    copies.pop(piece).wait()
            for p in range(peers):
                t, h = plan[p][u]
                at = place(h)[1]
                tiles[p, u] = rows[t, :, at : at + HD]
            sent.append(pltpu.make_async_copy(tiles.at[:, u], o_ref.at[:, u], out_sem.at[u]))
            sent[-1].start()
        for copy in sent:
            copy.wait()

    return pl.pallas_call(
        body,
        in_specs=[pl.BlockSpec(memory_space=pl.ANY)] * len(tensors),
        out_specs=pl.BlockSpec(memory_space=pl.ANY),
        out_shape=jax.ShapeDtypeStruct((peers, units, TOK, HD), jnp.bfloat16),
        scratch_shapes=[
            pltpu.VMEM((len(tensors), TOK, sum(widths)), jnp.bfloat16),
            pltpu.VMEM((peers, units, TOK, HD), jnp.bfloat16),
            pltpu.SemaphoreType.DMA((len(fetch),)),
            pltpu.SemaphoreType.DMA((units,)),
        ],
        compiler_params=WHOLE,
        cost_estimate=cost(0, peers, 2 * units),
    )(*tensors)


def unpack(places, back):
    def body(x_ref, *o_refs):
        for o_ref, place in zip(o_refs, places):
            for h, (p, u) in enumerate(place):
                o_ref[0, :, h * HD : (h + 1) * HD] = x_ref[p, u]

    width = len(places[0]) * HD
    return pl.pallas_call(
        body,
        out_shape=[jax.ShapeDtypeStruct((1, TOK, width), jnp.bfloat16) for _ in places],
        compiler_params=LOCAL,
        cost_estimate=cost(0, 1, 4 * len(places[0])),
    )(back)


def student_kernel(blocks, first, role, arrived):
    def body(first_ref, role_ref, x_ref, o_ref):
        @pl.when(role_ref[0] == 1)
        def _():
            sources = [(x_ref, t) for t in range(3)]
            student_head(range(0, blocks, 2), first_ref[0], sources, o_ref, 0)

    return pl.pallas_call(
        body,
        in_specs=[SMEM, SMEM, VMEM],
        out_specs=VMEM,
        out_shape=jax.ShapeDtypeStruct((blocks, 1, TOK, HD), jnp.bfloat16),
        compiler_params=LOCAL,
        cost_estimate=cost(1, blocks, 4),
    )(first, role, arrived)


def rest_teacher(blocks, clips, role, arrived, offset, gen, shared):
    def body(clip_ref, role_ref, x_ref, gen_ref, shared_ref, o_ref):
        @pl.when(role_ref[0] == 1)
        def _():
            o_ref[...] = gen_ref[...]

        @pl.when(role_ref[0] == 2)
        def _():
            sources = [(x_ref, offset + t) for t in range(2)]
            teacher_head(
                blocks, range(blocks), clip_ref, sources, lambda at: shared_ref[at, 0], o_ref, 0
            )

    return pl.pallas_call(
        body,
        in_specs=[SMEM, SMEM, VMEM, VMEM, VMEM],
        out_specs=VMEM,
        out_shape=jax.ShapeDtypeStruct((blocks, 1, TOK, HD), jnp.bfloat16),
        compiler_params=LOCAL,
        cost_estimate=cost(1, blocks, 5),
    )(clips, role, arrived, gen, shared)


def slots_kernel(full, blocks, first, clips, where, arrived):
    def body(first_ref, clip_ref, where_ref, *refs):
        x_refs, o_refs, (x, y) = refs[:blocks], refs[blocks : 2 * blocks], refs[2 * blocks :]
        at = [where_ref[2] ^ d for d in range(blocks)]
        for d in range(blocks):
            x[at[d]] = x_refs[d][...]

        def head(s, carry):
            sources = [(x, 5 * s + t) for t in range(5)]
            student_head(range(0, blocks, 2), first_ref[0], sources[:3], y, 2 * s)
            gen = lambda at: y[at, 2 * s]
            teacher_whole_head(blocks, clip_ref, sources[3:], gen, y, 2 * s + 1)

        lax.fori_loop(0, full, head, None)
        for d in range(blocks):
            o_refs[d][...] = y[at[d]]

    return pl.pallas_call(
        body,
        in_specs=[SMEM] * 3 + [VMEM] * blocks,
        out_specs=[VMEM] * blocks,
        out_shape=[jax.ShapeDtypeStruct((2 * full, TOK, HD), jnp.bfloat16)] * blocks,
        scratch_shapes=[
            pltpu.VMEM((blocks, 5 * full, TOK, HD), jnp.bfloat16),
            pltpu.VMEM((blocks, 2 * full, TOK, HD), jnp.bfloat16),
        ],
        compiler_params=LOCAL,
        cost_estimate=cost(2 * full, blocks, 7 * full),
    )(first, clips, where, *arrived)


def slots_pack(full, peers, where, tensors):
    def body(where_ref, *refs):
        o_refs, (rows, sems) = refs[5 : 5 + peers], refs[5 + peers :]
        copies = []
        for t in range(5):
            source = refs[t].at[0, :, pl.ds(0, full * peers * HD)]
            copies.append(pltpu.make_async_copy(source, rows.at[t], sems.at[t]))
            copies[-1].start()
        for t in range(5):
            copies[t].wait()
            for s in range(full):
                for d in range(peers):
                    at = pl.multiple_of((s * peers + (where_ref[2] ^ d)) * HD, HD)
                    o_refs[d][5 * s + t] = rows[t, :, pl.ds(at, HD)]

    return pl.pallas_call(
        body,
        in_specs=[SMEM] + [pl.BlockSpec(memory_space=pl.ANY)] * 5,
        out_specs=[VMEM] * peers,
        out_shape=[jax.ShapeDtypeStruct((5 * full, TOK, HD), jnp.bfloat16)] * peers,
        scratch_shapes=[
            pltpu.VMEM((5, TOK, full * peers * HD), jnp.bfloat16),
            pltpu.SemaphoreType.DMA((5,)),
        ],
        compiler_params=WHOLE,
        cost_estimate=cost(0, peers, 10 * full),
    )(where, *tensors)


def rest_pack(base, columns, column, tensors):
    def body(column_ref, *refs):
        rows, sems = refs[-2:]
        copies = []
        for t in range(5):
            source = refs[t].at[0, :, pl.ds(base * HD, columns * HD)]
            copies.append(pltpu.make_async_copy(source, rows.at[t], sems.at[t]))
            copies[-1].start()
        for t in range(5):
            copies[t].wait()
            for s in range(columns):
                at = pl.multiple_of((column_ref[0] ^ s) * HD, HD)
                refs[5 + s][t] = rows[t, :, pl.ds(at, HD)]

    return pl.pallas_call(
        body,
        in_specs=[SMEM] + [pl.BlockSpec(memory_space=pl.ANY)] * 5,
        out_specs=[VMEM] * columns,
        out_shape=[jax.ShapeDtypeStruct((5, TOK, HD), jnp.bfloat16)] * columns,
        scratch_shapes=[
            pltpu.VMEM((5, TOK, columns * HD), jnp.bfloat16),
            pltpu.SemaphoreType.DMA((5,)),
        ],
        compiler_params=WHOLE,
        cost_estimate=cost(0, 1, 10 * columns),
    )(column, *tensors)


def rest_kernel(columns, first, clips, where, own, other):
    blocks = 2 * columns

    def body(first_ref, clip_ref, where_ref, *refs):
        x, gen = refs[-2:]
        column, side = where_ref[0], where_ref[1]
        mine = [2 * (column ^ s) + side for s in range(columns)]
        for s in range(columns):
            x[mine[s]] = refs[s][...]
            x[mine[s] ^ 1] = refs[columns + s][...]
        sources = [(x, t) for t in range(5)]
        student_head(range(0, blocks, 2), first_ref[0], sources[:3], gen, 0)
        at_gen = lambda at: gen[at, 0]
        for s in range(columns):
            o_ref = refs[2 * columns + s]
            o_ref[0:1] = gen[mine[s]]
            teacher_head(blocks, [mine[s]], clip_ref, sources[3:], at_gen, o_ref, None)

    return pl.pallas_call(
        body,
        in_specs=[SMEM] * 3 + [VMEM] * (2 * columns),
        out_specs=[VMEM] * columns,
        out_shape=[jax.ShapeDtypeStruct((2, TOK, HD), jnp.bfloat16)] * columns,
        scratch_shapes=[
            pltpu.VMEM((blocks, 5, TOK, HD), jnp.bfloat16),
            pltpu.VMEM((blocks, 1, TOK, HD), jnp.bfloat16),
        ],
        compiler_params=LOCAL,
        cost_estimate=cost(2, blocks, 7),
    )(first, clips, where, *own, *other)


def join(full, peers, columns, where, slots, rests):
    def body(where_ref, *refs):
        for i, o_ref in enumerate(refs[peers + columns :]):

            def put(h, tile):
                o_ref[0, :, pl.ds(pl.multiple_of(h * HD, HD), HD)] = tile

            for d in range(peers):
                for s in range(full):
                    put(s * peers + (where_ref[2] ^ d), refs[d][2 * s + i])
            for s in range(columns):
                put(full * peers + (where_ref[0] ^ s), refs[peers + s][i])

    width = (full * peers + columns) * HD
    return pl.pallas_call(
        body,
        in_specs=[SMEM] + [VMEM] * (peers + columns),
        out_specs=[VMEM] * 2,
        out_shape=[jax.ShapeDtypeStruct((1, TOK, width), jnp.bfloat16)] * 2,
        compiler_params=LOCAL,
        cost_estimate=cost(0, 1, 4 * width // HD),
    )(where, *slots, *rests)


def by_slots_and_columns(tensors, peers, full, rest, first, clips):
    here = lax.axis_index("tm")
    where = jnp.stack([here // 2, here % 2, here]).astype(jnp.int32)

    def swapped(x, by):
        return lax.ppermute(x, "tm", [(i, i ^ by) for i in range(peers)]) if by else x

    pieces = rest_pack(full * peers, rest, where[:1], tensors)
    own = [swapped(x, 2 * s) for s, x in enumerate(pieces)]
    packed = slots_pack(full, peers, where, tensors)
    packed, own = lax.optimization_barrier((packed, own))
    arrived = [swapped(x, d) for d, x in enumerate(packed)]
    other = [swapped(x, 1) for x in own]
    pieces = rest_kernel(rest, first, clips, where, own, other)
    arrived, pieces = lax.optimization_barrier((arrived, pieces))
    rests = [swapped(x, 2 * s) for s, x in enumerate(pieces)]
    results = slots_kernel(full, peers, first, clips, where, arrived)
    results, rests = lax.optimization_barrier((results, rests))
    slots = [swapped(x, d) for d, x in enumerate(results)]
    return tuple(join(full, peers, rest, where, slots, rests))


def by_roles(tensors, peers, heads, first, clips):
    here = lax.axis_index("tm")
    role = jnp.where(here < 2 * heads, 1 + here % 2, 0).astype(jnp.int32)[None]
    plan = [
        [(t, min(p // 2, heads - 1)) for t in ((3, 4, 4) if p % 2 else (0, 1, 2))]
        for p in range(peers)
    ]
    arrived = lax.all_to_all(pack(plan, [(0, heads)], tensors), "tm", 0, 0)
    gen = student_kernel(peers, first, role, arrived)
    shared = lax.ppermute(gen, "tm", [(2 * r, 2 * r + 1) for r in range(heads)])
    results = rest_teacher(peers, clips, role, arrived, 0, gen, shared)
    back = lax.all_to_all(results, "tm", 0, 0)
    return tuple(unpack([[(2 * r + i, 0) for r in range(heads)] for i in (0, 1)], back))


def per_device(student_q, student_k, student_v, teacher_q, teacher_k, stagger, clip_lengths):
    heads = student_q.shape[2] // HD
    peers = lax.axis_size("tm")
    full, rest = divmod(heads, peers)
    running = jnp.cumsum(clip_lengths[0])
    block = jnp.arange(peers, dtype=jnp.int32)
    before = running[None, :] <= block[:, None]
    low = jnp.max(jnp.where(before, running[None, :], 0), axis=1)
    high = jnp.min(jnp.where(before, peers, running[None, :]), axis=1)
    large = jnp.where(clip_lengths[0] == peers // 2 + 1, running - clip_lengths[0], 0)
    large = jnp.broadcast_to(jnp.max(large), (peers,))
    clips = jnp.stack([low, high, large]).astype(jnp.int32)
    tensors = (student_q, student_k, student_v, teacher_q, teacher_k)
    if full == 0:
        assert 2 * rest <= peers
        return by_roles(tensors, peers, rest, stagger, clips)
    assert peers == 2 * rest and rest & (rest - 1) == 0
    return by_slots_and_columns(tensors, peers, full, rest, stagger, clips)


def solution(mesh):
    spec = P("seq", "tm", "mp")
    return jax.shard_map(
        per_device,
        mesh=mesh,
        in_specs=(spec,) * 5 + (P("seq"), P("seq", None)),
        out_specs=(spec, spec),
        check_vma=False,
    )
```

```python
import functools
import math

import jax
import jax.numpy as jnp
from jax import lax
from jax.experimental import pallas as pl
from jax.experimental.pallas import tpu as pltpu
from jax.sharding import PartitionSpec as P

HD = 128
TOK = 128
NEG = -1e30
RATE = math.log2(math.e) / math.sqrt(HD)
MIB = 2**20
VMEM = pl.BlockSpec(memory_space=pltpu.VMEM)
SMEM = pl.BlockSpec(memory_space=pltpu.SMEM)
WHOLE = pltpu.CompilerParams(vmem_limit_bytes=60 * MIB)
LOCAL = pltpu.CompilerParams(vmem_limit_bytes=24 * MIB)


def attend(q, k, v, bias):
    g = q.shape[0]
    scores = lax.dot_general(
        q.reshape(g * TOK, HD), k, (((1,), (1,)), ((), ())), preferred_element_type=jnp.float32
    )
    scores = scores.reshape(g, TOK, -1)
    if bias is not None:
        scores = scores + bias
    top = jnp.max(scores, axis=-1, keepdims=True)
    weights = jnp.exp2((scores - top) * RATE)
    total = jnp.sum(weights, axis=-1, keepdims=True)
    weights = weights.astype(jnp.bfloat16).reshape(g * TOK, -1)
    mixed = jnp.dot(weights, v, preferred_element_type=jnp.float32)
    return mixed.reshape(g, TOK, HD) / total


def student_head(pairs, first, sources, o_ref, o_at):
    (q_ref, q_at), (k_ref, k_at), (v_ref, v_at) = sources
    for i in pairs:
        width = (i + 2) * TOK
        block = lax.broadcasted_iota(jnp.int32, (2, 1, width), 2) // TOK
        own = lax.broadcasted_iota(jnp.int32, (2, 1, width), 0) + i
        bias = jnp.where((block == own) | (block >= first) & (block < own), 0.0, NEG)
        k = k_ref[0 : i + 2, k_at].reshape(width, HD)
        v = v_ref[0 : i + 2, v_at].reshape(width, HD)
        o_ref[i : i + 2, o_at] = attend(q_ref[i : i + 2, q_at], k, v, bias).astype(jnp.bfloat16)


def teacher_head(blocks, rows, clip_ref, sources, gen, o_ref, o_at):
    (q_ref, q_at), (k_ref, k_at) = sources
    reach = blocks // 2 + 1
    width = reach * TOK
    offset = lax.broadcasted_iota(jnp.int32, (1, 1, width), 2) // TOK
    for i in rows:
        low = clip_ref[0, i]
        high = clip_ref[1, i]
        start = jnp.minimum(low, blocks - reach)
        block = offset + start
        bias = jnp.where((block >= low) & (block < high), 0.0, NEG)
        k = k_ref[pl.ds(start, reach), k_at].reshape(width, HD)
        v = gen(pl.ds(start, reach)).reshape(width, HD)
        out = attend(q_ref[pl.ds(i, 1), q_at], k, v, bias)
        score = (out[0] - gen(i).astype(jnp.float32)).astype(jnp.bfloat16)
        if o_at is None:
            o_ref[1] = score
        else:
            o_ref[i, o_at] = score


def teacher_whole_head(blocks, clip_ref, sources, gen, o_ref, o_at):
    (q_ref, q_at), (k_ref, k_at) = sources
    reach = blocks // 2 + 1

    def put(at, out):
        score = out - gen(at).astype(jnp.float32)
        o_ref[at, o_at] = score.astype(jnp.bfloat16)

    large = clip_ref[2, 0]
    k = k_ref[pl.ds(large, reach), k_at].reshape(reach * TOK, HD)
    v = gen(pl.ds(large, reach)).reshape(reach * TOK, HD)
    for i in range(0, reach, 2):
        at = pl.ds(large + i, min(2, reach - i))
        put(at, attend(q_ref[at, q_at], k, v, None))
    span = blocks - reach - 1
    offset = lax.broadcasted_iota(jnp.int32, (1, 1, span * TOK), 2) // TOK
    for j in range(blocks - reach):
        i = jnp.where(j < large, j, j + reach)
        low, high = clip_ref[0, i], clip_ref[1, i]
        start = jnp.minimum(low, blocks - span)
        block = offset + start
        bias = jnp.where((block >= low) & (block < high), 0.0, NEG)
        k = k_ref[pl.ds(start, span), k_at].reshape(span * TOK, HD)
        v = gen(pl.ds(start, span)).reshape(span * TOK, HD)
        put(pl.ds(i, 1), attend(q_ref[pl.ds(i, 1), q_at], k, v, bias))


def cost(heads, blocks, units):
    return pl.CostEstimate(
        flops=heads * blocks * blocks * 4 * TOK * TOK * HD,
        bytes_accessed=units * blocks * TOK * HD * 2,
        transcendentals=heads * blocks * blocks * TOK * TOK,
    )


def pack(plan, ranges, tensors):
    peers, units = len(plan), len(plan[0])
    widths = [count * HD for _, count in ranges]
    starts = [sum(widths[:r]) for r in range(len(ranges))]

    def place(h):
        for r, (head, count) in enumerate(ranges):
            if head <= h < head + count:
                return r, starts[r] + (h - head) * HD

    need = []
    for u in range(units):
        need.append(list(dict.fromkeys((plan[p][u][0], place(plan[p][u][1])[0]) for p in range(peers))))
    order = sorted(range(units), key=lambda u: (len(need[u]), u))
    fetch = list(dict.fromkeys(piece for u in order for piece in need[u]))

    def body(*refs):
        o_ref, rows, tiles, in_sem, out_sem = refs[len(tensors) :]
        copies = {}
        for n, (t, r) in enumerate(fetch):
            source = refs[t].at[0, :, pl.ds(ranges[r][0] * HD, widths[r])]
            target = rows.at[t, :, pl.ds(starts[r], widths[r])]
            copies[t, r] = pltpu.make_async_copy(source, target, in_sem.at[n])
            copies[t, r].start()
        sent = []
        for u in order:
            for piece in need[u]:
                if piece in copies:
                    copies.pop(piece).wait()
            for p in range(peers):
                t, h = plan[p][u]
                at = place(h)[1]
                tiles[p, u] = rows[t, :, at : at + HD]
            sent.append(pltpu.make_async_copy(tiles.at[:, u], o_ref.at[:, u], out_sem.at[u]))
            sent[-1].start()
        for copy in sent:
            copy.wait()

    return pl.pallas_call(
        body,
        in_specs=[pl.BlockSpec(memory_space=pl.ANY)] * len(tensors),
        out_specs=pl.BlockSpec(memory_space=pl.ANY),
        out_shape=jax.ShapeDtypeStruct((peers, units, TOK, HD), jnp.bfloat16),
        scratch_shapes=[
            pltpu.VMEM((len(tensors), TOK, sum(widths)), jnp.bfloat16),
            pltpu.VMEM((peers, units, TOK, HD), jnp.bfloat16),
            pltpu.SemaphoreType.DMA((len(fetch),)),
            pltpu.SemaphoreType.DMA((units,)),
        ],
        compiler_params=WHOLE,
        cost_estimate=cost(0, peers, 2 * units),
    )(*tensors)


def unpack(places, back):
    def body(x_ref, *o_refs):
        for o_ref, place in zip(o_refs, places):
            for h, (p, u) in enumerate(place):
                o_ref[0, :, h * HD : (h + 1) * HD] = x_ref[p, u]

    width = len(places[0]) * HD
    return pl.pallas_call(
        body,
        out_shape=[jax.ShapeDtypeStruct((1, TOK, width), jnp.bfloat16) for _ in places],
        compiler_params=LOCAL,
        cost_estimate=cost(0, 1, 4 * len(places[0])),
    )(back)


def student_kernel(blocks, first, role, arrived):
    def body(first_ref, role_ref, x_ref, o_ref):
        @pl.when(role_ref[0] == 1)
        def _():
            sources = [(x_ref, t) for t in range(3)]
            student_head(range(0, blocks, 2), first_ref[0], sources, o_ref, 0)

    return pl.pallas_call(
        body,
        in_specs=[SMEM, SMEM, VMEM],
        out_specs=VMEM,
        out_shape=jax.ShapeDtypeStruct((blocks, 1, TOK, HD), jnp.bfloat16),
        compiler_params=LOCAL,
        cost_estimate=cost(1, blocks, 4),
    )(first, role, arrived)


def rest_teacher(blocks, clips, role, arrived, offset, gen, shared):
    def body(clip_ref, role_ref, x_ref, gen_ref, shared_ref, o_ref):
        @pl.when(role_ref[0] == 1)
        def _():
            o_ref[...] = gen_ref[...]

        @pl.when(role_ref[0] == 2)
        def _():
            sources = [(x_ref, offset + t) for t in range(2)]
            teacher_head(
                blocks, range(blocks), clip_ref, sources, lambda at: shared_ref[at, 0], o_ref, 0
            )

    return pl.pallas_call(
        body,
        in_specs=[SMEM, SMEM, VMEM, VMEM, VMEM],
        out_specs=VMEM,
        out_shape=jax.ShapeDtypeStruct((blocks, 1, TOK, HD), jnp.bfloat16),
        compiler_params=LOCAL,
        cost_estimate=cost(1, blocks, 5),
    )(clips, role, arrived, gen, shared)


def slots_kernel(full, blocks, first, clips, where, arrived):
    def body(first_ref, clip_ref, where_ref, x, *refs):
        o_refs, y = refs[:blocks], refs[blocks]
        at = [where_ref[2] ^ d for d in range(blocks)]

        def head(s, carry):
            sources = [(x, 5 * s + t) for t in range(5)]
            student_head(range(0, blocks, 2), first_ref[0], sources[:3], y, 2 * s)
            gen = lambda at: y[at, 2 * s]
            teacher_whole_head(blocks, clip_ref, sources[3:], gen, y, 2 * s + 1)

        lax.fori_loop(0, full, head, None)
        for d in range(blocks):
            o_refs[d][...] = y[at[d]]

    return pl.pallas_call(
        body,
        in_specs=[SMEM] * 3 + [VMEM],
        out_specs=[VMEM] * blocks,
        out_shape=[jax.ShapeDtypeStruct((2 * full, TOK, HD), jnp.bfloat16)] * blocks,
        scratch_shapes=[pltpu.VMEM((blocks, 2 * full, TOK, HD), jnp.bfloat16)],
        compiler_params=LOCAL,
        cost_estimate=cost(2 * full, blocks, 7 * full),
    )(first, clips, where, arrived)


def rest_pack(base, columns, column, tensors):
    def body(column_ref, *refs):
        rows, sems = refs[-2:]
        copies = []
        for t in range(5):
            source = refs[t].at[0, :, pl.ds(base * HD, columns * HD)]
            copies.append(pltpu.make_async_copy(source, rows.at[t], sems.at[t]))
            copies[-1].start()
        for t in range(5):
            copies[t].wait()
            for s in range(columns):
                at = pl.multiple_of((column_ref[0] ^ s) * HD, HD)
                refs[5 + s][t] = rows[t, :, pl.ds(at, HD)]

    return pl.pallas_call(
        body,
        in_specs=[SMEM] + [pl.BlockSpec(memory_space=pl.ANY)] * 5,
        out_specs=[VMEM] * columns,
        out_shape=[jax.ShapeDtypeStruct((5, TOK, HD), jnp.bfloat16)] * columns,
        scratch_shapes=[
            pltpu.VMEM((5, TOK, columns * HD), jnp.bfloat16),
            pltpu.SemaphoreType.DMA((5,)),
        ],
        compiler_params=WHOLE,
        cost_estimate=cost(0, 1, 10 * columns),
    )(column, *tensors)


def rest_kernel(columns, first, clips, where, own, other):
    blocks = 2 * columns

    def body(first_ref, clip_ref, where_ref, *refs):
        x, gen = refs[-2:]
        column, side = where_ref[0], where_ref[1]
        mine = [2 * (column ^ s) + side for s in range(columns)]
        for s in range(columns):
            x[mine[s]] = refs[s][...]
            x[mine[s] ^ 1] = refs[columns + s][...]
        sources = [(x, t) for t in range(5)]
        student_head(range(0, blocks, 2), first_ref[0], sources[:3], gen, 0)
        at_gen = lambda at: gen[at, 0]
        for s in range(columns):
            o_ref = refs[2 * columns + s]
            o_ref[0:1] = gen[mine[s]]
            teacher_head(blocks, [mine[s]], clip_ref, sources[3:], at_gen, o_ref, None)

    return pl.pallas_call(
        body,
        in_specs=[SMEM] * 3 + [VMEM] * (2 * columns),
        out_specs=[VMEM] * columns,
        out_shape=[jax.ShapeDtypeStruct((2, TOK, HD), jnp.bfloat16)] * columns,
        scratch_shapes=[
            pltpu.VMEM((blocks, 5, TOK, HD), jnp.bfloat16),
            pltpu.VMEM((blocks, 1, TOK, HD), jnp.bfloat16),
        ],
        compiler_params=LOCAL,
        cost_estimate=cost(2, blocks, 7),
    )(first, clips, where, *own, *other)


def join(full, peers, columns, where, slots, rests):
    def body(where_ref, *refs):
        for i, o_ref in enumerate(refs[peers + columns :]):

            def put(h, tile):
                o_ref[0, :, pl.ds(pl.multiple_of(h * HD, HD), HD)] = tile

            for d in range(peers):
                for s in range(full):
                    put(s * peers + (where_ref[2] ^ d), refs[d][2 * s + i])
            for s in range(columns):
                put(full * peers + (where_ref[0] ^ s), refs[peers + s][i])

    width = (full * peers + columns) * HD
    return pl.pallas_call(
        body,
        in_specs=[SMEM] + [VMEM] * (peers + columns),
        out_specs=[VMEM] * 2,
        out_shape=[jax.ShapeDtypeStruct((1, TOK, width), jnp.bfloat16)] * 2,
        compiler_params=LOCAL,
        cost_estimate=cost(0, 1, 4 * width // HD),
    )(where, *slots, *rests)


def by_slots_and_columns(tensors, peers, full, rest, first, clips):
    here = lax.axis_index("tm")
    where = jnp.stack([here // 2, here % 2, here]).astype(jnp.int32)

    def swapped(x, by):
        return lax.ppermute(x, "tm", [(i, i ^ by) for i in range(peers)]) if by else x

    pieces = rest_pack(full * peers, rest, where[:1], tensors)
    own = [swapped(x, 2 * s) for s, x in enumerate(pieces)]
    plan = [[(t, s * peers + p) for s in range(full) for t in range(5)] for p in range(peers)]
    packed = pack(plan, [(s * peers, peers) for s in range(full)], tensors)
    packed, own = lax.optimization_barrier((packed, own))
    arrived = lax.all_to_all(packed, "tm", 0, 0)
    other = [swapped(x, 1) for x in own]
    pieces = rest_kernel(rest, first, clips, where, own, other)
    arrived, pieces = lax.optimization_barrier((arrived, pieces))
    rests = [swapped(x, 2 * s) for s, x in enumerate(pieces)]
    results = slots_kernel(full, peers, first, clips, where, arrived)
    results, rests = lax.optimization_barrier((results, rests))
    slots = [swapped(x, d) for d, x in enumerate(results)]
    return tuple(join(full, peers, rest, where, slots, rests))


def by_roles(tensors, peers, heads, first, clips):
    here = lax.axis_index("tm")
    role = jnp.where(here < 2 * heads, 1 + here % 2, 0).astype(jnp.int32)[None]
    plan = [
        [(t, min(p // 2, heads - 1)) for t in ((3, 4, 4) if p % 2 else (0, 1, 2))]
        for p in range(peers)
    ]
    arrived = lax.all_to_all(pack(plan, [(0, heads)], tensors), "tm", 0, 0)
    gen = student_kernel(peers, first, role, arrived)
    shared = lax.ppermute(gen, "tm", [(2 * r, 2 * r + 1) for r in range(heads)])
    results = rest_teacher(peers, clips, role, arrived, 0, gen, shared)
    back = lax.all_to_all(results, "tm", 0, 0)
    return tuple(unpack([[(2 * r + i, 0) for r in range(heads)] for i in (0, 1)], back))


def per_device(student_q, student_k, student_v, teacher_q, teacher_k, stagger, clip_lengths):
    heads = student_q.shape[2] // HD
    peers = lax.axis_size("tm")
    full, rest = divmod(heads, peers)
    running = jnp.cumsum(clip_lengths[0])
    block = jnp.arange(peers, dtype=jnp.int32)
    before = running[None, :] <= block[:, None]
    low = jnp.max(jnp.where(before, running[None, :], 0), axis=1)
    high = jnp.min(jnp.where(before, peers, running[None, :]), axis=1)
    large = jnp.where(clip_lengths[0] == peers // 2 + 1, running - clip_lengths[0], 0)
    large = jnp.broadcast_to(jnp.max(large), (peers,))
    clips = jnp.stack([low, high, large]).astype(jnp.int32)
    tensors = (student_q, student_k, student_v, teacher_q, teacher_k)
    if full == 0:
        assert 2 * rest <= peers
        return by_roles(tensors, peers, rest, stagger, clips)
    assert peers == 2 * rest and rest & (rest - 1) == 0
    return by_slots_and_columns(tensors, peers, full, rest, stagger, clips)


def solution(mesh):
    spec = P("seq", "tm", "mp")
    return jax.shard_map(
        per_device,
        mesh=mesh,
        in_specs=(spec,) * 5 + (P("seq"), P("seq", None)),
        out_specs=(spec, spec),
        check_vma=False,
    )
```

```python
import functools
import math

import jax
import jax.numpy as jnp
from jax import lax
from jax.experimental import pallas as pl
from jax.experimental.pallas import tpu as pltpu
from jax.sharding import PartitionSpec as P

HD = 128
TOK = 128
NEG = -1e30
RATE = math.log2(math.e) / math.sqrt(HD)
MIB = 2**20
VMEM = pl.BlockSpec(memory_space=pltpu.VMEM)
SMEM = pl.BlockSpec(memory_space=pltpu.SMEM)
WHOLE = pltpu.CompilerParams(vmem_limit_bytes=60 * MIB)
LOCAL = pltpu.CompilerParams(vmem_limit_bytes=24 * MIB)


def attend(q, k, v, bias):
    g = q.shape[0]
    scores = lax.dot_general(
        q.reshape(g * TOK, HD), k, (((1,), (1,)), ((), ())), preferred_element_type=jnp.float32
    )
    scores = scores.reshape(g, TOK, -1)
    if bias is not None:
        scores = scores + bias
    top = jnp.max(scores, axis=-1, keepdims=True)
    weights = jnp.exp2((scores - top) * RATE)
    total = jnp.sum(weights, axis=-1, keepdims=True)
    weights = weights.astype(jnp.bfloat16).reshape(g * TOK, -1)
    mixed = jnp.dot(weights, v, preferred_element_type=jnp.float32)
    return mixed.reshape(g, TOK, HD) / total


def student_head(pairs, first, sources, o_ref, o_at):
    (q_ref, q_at), (k_ref, k_at), (v_ref, v_at) = sources
    for i in pairs:
        width = (i + 2) * TOK
        block = lax.broadcasted_iota(jnp.int32, (2, 1, width), 2) // TOK
        own = lax.broadcasted_iota(jnp.int32, (2, 1, width), 0) + i
        bias = jnp.where((block == own) | (block >= first) & (block < own), 0.0, NEG)
        k = k_ref[0 : i + 2, k_at].reshape(width, HD)
        v = v_ref[0 : i + 2, v_at].reshape(width, HD)
        o_ref[i : i + 2, o_at] = attend(q_ref[i : i + 2, q_at], k, v, bias).astype(jnp.bfloat16)


def teacher_head(blocks, rows, clip_ref, sources, gen, o_ref, o_at):
    (q_ref, q_at), (k_ref, k_at) = sources
    reach = blocks // 2 + 1
    width = reach * TOK
    offset = lax.broadcasted_iota(jnp.int32, (1, 1, width), 2) // TOK
    for i in rows:
        low = clip_ref[0, i]
        high = clip_ref[1, i]
        start = jnp.minimum(low, blocks - reach)
        block = offset + start
        bias = jnp.where((block >= low) & (block < high), 0.0, NEG)
        k = k_ref[pl.ds(start, reach), k_at].reshape(width, HD)
        v = gen(pl.ds(start, reach)).reshape(width, HD)
        out = attend(q_ref[pl.ds(i, 1), q_at], k, v, bias)
        score = (out[0] - gen(i).astype(jnp.float32)).astype(jnp.bfloat16)
        if o_at is None:
            o_ref[1] = score
        else:
            o_ref[i, o_at] = score


def teacher_whole_head(blocks, clip_ref, sources, gen, o_ref, o_at):
    (q_ref, q_at), (k_ref, k_at) = sources
    reach = blocks // 2 + 1

    def put(at, out):
        score = out - gen(at).astype(jnp.float32)
        o_ref[at, o_at] = score.astype(jnp.bfloat16)

    large = clip_ref[2, 0]
    k = k_ref[pl.ds(large, reach), k_at].reshape(reach * TOK, HD)
    v = gen(pl.ds(large, reach)).reshape(reach * TOK, HD)
    for i in range(0, reach, 2):
        at = pl.ds(large + i, min(2, reach - i))
        put(at, attend(q_ref[at, q_at], k, v, None))
    span = blocks - reach - 1
    offset = lax.broadcasted_iota(jnp.int32, (1, 1, span * TOK), 2) // TOK
    for j in range(blocks - reach):
        i = jnp.where(j < large, j, j + reach)
        low, high = clip_ref[0, i], clip_ref[1, i]
        start = jnp.minimum(low, blocks - span)
        block = offset + start
        bias = jnp.where((block >= low) & (block < high), 0.0, NEG)
        k = k_ref[pl.ds(start, span), k_at].reshape(span * TOK, HD)
        v = gen(pl.ds(start, span)).reshape(span * TOK, HD)
        put(pl.ds(i, 1), attend(q_ref[pl.ds(i, 1), q_at], k, v, bias))


def cost(heads, blocks, units):
    return pl.CostEstimate(
        flops=heads * blocks * blocks * 4 * TOK * TOK * HD,
        bytes_accessed=units * blocks * TOK * HD * 2,
        transcendentals=heads * blocks * blocks * TOK * TOK,
    )


def pack(plan, ranges, tensors):
    peers, units = len(plan), len(plan[0])
    widths = [count * HD for _, count in ranges]
    starts = [sum(widths[:r]) for r in range(len(ranges))]

    def place(h):
        for r, (head, count) in enumerate(ranges):
            if head <= h < head + count:
                return r, starts[r] + (h - head) * HD

    need = []
    for u in range(units):
        need.append(list(dict.fromkeys((plan[p][u][0], place(plan[p][u][1])[0]) for p in range(peers))))
    order = sorted(range(units), key=lambda u: (len(need[u]), u))
    fetch = list(dict.fromkeys(piece for u in order for piece in need[u]))

    def body(*refs):
        o_ref, rows, tiles, in_sem, out_sem = refs[len(tensors) :]
        copies = {}
        for n, (t, r) in enumerate(fetch):
            source = refs[t].at[0, :, pl.ds(ranges[r][0] * HD, widths[r])]
            target = rows.at[t, :, pl.ds(starts[r], widths[r])]
            copies[t, r] = pltpu.make_async_copy(source, target, in_sem.at[n])
            copies[t, r].start()
        sent = []
        for u in order:
            for piece in need[u]:
                if piece in copies:
                    copies.pop(piece).wait()
            for p in range(peers):
                t, h = plan[p][u]
                at = place(h)[1]
                tiles[p, u] = rows[t, :, at : at + HD]
            sent.append(pltpu.make_async_copy(tiles.at[:, u], o_ref.at[:, u], out_sem.at[u]))
            sent[-1].start()
        for copy in sent:
            copy.wait()

    return pl.pallas_call(
        body,
        in_specs=[pl.BlockSpec(memory_space=pl.ANY)] * len(tensors),
        out_specs=pl.BlockSpec(memory_space=pl.ANY),
        out_shape=jax.ShapeDtypeStruct((peers, units, TOK, HD), jnp.bfloat16),
        scratch_shapes=[
            pltpu.VMEM((len(tensors), TOK, sum(widths)), jnp.bfloat16),
            pltpu.VMEM((peers, units, TOK, HD), jnp.bfloat16),
            pltpu.SemaphoreType.DMA((len(fetch),)),
            pltpu.SemaphoreType.DMA((units,)),
        ],
        compiler_params=WHOLE,
        cost_estimate=cost(0, peers, 2 * units),
    )(*tensors)


def unpack(places, back):
    def body(x_ref, *o_refs):
        for o_ref, place in zip(o_refs, places):
            for h, (p, u) in enumerate(place):
                o_ref[0, :, h * HD : (h + 1) * HD] = x_ref[p, u]

    width = len(places[0]) * HD
    return pl.pallas_call(
        body,
        out_shape=[jax.ShapeDtypeStruct((1, TOK, width), jnp.bfloat16) for _ in places],
        compiler_params=LOCAL,
        cost_estimate=cost(0, 1, 4 * len(places[0])),
    )(back)


def student_kernel(blocks, first, role, arrived):
    def body(first_ref, role_ref, x_ref, o_ref):
        @pl.when(role_ref[0] == 1)
        def _():
            sources = [(x_ref, t) for t in range(3)]
            student_head(range(0, blocks, 2), first_ref[0], sources, o_ref, 0)

    return pl.pallas_call(
        body,
        in_specs=[SMEM, SMEM, VMEM],
        out_specs=VMEM,
        out_shape=jax.ShapeDtypeStruct((blocks, 1, TOK, HD), jnp.bfloat16),
        compiler_params=LOCAL,
        cost_estimate=cost(1, blocks, 4),
    )(first, role, arrived)


def rest_teacher(blocks, clips, role, arrived, offset, gen, shared):
    def body(clip_ref, role_ref, x_ref, gen_ref, shared_ref, o_ref):
        @pl.when(role_ref[0] == 1)
        def _():
            o_ref[...] = gen_ref[...]

        @pl.when(role_ref[0] == 2)
        def _():
            sources = [(x_ref, offset + t) for t in range(2)]
            teacher_head(
                blocks, range(blocks), clip_ref, sources, lambda at: shared_ref[at, 0], o_ref, 0
            )

    return pl.pallas_call(
        body,
        in_specs=[SMEM, SMEM, VMEM, VMEM, VMEM],
        out_specs=VMEM,
        out_shape=jax.ShapeDtypeStruct((blocks, 1, TOK, HD), jnp.bfloat16),
        compiler_params=LOCAL,
        cost_estimate=cost(1, blocks, 5),
    )(clips, role, arrived, gen, shared)


def slots_kernel(full, blocks, first, clips, where, arrived):
    def body(first_ref, clip_ref, where_ref, *refs):
        x_refs, o_refs, (x, y) = refs[:blocks], refs[blocks : 2 * blocks], refs[2 * blocks :]
        at = [where_ref[2] ^ d for d in range(blocks)]
        for d in range(blocks):
            x[at[d]] = x_refs[d][...]

        def head(s, carry):
            sources = [(x, 5 * s + t) for t in range(5)]
            student_head(range(0, blocks, 2), first_ref[0], sources[:3], y, 2 * s)
            gen = lambda at: y[at, 2 * s]
            teacher_whole_head(blocks, clip_ref, sources[3:], gen, y, 2 * s + 1)

        lax.fori_loop(0, full, head, None)
        for d in range(blocks):
            o_refs[d][...] = y[at[d]]

    return pl.pallas_call(
        body,
        in_specs=[SMEM] * 3 + [VMEM] * blocks,
        out_specs=[VMEM] * blocks,
        out_shape=[jax.ShapeDtypeStruct((2 * full, TOK, HD), jnp.bfloat16)] * blocks,
        scratch_shapes=[
            pltpu.VMEM((blocks, 5 * full, TOK, HD), jnp.bfloat16),
            pltpu.VMEM((blocks, 2 * full, TOK, HD), jnp.bfloat16),
        ],
        compiler_params=LOCAL,
        cost_estimate=cost(2 * full, blocks, 7 * full),
    )(first, clips, where, *arrived)


def slots_pack(full, peers, where, tensors):
    def body(where_ref, *refs):
        o_refs, (rows, sems) = refs[5 : 5 + peers], refs[5 + peers :]
        copies = []
        for t in range(5):
            source = refs[t].at[0, :, pl.ds(0, full * peers * HD)]
            copies.append(pltpu.make_async_copy(source, rows.at[t], sems.at[t]))
            copies[-1].start()
        for t in range(5):
            copies[t].wait()
            for s in range(full):
                for d in range(peers):
                    at = pl.multiple_of((s * peers + (where_ref[2] ^ d)) * HD, HD)
                    o_refs[d][5 * s + t] = rows[t, :, pl.ds(at, HD)]

    return pl.pallas_call(
        body,
        in_specs=[SMEM] + [pl.BlockSpec(memory_space=pl.ANY)] * 5,
        out_specs=[VMEM] * peers,
        out_shape=[jax.ShapeDtypeStruct((5 * full, TOK, HD), jnp.bfloat16)] * peers,
        scratch_shapes=[
            pltpu.VMEM((5, TOK, full * peers * HD), jnp.bfloat16),
            pltpu.SemaphoreType.DMA((5,)),
        ],
        compiler_params=WHOLE,
        cost_estimate=cost(0, peers, 10 * full),
    )(where, *tensors)


def rest_pack(base, columns, column, tensors):
    def body(column_ref, *refs):
        rows, sems = refs[-2:]
        copies = []
        for t in range(5):
            source = refs[t].at[0, :, pl.ds(base * HD, columns * HD)]
            copies.append(pltpu.make_async_copy(source, rows.at[t], sems.at[t]))
            copies[-1].start()
        for t in range(5):
            copies[t].wait()
            for s in range(columns):
                at = pl.multiple_of((column_ref[0] ^ s) * HD, HD)
                refs[5 + s][t] = rows[t, :, pl.ds(at, HD)]

    return pl.pallas_call(
        body,
        in_specs=[SMEM] + [pl.BlockSpec(memory_space=pl.ANY)] * 5,
        out_specs=[VMEM] * columns,
        out_shape=[jax.ShapeDtypeStruct((5, TOK, HD), jnp.bfloat16)] * columns,
        scratch_shapes=[
            pltpu.VMEM((5, TOK, columns * HD), jnp.bfloat16),
            pltpu.SemaphoreType.DMA((5,)),
        ],
        compiler_params=WHOLE,
        cost_estimate=cost(0, 1, 10 * columns),
    )(column, *tensors)


def rest_kernel(columns, first, clips, where, own, other):
    blocks = 2 * columns

    def body(first_ref, clip_ref, where_ref, *refs):
        x, gen = refs[-2:]
        column, side = where_ref[0], where_ref[1]
        mine = [2 * (column ^ s) + side for s in range(columns)]
        for s in range(columns):
            x[mine[s]] = refs[s][...]
            x[mine[s] ^ 1] = refs[columns + s][...]
        sources = [(x, t) for t in range(5)]
        student_head(range(0, blocks, 2), first_ref[0], sources[:3], gen, 0)
        at_gen = lambda at: gen[at, 0]
        for s in range(columns):
            o_ref = refs[2 * columns + s]
            o_ref[0:1] = gen[mine[s]]
            teacher_head(blocks, [mine[s]], clip_ref, sources[3:], at_gen, o_ref, None)

    return pl.pallas_call(
        body,
        in_specs=[SMEM] * 3 + [VMEM] * (2 * columns),
        out_specs=[VMEM] * columns,
        out_shape=[jax.ShapeDtypeStruct((2, TOK, HD), jnp.bfloat16)] * columns,
        scratch_shapes=[
            pltpu.VMEM((blocks, 5, TOK, HD), jnp.bfloat16),
            pltpu.VMEM((blocks, 1, TOK, HD), jnp.bfloat16),
        ],
        compiler_params=LOCAL,
        cost_estimate=cost(0, 1, 1),
    )(first, clips, where, *own, *other)


def join(full, peers, columns, where, slots, rests):
    def body(where_ref, *refs):
        for i, o_ref in enumerate(refs[peers + columns :]):

            def put(h, tile):
                o_ref[0, :, pl.ds(pl.multiple_of(h * HD, HD), HD)] = tile

            for d in range(peers):
                for s in range(full):
                    put(s * peers + (where_ref[2] ^ d), refs[d][2 * s + i])
            for s in range(columns):
                put(full * peers + (where_ref[0] ^ s), refs[peers + s][i])

    width = (full * peers + columns) * HD
    return pl.pallas_call(
        body,
        in_specs=[SMEM] + [VMEM] * (peers + columns),
        out_specs=[VMEM] * 2,
        out_shape=[jax.ShapeDtypeStruct((1, TOK, width), jnp.bfloat16)] * 2,
        compiler_params=LOCAL,
        cost_estimate=cost(0, 1, 4 * width // HD),
    )(where, *slots, *rests)


def by_slots_and_columns(tensors, peers, full, rest, first, clips):
    here = lax.axis_index("tm")
    where = jnp.stack([here // 2, here % 2, here]).astype(jnp.int32)

    def swapped(x, by):
        return lax.ppermute(x, "tm", [(i, i ^ by) for i in range(peers)]) if by else x

    order = sorted(range(peers), key=lambda d: (-(d // rest), d % 2, d))

    def all_swapped(xs):
        done = {d: swapped(xs[d], d) for d in order}
        return [done[d] for d in range(peers)]

    pieces = rest_pack(full * peers, rest, where[:1], tensors)
    own = [swapped(x, 2 * s) for s, x in enumerate(pieces)]
    packed = slots_pack(full, peers, where, tensors)
    packed, own = lax.optimization_barrier((packed, own))
    arrived = all_swapped(packed)
    other = [swapped(x, 1) for x in own]
    pieces = rest_kernel(rest, first, clips, where, own, other)
    arrived, pieces = lax.optimization_barrier((arrived, pieces))
    rests = [swapped(x, 2 * s) for s, x in enumerate(pieces)]
    results = slots_kernel(full, peers, first, clips, where, arrived)
    results, rests = lax.optimization_barrier((results, rests))
    slots = all_swapped(results)
    return tuple(join(full, peers, rest, where, slots, rests))


def by_roles(tensors, peers, heads, first, clips):
    here = lax.axis_index("tm")
    role = jnp.where(here < 2 * heads, 1 + here % 2, 0).astype(jnp.int32)[None]
    plan = [
        [(t, min(p // 2, heads - 1)) for t in ((3, 4, 4) if p % 2 else (0, 1, 2))]
        for p in range(peers)
    ]
    arrived = lax.all_to_all(pack(plan, [(0, heads)], tensors), "tm", 0, 0)
    gen = student_kernel(peers, first, role, arrived)
    shared = lax.ppermute(gen, "tm", [(2 * r, 2 * r + 1) for r in range(heads)])
    results = rest_teacher(peers, clips, role, arrived, 0, gen, shared)
    back = lax.all_to_all(results, "tm", 0, 0)
    return tuple(unpack([[(2 * r + i, 0) for r in range(heads)] for i in (0, 1)], back))


def per_device(student_q, student_k, student_v, teacher_q, teacher_k, stagger, clip_lengths):
    heads = student_q.shape[2] // HD
    peers = lax.axis_size("tm")
    full, rest = divmod(heads, peers)
    running = jnp.cumsum(clip_lengths[0])
    block = jnp.arange(peers, dtype=jnp.int32)
    before = running[None, :] <= block[:, None]
    low = jnp.max(jnp.where(before, running[None, :], 0), axis=1)
    high = jnp.min(jnp.where(before, peers, running[None, :]), axis=1)
    large = jnp.where(clip_lengths[0] == peers // 2 + 1, running - clip_lengths[0], 0)
    large = jnp.broadcast_to(jnp.max(large), (peers,))
    clips = jnp.stack([low, high, large]).astype(jnp.int32)
    tensors = (student_q, student_k, student_v, teacher_q, teacher_k)
    if full == 0:
        assert 2 * rest <= peers
        return by_roles(tensors, peers, rest, stagger, clips)
    assert peers == 2 * rest and rest & (rest - 1) == 0
    return by_slots_and_columns(tensors, peers, full, rest, stagger, clips)


def solution(mesh):
    spec = P("seq", "tm", "mp")
    return jax.shard_map(
        per_device,
        mesh=mesh,
        in_specs=(spec,) * 5 + (P("seq"), P("seq", None)),
        out_specs=(spec, spec),
        check_vma=False,
    )
```

```python
import functools
import math

import jax
import jax.numpy as jnp
from jax import lax
from jax.experimental import pallas as pl
from jax.experimental.pallas import tpu as pltpu
from jax.sharding import PartitionSpec as P

HD = 128
TOK = 128
NEG = -1e30
RATE = math.log2(math.e) / math.sqrt(HD)
MIB = 2**20
VMEM = pl.BlockSpec(memory_space=pltpu.VMEM)
SMEM = pl.BlockSpec(memory_space=pltpu.SMEM)
WHOLE = pltpu.CompilerParams(vmem_limit_bytes=60 * MIB)
LOCAL = pltpu.CompilerParams(vmem_limit_bytes=24 * MIB)


def attend(q, k, v, bias):
    g = q.shape[0]
    scores = lax.dot_general(
        q.reshape(g * TOK, HD), k, (((1,), (1,)), ((), ())), preferred_element_type=jnp.float32
    )
    scores = scores.reshape(g, TOK, -1)
    if bias is not None:
        scores = scores + bias
    top = jnp.max(scores, axis=-1, keepdims=True)
    weights = jnp.exp2((scores - top) * RATE)
    total = jnp.sum(weights, axis=-1, keepdims=True)
    weights = weights.astype(jnp.bfloat16).reshape(g * TOK, -1)
    mixed = jnp.dot(weights, v, preferred_element_type=jnp.float32)
    return mixed.reshape(g, TOK, HD) / total


def student_head(pairs, first, sources, o_ref, o_at):
    (q_ref, q_at), (k_ref, k_at), (v_ref, v_at) = sources
    for i in pairs:
        width = (i + 2) * TOK
        block = lax.broadcasted_iota(jnp.int32, (2, 1, width), 2) // TOK
        own = lax.broadcasted_iota(jnp.int32, (2, 1, width), 0) + i
        bias = jnp.where((block == own) | (block >= first) & (block < own), 0.0, NEG)
        k = k_ref[0 : i + 2, k_at].reshape(width, HD)
        v = v_ref[0 : i + 2, v_at].reshape(width, HD)
        o_ref[i : i + 2, o_at] = attend(q_ref[i : i + 2, q_at], k, v, bias).astype(jnp.bfloat16)


def teacher_head(blocks, rows, clip_ref, sources, gen, o_ref, o_at):
    (q_ref, q_at), (k_ref, k_at) = sources
    reach = blocks // 2 + 1
    width = reach * TOK
    offset = lax.broadcasted_iota(jnp.int32, (1, 1, width), 2) // TOK
    for i in rows:
        low = clip_ref[0, i]
        high = clip_ref[1, i]
        start = jnp.minimum(low, blocks - reach)
        block = offset + start
        bias = jnp.where((block >= low) & (block < high), 0.0, NEG)
        k = k_ref[pl.ds(start, reach), k_at].reshape(width, HD)
        v = gen(pl.ds(start, reach)).reshape(width, HD)
        out = attend(q_ref[pl.ds(i, 1), q_at], k, v, bias)
        score = (out[0] - gen(i).astype(jnp.float32)).astype(jnp.bfloat16)
        if o_at is None:
            o_ref[1] = score
        else:
            o_ref[i, o_at] = score


def teacher_whole_head(blocks, clip_ref, sources, gen, o_ref, o_at):
    (q_ref, q_at), (k_ref, k_at) = sources
    reach = blocks // 2 + 1

    def put(at, out):
        score = out - gen(at).astype(jnp.float32)
        o_ref[at, o_at] = score.astype(jnp.bfloat16)

    large = clip_ref[2, 0]
    k = k_ref[pl.ds(large, reach), k_at].reshape(reach * TOK, HD)
    v = gen(pl.ds(large, reach)).reshape(reach * TOK, HD)
    for i in range(0, reach, 2):
        at = pl.ds(large + i, min(2, reach - i))
        put(at, attend(q_ref[at, q_at], k, v, None))
    span = blocks - reach - 1
    offset = lax.broadcasted_iota(jnp.int32, (1, 1, span * TOK), 2) // TOK
    for j in range(blocks - reach):
        i = jnp.where(j < large, j, j + reach)
        low, high = clip_ref[0, i], clip_ref[1, i]
        start = jnp.minimum(low, blocks - span)
        block = offset + start
        bias = jnp.where((block >= low) & (block < high), 0.0, NEG)
        k = k_ref[pl.ds(start, span), k_at].reshape(span * TOK, HD)
        v = gen(pl.ds(start, span)).reshape(span * TOK, HD)
        put(pl.ds(i, 1), attend(q_ref[pl.ds(i, 1), q_at], k, v, bias))


def cost(heads, blocks, units):
    return pl.CostEstimate(
        flops=heads * blocks * blocks * 4 * TOK * TOK * HD,
        bytes_accessed=units * blocks * TOK * HD * 2,
        transcendentals=heads * blocks * blocks * TOK * TOK,
    )


def pack(plan, ranges, tensors):
    peers, units = len(plan), len(plan[0])
    widths = [count * HD for _, count in ranges]
    starts = [sum(widths[:r]) for r in range(len(ranges))]

    def place(h):
        for r, (head, count) in enumerate(ranges):
            if head <= h < head + count:
                return r, starts[r] + (h - head) * HD

    need = []
    for u in range(units):
        need.append(list(dict.fromkeys((plan[p][u][0], place(plan[p][u][1])[0]) for p in range(peers))))
    order = sorted(range(units), key=lambda u: (len(need[u]), u))
    fetch = list(dict.fromkeys(piece for u in order for piece in need[u]))

    def body(*refs):
        o_ref, rows, tiles, in_sem, out_sem = refs[len(tensors) :]
        copies = {}
        for n, (t, r) in enumerate(fetch):
            source = refs[t].at[0, :, pl.ds(ranges[r][0] * HD, widths[r])]
            target = rows.at[t, :, pl.ds(starts[r], widths[r])]
            copies[t, r] = pltpu.make_async_copy(source, target, in_sem.at[n])
            copies[t, r].start()
        sent = []
        for u in order:
            for piece in need[u]:
                if piece in copies:
                    copies.pop(piece).wait()
            for p in range(peers):
                t, h = plan[p][u]
                at = place(h)[1]
                tiles[p, u] = rows[t, :, at : at + HD]
            sent.append(pltpu.make_async_copy(tiles.at[:, u], o_ref.at[:, u], out_sem.at[u]))
            sent[-1].start()
        for copy in sent:
            copy.wait()

    return pl.pallas_call(
        body,
        in_specs=[pl.BlockSpec(memory_space=pl.ANY)] * len(tensors),
        out_specs=pl.BlockSpec(memory_space=pl.ANY),
        out_shape=jax.ShapeDtypeStruct((peers, units, TOK, HD), jnp.bfloat16),
        scratch_shapes=[
            pltpu.VMEM((len(tensors), TOK, sum(widths)), jnp.bfloat16),
            pltpu.VMEM((peers, units, TOK, HD), jnp.bfloat16),
            pltpu.SemaphoreType.DMA((len(fetch),)),
            pltpu.SemaphoreType.DMA((units,)),
        ],
        compiler_params=WHOLE,
        cost_estimate=cost(0, peers, 2 * units),
    )(*tensors)


def unpack(places, back):
    def body(x_ref, *o_refs):
        for o_ref, place in zip(o_refs, places):
            for h, (p, u) in enumerate(place):
                o_ref[0, :, h * HD : (h + 1) * HD] = x_ref[p, u]

    width = len(places[0]) * HD
    return pl.pallas_call(
        body,
        out_shape=[jax.ShapeDtypeStruct((1, TOK, width), jnp.bfloat16) for _ in places],
        compiler_params=LOCAL,
        cost_estimate=cost(0, 1, 4 * len(places[0])),
    )(back)


def student_kernel(blocks, first, role, arrived):
    def body(first_ref, role_ref, x_ref, o_ref):
        @pl.when(role_ref[0] == 1)
        def _():
            sources = [(x_ref, t) for t in range(3)]
            student_head(range(0, blocks, 2), first_ref[0], sources, o_ref, 0)

    return pl.pallas_call(
        body,
        in_specs=[SMEM, SMEM, VMEM],
        out_specs=VMEM,
        out_shape=jax.ShapeDtypeStruct((blocks, 1, TOK, HD), jnp.bfloat16),
        compiler_params=LOCAL,
        cost_estimate=cost(1, blocks, 4),
    )(first, role, arrived)


def rest_teacher(blocks, clips, role, arrived, offset, gen, shared):
    def body(clip_ref, role_ref, x_ref, gen_ref, shared_ref, o_ref):
        @pl.when(role_ref[0] == 1)
        def _():
            o_ref[...] = gen_ref[...]

        @pl.when(role_ref[0] == 2)
        def _():
            sources = [(x_ref, offset + t) for t in range(2)]
            teacher_head(
                blocks, range(blocks), clip_ref, sources, lambda at: shared_ref[at, 0], o_ref, 0
            )

    return pl.pallas_call(
        body,
        in_specs=[SMEM, SMEM, VMEM, VMEM, VMEM],
        out_specs=VMEM,
        out_shape=jax.ShapeDtypeStruct((blocks, 1, TOK, HD), jnp.bfloat16),
        compiler_params=LOCAL,
        cost_estimate=cost(1, blocks, 5),
    )(clips, role, arrived, gen, shared)


def slots_kernel(full, order, first, clips, where, arrived):
    blocks = len(order)

    def body(first_ref, clip_ref, where_ref, *refs):
        x_refs, o_refs, (x, y) = refs[:blocks], refs[blocks : 2 * blocks], refs[2 * blocks :]
        at = [where_ref[2] ^ d for d in order]
        for i in range(blocks):
            x[at[i]] = x_refs[i][...]

        def head(s, carry):
            sources = [(x, 5 * s + t) for t in range(5)]
            student_head(range(0, blocks, 2), first_ref[0], sources[:3], y, 2 * s)
            gen = lambda at: y[at, 2 * s]
            teacher_whole_head(blocks, clip_ref, sources[3:], gen, y, 2 * s + 1)

        lax.fori_loop(0, full, head, None)
        for i in range(blocks):
            o_refs[i][...] = y[at[i]]

    return pl.pallas_call(
        body,
        in_specs=[SMEM] * 3 + [VMEM] * blocks,
        out_specs=[VMEM] * blocks,
        out_shape=[jax.ShapeDtypeStruct((2 * full, TOK, HD), jnp.bfloat16)] * blocks,
        scratch_shapes=[
            pltpu.VMEM((blocks, 5 * full, TOK, HD), jnp.bfloat16),
            pltpu.VMEM((blocks, 2 * full, TOK, HD), jnp.bfloat16),
        ],
        compiler_params=LOCAL,
        cost_estimate=cost(2 * full, blocks, 7 * full),
    )(first, clips, where, *arrived)


def slots_pack(full, order, where, tensors):
    peers = len(order)

    def body(where_ref, *refs):
        o_refs, (rows, sems) = refs[5 : 5 + peers], refs[5 + peers :]
        copies = []
        for t in range(5):
            source = refs[t].at[0, :, pl.ds(0, full * peers * HD)]
            copies.append(pltpu.make_async_copy(source, rows.at[t], sems.at[t]))
            copies[-1].start()
        for t in range(5):
            copies[t].wait()
            for s in range(full):
                for i, d in enumerate(order):
                    at = pl.multiple_of((s * peers + (where_ref[2] ^ d)) * HD, HD)
                    o_refs[i][5 * s + t] = rows[t, :, pl.ds(at, HD)]

    return pl.pallas_call(
        body,
        in_specs=[SMEM] + [pl.BlockSpec(memory_space=pl.ANY)] * 5,
        out_specs=[VMEM] * peers,
        out_shape=[jax.ShapeDtypeStruct((5 * full, TOK, HD), jnp.bfloat16)] * peers,
        scratch_shapes=[
            pltpu.VMEM((5, TOK, full * peers * HD), jnp.bfloat16),
            pltpu.SemaphoreType.DMA((5,)),
        ],
        compiler_params=WHOLE,
        cost_estimate=cost(0, peers, 10 * full),
    )(where, *tensors)


def rest_pack(base, columns, column, tensors):
    def body(column_ref, *refs):
        rows, sems = refs[-2:]
        copies = []
        for t in range(5):
            source = refs[t].at[0, :, pl.ds(base * HD, columns * HD)]
            copies.append(pltpu.make_async_copy(source, rows.at[t], sems.at[t]))
            copies[-1].start()
        for t in range(5):
            copies[t].wait()
            for s in range(columns):
                at = pl.multiple_of((column_ref[0] ^ s) * HD, HD)
                refs[5 + s][t] = rows[t, :, pl.ds(at, HD)]

    return pl.pallas_call(
        body,
        in_specs=[SMEM] + [pl.BlockSpec(memory_space=pl.ANY)] * 5,
        out_specs=[VMEM] * columns,
        out_shape=[jax.ShapeDtypeStruct((5, TOK, HD), jnp.bfloat16)] * columns,
        scratch_shapes=[
            pltpu.VMEM((5, TOK, columns * HD), jnp.bfloat16),
            pltpu.SemaphoreType.DMA((5,)),
        ],
        compiler_params=WHOLE,
        cost_estimate=cost(0, 1, 10 * columns),
    )(column, *tensors)


def rest_kernel(columns, first, clips, where, own, other):
    blocks = 2 * columns

    def body(first_ref, clip_ref, where_ref, *refs):
        x, gen = refs[-2:]
        column, side = where_ref[0], where_ref[1]
        mine = [2 * (column ^ s) + side for s in range(columns)]
        for s in range(columns):
            x[mine[s]] = refs[s][...]
            x[mine[s] ^ 1] = refs[columns + s][...]
        sources = [(x, t) for t in range(5)]
        student_head(range(0, blocks, 2), first_ref[0], sources[:3], gen, 0)
        at_gen = lambda at: gen[at, 0]
        for s in range(columns):
            o_ref = refs[2 * columns + s]
            o_ref[0:1] = gen[mine[s]]
            teacher_head(blocks, [mine[s]], clip_ref, sources[3:], at_gen, o_ref, None)

    return pl.pallas_call(
        body,
        in_specs=[SMEM] * 3 + [VMEM] * (2 * columns),
        out_specs=[VMEM] * columns,
        out_shape=[jax.ShapeDtypeStruct((2, TOK, HD), jnp.bfloat16)] * columns,
        scratch_shapes=[
            pltpu.VMEM((blocks, 5, TOK, HD), jnp.bfloat16),
            pltpu.VMEM((blocks, 1, TOK, HD), jnp.bfloat16),
        ],
        compiler_params=LOCAL,
        cost_estimate=cost(0, 1, 1),
    )(first, clips, where, *own, *other)


def join(full, order, columns, where, slots, rests):
    peers = len(order)

    def body(where_ref, *refs):
        for i, o_ref in enumerate(refs[peers + columns :]):

            def put(h, tile):
                o_ref[0, :, pl.ds(pl.multiple_of(h * HD, HD), HD)] = tile

            for n, d in enumerate(order):
                for s in range(full):
                    put(s * peers + (where_ref[2] ^ d), refs[n][2 * s + i])
            for s in range(columns):
                put(full * peers + (where_ref[0] ^ s), refs[peers + s][i])

    width = (full * peers + columns) * HD
    return pl.pallas_call(
        body,
        in_specs=[SMEM] + [VMEM] * (peers + columns),
        out_specs=[VMEM] * 2,
        out_shape=[jax.ShapeDtypeStruct((1, TOK, width), jnp.bfloat16)] * 2,
        compiler_params=LOCAL,
        cost_estimate=cost(0, 1, 4 * width // HD),
    )(where, *slots, *rests)


def by_slots_and_columns(tensors, peers, full, rest, first, clips):
    here = lax.axis_index("tm")
    where = jnp.stack([here // 2, here % 2, here]).astype(jnp.int32)

    def swapped(x, by):
        return lax.ppermute(x, "tm", [(i, i ^ by) for i in range(peers)]) if by else x

    order = sorted(range(peers), key=lambda d: (-(d // rest), d % 2, d))

    pieces = rest_pack(full * peers, rest, where[:1], tensors)
    own = [swapped(x, 2 * s) for s, x in enumerate(pieces)]
    packed = slots_pack(full, order, where, tensors)
    packed, own = lax.optimization_barrier((packed, own))
    arrived = [swapped(x, d) for x, d in zip(packed, order)]
    other = [swapped(x, 1) for x in own]
    pieces = rest_kernel(rest, first, clips, where, own, other)
    arrived, pieces = lax.optimization_barrier((arrived, pieces))
    rests = [swapped(x, 2 * s) for s, x in enumerate(pieces)]
    results = slots_kernel(full, order, first, clips, where, arrived)
    results, rests = lax.optimization_barrier((results, rests))
    slots = [swapped(x, d) for x, d in zip(results, order)]
    return tuple(join(full, order, rest, where, slots, rests))


def by_roles(tensors, peers, heads, first, clips):
    here = lax.axis_index("tm")
    role = jnp.where(here < 2 * heads, 1 + here % 2, 0).astype(jnp.int32)[None]
    plan = [
        [(t, min(p // 2, heads - 1)) for t in ((3, 4, 4) if p % 2 else (0, 1, 2))]
        for p in range(peers)
    ]
    arrived = lax.all_to_all(pack(plan, [(0, heads)], tensors), "tm", 0, 0)
    gen = student_kernel(peers, first, role, arrived)
    shared = lax.ppermute(gen, "tm", [(2 * r, 2 * r + 1) for r in range(heads)])
    results = rest_teacher(peers, clips, role, arrived, 0, gen, shared)
    back = lax.all_to_all(results, "tm", 0, 0)
    return tuple(unpack([[(2 * r + i, 0) for r in range(heads)] for i in (0, 1)], back))


def per_device(student_q, student_k, student_v, teacher_q, teacher_k, stagger, clip_lengths):
    heads = student_q.shape[2] // HD
    peers = lax.axis_size("tm")
    full, rest = divmod(heads, peers)
    running = jnp.cumsum(clip_lengths[0])
    block = jnp.arange(peers, dtype=jnp.int32)
    before = running[None, :] <= block[:, None]
    low = jnp.max(jnp.where(before, running[None, :], 0), axis=1)
    high = jnp.min(jnp.where(before, peers, running[None, :]), axis=1)
    large = jnp.where(clip_lengths[0] == peers // 2 + 1, running - clip_lengths[0], 0)
    large = jnp.broadcast_to(jnp.max(large), (peers,))
    clips = jnp.stack([low, high, large]).astype(jnp.int32)
    tensors = (student_q, student_k, student_v, teacher_q, teacher_k)
    if full == 0:
        assert 2 * rest <= peers
        return by_roles(tensors, peers, rest, stagger, clips)
    assert peers == 2 * rest and rest & (rest - 1) == 0
    return by_slots_and_columns(tensors, peers, full, rest, stagger, clips)


def solution(mesh):
    spec = P("seq", "tm", "mp")
    return jax.shard_map(
        per_device,
        mesh=mesh,
        in_specs=(spec,) * 5 + (P("seq"), P("seq", None)),
        out_specs=(spec, spec),
        check_vma=False,
    )
```

```python
import functools
import math

import jax
import jax.numpy as jnp
from jax import lax
from jax.experimental import pallas as pl
from jax.experimental.pallas import tpu as pltpu
from jax.sharding import PartitionSpec as P

HD = 128
TOK = 128
NEG = -1e30
RATE = math.log2(math.e) / math.sqrt(HD)
MIB = 2**20
VMEM = pl.BlockSpec(memory_space=pltpu.VMEM)
SMEM = pl.BlockSpec(memory_space=pltpu.SMEM)
WHOLE = pltpu.CompilerParams(vmem_limit_bytes=60 * MIB)
LOCAL = pltpu.CompilerParams(vmem_limit_bytes=24 * MIB)


def attend(q, k, v, bias):
    g = q.shape[0]
    scores = lax.dot_general(
        q.reshape(g * TOK, HD), k, (((1,), (1,)), ((), ())), preferred_element_type=jnp.float32
    )
    scores = scores.reshape(g, TOK, -1)
    if bias is not None:
        scores = scores + bias
    top = jnp.max(scores, axis=-1, keepdims=True)
    weights = jnp.exp2((scores - top) * RATE)
    total = jnp.sum(weights, axis=-1, keepdims=True)
    weights = weights.astype(jnp.bfloat16).reshape(g * TOK, -1)
    mixed = jnp.dot(weights, v, preferred_element_type=jnp.float32)
    return mixed.reshape(g, TOK, HD) / total


def student_head(pairs, first, sources, o_ref, o_at):
    (q_ref, q_at), (k_ref, k_at), (v_ref, v_at) = sources
    for i in pairs:
        width = (i + 2) * TOK
        block = lax.broadcasted_iota(jnp.int32, (2, 1, width), 2) // TOK
        own = lax.broadcasted_iota(jnp.int32, (2, 1, width), 0) + i
        bias = jnp.where((block == own) | (block >= first) & (block < own), 0.0, NEG)
        k = k_ref[0 : i + 2, k_at].reshape(width, HD)
        v = v_ref[0 : i + 2, v_at].reshape(width, HD)
        o_ref[i : i + 2, o_at] = attend(q_ref[i : i + 2, q_at], k, v, bias).astype(jnp.bfloat16)


def teacher_head(blocks, rows, clip_ref, sources, gen, o_ref, o_at):
    (q_ref, q_at), (k_ref, k_at) = sources
    reach = blocks // 2 + 1
    width = reach * TOK
    offset = lax.broadcasted_iota(jnp.int32, (1, 1, width), 2) // TOK
    for i in rows:
        low = clip_ref[0, i]
        high = clip_ref[1, i]
        start = jnp.minimum(low, blocks - reach)
        block = offset + start
        bias = jnp.where((block >= low) & (block < high), 0.0, NEG)
        k = k_ref[pl.ds(start, reach), k_at].reshape(width, HD)
        v = gen(pl.ds(start, reach)).reshape(width, HD)
        out = attend(q_ref[pl.ds(i, 1), q_at], k, v, bias)
        score = (out[0] - gen(i).astype(jnp.float32)).astype(jnp.bfloat16)
        if o_at is None:
            o_ref[1] = score
        else:
            o_ref[i, o_at] = score


def teacher_whole_head(blocks, clip_ref, sources, gen, o_ref, o_at):
    (q_ref, q_at), (k_ref, k_at) = sources
    reach = blocks // 2 + 1

    def put(at, out):
        score = out - gen(at).astype(jnp.float32)
        o_ref[at, o_at] = score.astype(jnp.bfloat16)

    large = clip_ref[2, 0]
    k = k_ref[pl.ds(large, reach), k_at].reshape(reach * TOK, HD)
    v = gen(pl.ds(large, reach)).reshape(reach * TOK, HD)
    for i in range(0, reach, 2):
        at = pl.ds(large + i, min(2, reach - i))
        put(at, attend(q_ref[at, q_at], k, v, None))
    span = blocks - reach - 1
    offset = lax.broadcasted_iota(jnp.int32, (1, 1, span * TOK), 2) // TOK
    for j in range(blocks - reach):
        i = jnp.where(j < large, j, j + reach)
        low, high = clip_ref[0, i], clip_ref[1, i]
        start = jnp.minimum(low, blocks - span)
        block = offset + start
        bias = jnp.where((block >= low) & (block < high), 0.0, NEG)
        k = k_ref[pl.ds(start, span), k_at].reshape(span * TOK, HD)
        v = gen(pl.ds(start, span)).reshape(span * TOK, HD)
        put(pl.ds(i, 1), attend(q_ref[pl.ds(i, 1), q_at], k, v, bias))


def cost(heads, blocks, units):
    return pl.CostEstimate(
        flops=heads * blocks * blocks * 4 * TOK * TOK * HD,
        bytes_accessed=units * blocks * TOK * HD * 2,
        transcendentals=heads * blocks * blocks * TOK * TOK,
    )


def pack(plan, ranges, tensors):
    peers, units = len(plan), len(plan[0])
    widths = [count * HD for _, count in ranges]
    starts = [sum(widths[:r]) for r in range(len(ranges))]

    def place(h):
        for r, (head, count) in enumerate(ranges):
            if head <= h < head + count:
                return r, starts[r] + (h - head) * HD

    need = []
    for u in range(units):
        need.append(list(dict.fromkeys((plan[p][u][0], place(plan[p][u][1])[0]) for p in range(peers))))
    order = sorted(range(units), key=lambda u: (len(need[u]), u))
    fetch = list(dict.fromkeys(piece for u in order for piece in need[u]))

    def body(*refs):
        o_ref, rows, tiles, in_sem, out_sem = refs[len(tensors) :]
        copies = {}
        for n, (t, r) in enumerate(fetch):
            source = refs[t].at[0, :, pl.ds(ranges[r][0] * HD, widths[r])]
            target = rows.at[t, :, pl.ds(starts[r], widths[r])]
            copies[t, r] = pltpu.make_async_copy(source, target, in_sem.at[n])
            copies[t, r].start()
        sent = []
        for u in order:
            for piece in need[u]:
                if piece in copies:
                    copies.pop(piece).wait()
            for p in range(peers):
                t, h = plan[p][u]
                at = place(h)[1]
                tiles[p, u] = rows[t, :, at : at + HD]
            sent.append(pltpu.make_async_copy(tiles.at[:, u], o_ref.at[:, u], out_sem.at[u]))
            sent[-1].start()
        for copy in sent:
            copy.wait()

    return pl.pallas_call(
        body,
        in_specs=[pl.BlockSpec(memory_space=pl.ANY)] * len(tensors),
        out_specs=pl.BlockSpec(memory_space=pl.ANY),
        out_shape=jax.ShapeDtypeStruct((peers, units, TOK, HD), jnp.bfloat16),
        scratch_shapes=[
            pltpu.VMEM((len(tensors), TOK, sum(widths)), jnp.bfloat16),
            pltpu.VMEM((peers, units, TOK, HD), jnp.bfloat16),
            pltpu.SemaphoreType.DMA((len(fetch),)),
            pltpu.SemaphoreType.DMA((units,)),
        ],
        compiler_params=WHOLE,
        cost_estimate=cost(0, peers, 2 * units),
    )(*tensors)


def unpack(places, back):
    def body(x_ref, *o_refs):
        for o_ref, place in zip(o_refs, places):
            for h, (p, u) in enumerate(place):
                o_ref[0, :, h * HD : (h + 1) * HD] = x_ref[p, u]

    width = len(places[0]) * HD
    return pl.pallas_call(
        body,
        out_shape=[jax.ShapeDtypeStruct((1, TOK, width), jnp.bfloat16) for _ in places],
        compiler_params=LOCAL,
        cost_estimate=cost(0, 1, 4 * len(places[0])),
    )(back)


def student_kernel(blocks, first, role, arrived):
    def body(first_ref, role_ref, x_ref, o_ref):
        @pl.when(role_ref[0] == 1)
        def _():
            sources = [(x_ref, t) for t in range(3)]
            student_head(range(0, blocks, 2), first_ref[0], sources, o_ref, 0)

    return pl.pallas_call(
        body,
        in_specs=[SMEM, SMEM, VMEM],
        out_specs=VMEM,
        out_shape=jax.ShapeDtypeStruct((blocks, 1, TOK, HD), jnp.bfloat16),
        compiler_params=LOCAL,
        cost_estimate=cost(1, blocks, 4),
    )(first, role, arrived)


def rest_teacher(blocks, clips, role, arrived, offset, gen, shared):
    def body(clip_ref, role_ref, x_ref, gen_ref, shared_ref, o_ref):
        @pl.when(role_ref[0] == 1)
        def _():
            o_ref[...] = gen_ref[...]

        @pl.when(role_ref[0] == 2)
        def _():
            sources = [(x_ref, offset + t) for t in range(2)]
            teacher_head(
                blocks, range(blocks), clip_ref, sources, lambda at: shared_ref[at, 0], o_ref, 0
            )

    return pl.pallas_call(
        body,
        in_specs=[SMEM, SMEM, VMEM, VMEM, VMEM],
        out_specs=VMEM,
        out_shape=jax.ShapeDtypeStruct((blocks, 1, TOK, HD), jnp.bfloat16),
        compiler_params=LOCAL,
        cost_estimate=cost(1, blocks, 5),
    )(clips, role, arrived, gen, shared)


def slots_kernel(full, order, first, clips, where, arrived):
    blocks = len(order)

    def body(first_ref, clip_ref, where_ref, *refs):
        x_refs, o_refs, (x, y) = refs[:blocks], refs[blocks : 2 * blocks], refs[2 * blocks :]
        at = [where_ref[2] ^ d for d in order]
        for i in range(blocks):
            x[at[i]] = x_refs[i][...]

        def head(s, carry):
            sources = [(x, 5 * s + t) for t in range(5)]
            student_head(range(0, blocks, 2), first_ref[0], sources[:3], y, 2 * s)
            gen = lambda at: y[at, 2 * s]
            teacher_whole_head(blocks, clip_ref, sources[3:], gen, y, 2 * s + 1)

        lax.fori_loop(0, full, head, None)
        for i in range(blocks):
            o_refs[i][...] = y[at[i]]

    return pl.pallas_call(
        body,
        in_specs=[SMEM] * 3 + [VMEM] * blocks,
        out_specs=[VMEM] * blocks,
        out_shape=[jax.ShapeDtypeStruct((2 * full, TOK, HD), jnp.bfloat16)] * blocks,
        scratch_shapes=[
            pltpu.VMEM((blocks, 5 * full, TOK, HD), jnp.bfloat16),
            pltpu.VMEM((blocks, 2 * full, TOK, HD), jnp.bfloat16),
        ],
        compiler_params=LOCAL,
        cost_estimate=cost(2 * full, blocks, 7 * full),
    )(first, clips, where, *arrived)


def slots_pack(full, order, where, tensors):
    peers = len(order)

    def body(where_ref, *refs):
        o_refs, (rows, sems) = refs[5 : 5 + peers], refs[5 + peers :]
        copies = []
        for t in range(5):
            source = refs[t].at[0, :, pl.ds(0, full * peers * HD)]
            copies.append(pltpu.make_async_copy(source, rows.at[t], sems.at[t]))
            copies[-1].start()
        for t in range(5):
            copies[t].wait()
            for s in range(full):
                for i, d in enumerate(order):
                    at = pl.multiple_of((s * peers + (where_ref[2] ^ d)) * HD, HD)
                    o_refs[i][5 * s + t] = rows[t, :, pl.ds(at, HD)]

    return pl.pallas_call(
        body,
        in_specs=[SMEM] + [pl.BlockSpec(memory_space=pl.ANY)] * 5,
        out_specs=[VMEM] * peers,
        out_shape=[jax.ShapeDtypeStruct((5 * full, TOK, HD), jnp.bfloat16)] * peers,
        scratch_shapes=[
            pltpu.VMEM((5, TOK, full * peers * HD), jnp.bfloat16),
            pltpu.SemaphoreType.DMA((5,)),
        ],
        compiler_params=WHOLE,
        cost_estimate=cost(0, peers, 10 * full),
    )(where, *tensors)


def rest_pack(base, columns, column, tensors):
    def body(column_ref, *refs):
        rows, sems = refs[-2:]
        copies = []
        for t in range(5):
            source = refs[t].at[0, :, pl.ds(base * HD, columns * HD)]
            copies.append(pltpu.make_async_copy(source, rows.at[t], sems.at[t]))
            copies[-1].start()
        for t in range(5):
            copies[t].wait()
            for s in range(columns):
                at = pl.multiple_of((column_ref[0] ^ s) * HD, HD)
                refs[5 + s][t] = rows[t, :, pl.ds(at, HD)]

    return pl.pallas_call(
        body,
        in_specs=[SMEM] + [pl.BlockSpec(memory_space=pl.ANY)] * 5,
        out_specs=[VMEM] * columns,
        out_shape=[jax.ShapeDtypeStruct((5, TOK, HD), jnp.bfloat16)] * columns,
        scratch_shapes=[
            pltpu.VMEM((5, TOK, columns * HD), jnp.bfloat16),
            pltpu.SemaphoreType.DMA((5,)),
        ],
        compiler_params=WHOLE,
        cost_estimate=cost(0, 1, 10 * columns),
    )(column, *tensors)


def rest_kernel(columns, first, clips, where, own, other):
    blocks = 2 * columns

    def body(first_ref, clip_ref, where_ref, *refs):
        x, gen = refs[-2:]
        column, side = where_ref[0], where_ref[1]
        mine = [2 * (column ^ s) + side for s in range(columns)]
        for s in range(columns):
            x[mine[s]] = refs[s][...]
            x[mine[s] ^ 1] = refs[columns + s][...]
        sources = [(x, t) for t in range(5)]
        student_head(range(0, blocks, 2), first_ref[0], sources[:3], gen, 0)
        at_gen = lambda at: gen[at, 0]
        for s in range(columns):
            o_ref = refs[2 * columns + s]
            o_ref[0:1] = gen[mine[s]]
            teacher_head(blocks, [mine[s]], clip_ref, sources[3:], at_gen, o_ref, None)

    return pl.pallas_call(
        body,
        in_specs=[SMEM] * 3 + [VMEM] * (2 * columns),
        out_specs=[VMEM] * columns,
        out_shape=[jax.ShapeDtypeStruct((2, TOK, HD), jnp.bfloat16)] * columns,
        scratch_shapes=[
            pltpu.VMEM((blocks, 5, TOK, HD), jnp.bfloat16),
            pltpu.VMEM((blocks, 1, TOK, HD), jnp.bfloat16),
        ],
        compiler_params=LOCAL,
        cost_estimate=cost(0, 1, 1),
    )(first, clips, where, *own, *other)


def join(full, order, columns, where, slots, rests):
    peers = len(order)

    def body(where_ref, *refs):
        for i, o_ref in enumerate(refs[peers + columns :]):

            def put(h, tile):
                o_ref[0, :, pl.ds(pl.multiple_of(h * HD, HD), HD)] = tile

            for n, d in enumerate(order):
                for s in range(full):
                    put(s * peers + (where_ref[2] ^ d), refs[n][2 * s + i])
            for s in range(columns):
                put(full * peers + (where_ref[0] ^ s), refs[peers + s][i])

    width = (full * peers + columns) * HD
    return pl.pallas_call(
        body,
        in_specs=[SMEM] + [VMEM] * (peers + columns),
        out_specs=[VMEM] * 2,
        out_shape=[jax.ShapeDtypeStruct((1, TOK, width), jnp.bfloat16)] * 2,
        compiler_params=LOCAL,
        cost_estimate=cost(0, 1, 4 * width // HD),
    )(where, *slots, *rests)


def by_slots_and_columns(tensors, peers, full, rest, first, clips):
    here = lax.axis_index("tm")
    where = jnp.stack([here // 2, here % 2, here]).astype(jnp.int32)

    def swapped(x, by):
        return lax.ppermute(x, "tm", [(i, i ^ by) for i in range(peers)]) if by else x

    far = sorted(range(rest, peers), key=lambda d: (d % 2, d))
    near = sorted(range(1, rest), key=lambda d: (d % 2, d))
    order = [far[0], near[0], far[1], *near[1:], *far[2:], 0]

    pieces = rest_pack(full * peers, rest, where[:1], tensors)
    own = [swapped(x, 2 * s) for s, x in enumerate(pieces)]
    packed = slots_pack(full, order, where, tensors)
    packed, own = lax.optimization_barrier((packed, own))
    arrived = [swapped(x, d) for x, d in zip(packed, order)]
    other = [swapped(x, 1) for x in own]
    pieces = rest_kernel(rest, first, clips, where, own, other)
    arrived, pieces = lax.optimization_barrier((arrived, pieces))
    rests = [swapped(x, 2 * s) for s, x in enumerate(pieces)]
    results = slots_kernel(full, order, first, clips, where, arrived)
    results, rests = lax.optimization_barrier((results, rests))
    slots = [swapped(x, d) for x, d in zip(results, order)]
    return tuple(join(full, order, rest, where, slots, rests))


def by_roles(tensors, peers, heads, first, clips):
    here = lax.axis_index("tm")
    role = jnp.where(here < 2 * heads, 1 + here % 2, 0).astype(jnp.int32)[None]
    plan = [
        [(t, min(p // 2, heads - 1)) for t in ((3, 4, 4) if p % 2 else (0, 1, 2))]
        for p in range(peers)
    ]
    arrived = lax.all_to_all(pack(plan, [(0, heads)], tensors), "tm", 0, 0)
    gen = student_kernel(peers, first, role, arrived)
    shared = lax.ppermute(gen, "tm", [(2 * r, 2 * r + 1) for r in range(heads)])
    results = rest_teacher(peers, clips, role, arrived, 0, gen, shared)
    back = lax.all_to_all(results, "tm", 0, 0)
    return tuple(unpack([[(2 * r + i, 0) for r in range(heads)] for i in (0, 1)], back))


def per_device(student_q, student_k, student_v, teacher_q, teacher_k, stagger, clip_lengths):
    heads = student_q.shape[2] // HD
    peers = lax.axis_size("tm")
    full, rest = divmod(heads, peers)
    running = jnp.cumsum(clip_lengths[0])
    block = jnp.arange(peers, dtype=jnp.int32)
    before = running[None, :] <= block[:, None]
    low = jnp.max(jnp.where(before, running[None, :], 0), axis=1)
    high = jnp.min(jnp.where(before, peers, running[None, :]), axis=1)
    large = jnp.where(clip_lengths[0] == peers // 2 + 1, running - clip_lengths[0], 0)
    large = jnp.broadcast_to(jnp.max(large), (peers,))
    clips = jnp.stack([low, high, large]).astype(jnp.int32)
    tensors = (student_q, student_k, student_v, teacher_q, teacher_k)
    if full == 0:
        assert 2 * rest <= peers
        return by_roles(tensors, peers, rest, stagger, clips)
    assert peers == 2 * rest and rest & (rest - 1) == 0
    return by_slots_and_columns(tensors, peers, full, rest, stagger, clips)


def solution(mesh):
    spec = P("seq", "tm", "mp")
    return jax.shard_map(
        per_device,
        mesh=mesh,
        in_specs=(spec,) * 5 + (P("seq"), P("seq", None)),
        out_specs=(spec, spec),
        check_vma=False,
    )
```

```python
import functools
import math

import jax
import jax.numpy as jnp
from jax import lax
from jax.experimental import pallas as pl
from jax.experimental.pallas import tpu as pltpu
from jax.sharding import PartitionSpec as P

HD = 128
TOK = 128
NEG = -1e30
RATE = math.log2(math.e) / math.sqrt(HD)
MIB = 2**20
VMEM = pl.BlockSpec(memory_space=pltpu.VMEM)
SMEM = pl.BlockSpec(memory_space=pltpu.SMEM)
WHOLE = pltpu.CompilerParams(vmem_limit_bytes=60 * MIB)
LOCAL = pltpu.CompilerParams(vmem_limit_bytes=24 * MIB)


def attend(q, k, v, bias):
    g = q.shape[0]
    scores = lax.dot_general(
        q.reshape(g * TOK, HD), k, (((1,), (1,)), ((), ())), preferred_element_type=jnp.float32
    )
    scores = scores.reshape(g, TOK, -1)
    if bias is not None:
        scores = scores + bias
    top = jnp.max(scores, axis=-1, keepdims=True)
    weights = jnp.exp2((scores - top) * RATE)
    total = jnp.sum(weights, axis=-1, keepdims=True)
    weights = weights.astype(jnp.bfloat16).reshape(g * TOK, -1)
    mixed = jnp.dot(weights, v, preferred_element_type=jnp.float32)
    return mixed.reshape(g, TOK, HD) / total


def student_head(pairs, first, sources, o_ref, o_at):
    (q_ref, q_at), (k_ref, k_at), (v_ref, v_at) = sources
    for i in pairs:
        width = (i + 2) * TOK
        block = lax.broadcasted_iota(jnp.int32, (2, 1, width), 2) // TOK
        own = lax.broadcasted_iota(jnp.int32, (2, 1, width), 0) + i
        bias = jnp.where((block == own) | (block >= first) & (block < own), 0.0, NEG)
        k = k_ref[0 : i + 2, k_at].reshape(width, HD)
        v = v_ref[0 : i + 2, v_at].reshape(width, HD)
        o_ref[i : i + 2, o_at] = attend(q_ref[i : i + 2, q_at], k, v, bias).astype(jnp.bfloat16)


def teacher_head(blocks, rows, clip_ref, sources, gen, o_ref, o_at):
    (q_ref, q_at), (k_ref, k_at) = sources
    reach = blocks // 2 + 1
    width = reach * TOK
    offset = lax.broadcasted_iota(jnp.int32, (1, 1, width), 2) // TOK
    for i in rows:
        low = clip_ref[0, i]
        high = clip_ref[1, i]
        start = jnp.minimum(low, blocks - reach)
        block = offset + start
        bias = jnp.where((block >= low) & (block < high), 0.0, NEG)
        k = k_ref[pl.ds(start, reach), k_at].reshape(width, HD)
        v = gen(pl.ds(start, reach)).reshape(width, HD)
        out = attend(q_ref[pl.ds(i, 1), q_at], k, v, bias)
        score = (out[0] - gen(i).astype(jnp.float32)).astype(jnp.bfloat16)
        if o_at is None:
            o_ref[1] = score
        else:
            o_ref[i, o_at] = score


def teacher_whole_head(blocks, clip_ref, sources, gen, o_ref, o_at):
    (q_ref, q_at), (k_ref, k_at) = sources
    reach = blocks // 2 + 1

    def put(at, out):
        score = out - gen(at).astype(jnp.float32)
        o_ref[at, o_at] = score.astype(jnp.bfloat16)

    large = clip_ref[2, 0]
    k = k_ref[pl.ds(large, reach), k_at].reshape(reach * TOK, HD)
    v = gen(pl.ds(large, reach)).reshape(reach * TOK, HD)
    for i in range(0, reach, 2):
        at = pl.ds(large + i, min(2, reach - i))
        put(at, attend(q_ref[at, q_at], k, v, None))
    span = blocks - reach - 1
    offset = lax.broadcasted_iota(jnp.int32, (1, 1, span * TOK), 2) // TOK
    for j in range(blocks - reach):
        i = jnp.where(j < large, j, j + reach)
        low, high = clip_ref[0, i], clip_ref[1, i]
        start = jnp.minimum(low, blocks - span)
        block = offset + start
        bias = jnp.where((block >= low) & (block < high), 0.0, NEG)
        k = k_ref[pl.ds(start, span), k_at].reshape(span * TOK, HD)
        v = gen(pl.ds(start, span)).reshape(span * TOK, HD)
        put(pl.ds(i, 1), attend(q_ref[pl.ds(i, 1), q_at], k, v, bias))


def cost(heads, blocks, units):
    return pl.CostEstimate(
        flops=heads * blocks * blocks * 4 * TOK * TOK * HD,
        bytes_accessed=units * blocks * TOK * HD * 2,
        transcendentals=heads * blocks * blocks * TOK * TOK,
    )


def pack(plan, ranges, tensors):
    peers, units = len(plan), len(plan[0])
    widths = [count * HD for _, count in ranges]
    starts = [sum(widths[:r]) for r in range(len(ranges))]

    def place(h):
        for r, (head, count) in enumerate(ranges):
            if head <= h < head + count:
                return r, starts[r] + (h - head) * HD

    need = []
    for u in range(units):
        need.append(list(dict.fromkeys((plan[p][u][0], place(plan[p][u][1])[0]) for p in range(peers))))
    order = sorted(range(units), key=lambda u: (len(need[u]), u))
    fetch = list(dict.fromkeys(piece for u in order for piece in need[u]))

    def body(*refs):
        o_ref, rows, tiles, in_sem, out_sem = refs[len(tensors) :]
        copies = {}
        for n, (t, r) in enumerate(fetch):
            source = refs[t].at[0, :, pl.ds(ranges[r][0] * HD, widths[r])]
            target = rows.at[t, :, pl.ds(starts[r], widths[r])]
            copies[t, r] = pltpu.make_async_copy(source, target, in_sem.at[n])
            copies[t, r].start()
        sent = []
        for u in order:
            for piece in need[u]:
                if piece in copies:
                    copies.pop(piece).wait()
            for p in range(peers):
                t, h = plan[p][u]
                at = place(h)[1]
                tiles[p, u] = rows[t, :, at : at + HD]
            sent.append(pltpu.make_async_copy(tiles.at[:, u], o_ref.at[:, u], out_sem.at[u]))
            sent[-1].start()
        for copy in sent:
            copy.wait()

    return pl.pallas_call(
        body,
        in_specs=[pl.BlockSpec(memory_space=pl.ANY)] * len(tensors),
        out_specs=pl.BlockSpec(memory_space=pl.ANY),
        out_shape=jax.ShapeDtypeStruct((peers, units, TOK, HD), jnp.bfloat16),
        scratch_shapes=[
            pltpu.VMEM((len(tensors), TOK, sum(widths)), jnp.bfloat16),
            pltpu.VMEM((peers, units, TOK, HD), jnp.bfloat16),
            pltpu.SemaphoreType.DMA((len(fetch),)),
            pltpu.SemaphoreType.DMA((units,)),
        ],
        compiler_params=WHOLE,
        cost_estimate=cost(0, peers, 2 * units),
    )(*tensors)


def unpack(places, back):
    def body(x_ref, *o_refs):
        for o_ref, place in zip(o_refs, places):
            for h, (p, u) in enumerate(place):
                o_ref[0, :, h * HD : (h + 1) * HD] = x_ref[p, u]

    width = len(places[0]) * HD
    return pl.pallas_call(
        body,
        out_shape=[jax.ShapeDtypeStruct((1, TOK, width), jnp.bfloat16) for _ in places],
        compiler_params=LOCAL,
        cost_estimate=cost(0, 1, 4 * len(places[0])),
    )(back)


def student_kernel(blocks, first, role, arrived):
    def body(first_ref, role_ref, x_ref, o_ref):
        @pl.when(role_ref[0] == 1)
        def _():
            sources = [(x_ref, t) for t in range(3)]
            student_head(range(0, blocks, 2), first_ref[0], sources, o_ref, 0)

    return pl.pallas_call(
        body,
        in_specs=[SMEM, SMEM, VMEM],
        out_specs=VMEM,
        out_shape=jax.ShapeDtypeStruct((blocks, 1, TOK, HD), jnp.bfloat16),
        compiler_params=LOCAL,
        cost_estimate=cost(1, blocks, 4),
    )(first, role, arrived)


def rest_teacher(blocks, clips, role, arrived, offset, gen, shared):
    def body(clip_ref, role_ref, x_ref, gen_ref, shared_ref, o_ref):
        @pl.when(role_ref[0] == 1)
        def _():
            o_ref[...] = gen_ref[...]

        @pl.when(role_ref[0] == 2)
        def _():
            sources = [(x_ref, offset + t) for t in range(2)]
            teacher_head(
                blocks, range(blocks), clip_ref, sources, lambda at: shared_ref[at, 0], o_ref, 0
            )

    return pl.pallas_call(
        body,
        in_specs=[SMEM, SMEM, VMEM, VMEM, VMEM],
        out_specs=VMEM,
        out_shape=jax.ShapeDtypeStruct((blocks, 1, TOK, HD), jnp.bfloat16),
        compiler_params=LOCAL,
        cost_estimate=cost(1, blocks, 5),
    )(clips, role, arrived, gen, shared)


def slots_kernel(full, order, home, first, clips, where, arrived):
    blocks = len(order)

    def body(first_ref, clip_ref, where_ref, *refs):
        x_refs, o_refs, (x, y) = refs[:blocks], refs[blocks : 2 * blocks], refs[2 * blocks :]
        at = [where_ref[2] ^ d for d in order]
        for i in range(blocks):
            x[at[i]] = x_refs[i][0 : 5 * full]

        def head(s, carry):
            sources = [(x, 5 * s + t) for t in range(5)]
            student_head(range(0, blocks, 2), first_ref[0], sources[:3], y, 2 * s)
            gen = lambda at: y[at, 2 * s]
            teacher_whole_head(blocks, clip_ref, sources[3:], gen, y, 2 * s + 1)

        lax.fori_loop(0, full, head, None)
        for i, d in enumerate(home):
            o_refs[i][...] = y[where_ref[2] ^ d]

    return pl.pallas_call(
        body,
        in_specs=[SMEM] * 3 + [VMEM] * blocks,
        out_specs=[VMEM] * blocks,
        out_shape=[jax.ShapeDtypeStruct((2 * full, TOK, HD), jnp.bfloat16)] * blocks,
        scratch_shapes=[
            pltpu.VMEM((blocks, 5 * full, TOK, HD), jnp.bfloat16),
            pltpu.VMEM((blocks, 2 * full, TOK, HD), jnp.bfloat16),
        ],
        compiler_params=LOCAL,
        cost_estimate=cost(2 * full, blocks, 7 * full),
    )(first, clips, where, *arrived)


def slots_pack(full, order, where, tensors):
    peers = len(order)

    def body(where_ref, *refs):
        o_refs, (rows, sems) = refs[5 : 5 + peers], refs[5 + peers :]
        copies = []
        for t in range(5):
            source = refs[t].at[0, :, pl.ds(0, full * peers * HD)]
            copies.append(pltpu.make_async_copy(source, rows.at[t], sems.at[t]))
            copies[-1].start()
        for t in range(5):
            copies[t].wait()
            for s in range(full):
                for i, d in enumerate(order):
                    at = pl.multiple_of((s * peers + (where_ref[2] ^ d)) * HD, HD)
                    o_refs[i][5 * s + t] = rows[t, :, pl.ds(at, HD)]

    return pl.pallas_call(
        body,
        in_specs=[SMEM] + [pl.BlockSpec(memory_space=pl.ANY)] * 5,
        out_specs=[VMEM] * peers,
        out_shape=[jax.ShapeDtypeStruct((5 * full, TOK, HD), jnp.bfloat16)] * peers,
        scratch_shapes=[
            pltpu.VMEM((5, TOK, full * peers * HD), jnp.bfloat16),
            pltpu.SemaphoreType.DMA((5,)),
        ],
        compiler_params=WHOLE,
        cost_estimate=cost(0, peers, 10 * full),
    )(where, *tensors)


def rest_pack(base, columns, column, tensors):
    def body(column_ref, *refs):
        rows, sems = refs[-2:]
        copies = []
        for t in range(5):
            source = refs[t].at[0, :, pl.ds(base * HD, columns * HD)]
            copies.append(pltpu.make_async_copy(source, rows.at[t], sems.at[t]))
            copies[-1].start()
        for t in range(5):
            copies[t].wait()
            for s in range(columns):
                at = pl.multiple_of((column_ref[0] ^ s) * HD, HD)
                refs[5 + s][t] = rows[t, :, pl.ds(at, HD)]

    return pl.pallas_call(
        body,
        in_specs=[SMEM] + [pl.BlockSpec(memory_space=pl.ANY)] * 5,
        out_specs=[VMEM] * columns,
        out_shape=[jax.ShapeDtypeStruct((5, TOK, HD), jnp.bfloat16)] * columns,
        scratch_shapes=[
            pltpu.VMEM((5, TOK, columns * HD), jnp.bfloat16),
            pltpu.SemaphoreType.DMA((5,)),
        ],
        compiler_params=WHOLE,
        cost_estimate=cost(0, 1, 10 * columns),
    )(column, *tensors)


def rest_kernel(columns, offset, first, clips, where, own, across):
    blocks = 2 * columns

    def body(first_ref, clip_ref, where_ref, *refs):
        x, gen = refs[-2:]
        column, side = where_ref[0], where_ref[1]
        mine = [2 * (column ^ s) + side for s in range(columns)]
        for s in range(columns):
            x[mine[s]] = refs[s][...]
            x[mine[s] ^ 1] = refs[columns][offset + 5 * s : offset + 5 * s + 5]
        sources = [(x, t) for t in range(5)]
        student_head(range(0, blocks, 2), first_ref[0], sources[:3], gen, 0)
        at_gen = lambda at: gen[at, 0]
        for s in range(columns):
            o_ref = refs[columns + 1 + s]
            o_ref[0:1] = gen[mine[s]]
            teacher_head(blocks, [mine[s]], clip_ref, sources[3:], at_gen, o_ref, None)

    return pl.pallas_call(
        body,
        in_specs=[SMEM] * 3 + [VMEM] * (columns + 1),
        out_specs=[VMEM] * columns,
        out_shape=[jax.ShapeDtypeStruct((2, TOK, HD), jnp.bfloat16)] * columns,
        scratch_shapes=[
            pltpu.VMEM((blocks, 5, TOK, HD), jnp.bfloat16),
            pltpu.VMEM((blocks, 1, TOK, HD), jnp.bfloat16),
        ],
        compiler_params=LOCAL,
        cost_estimate=cost(0, 1, 1),
    )(first, clips, where, *own, across)


def join(full, order, columns, where, slots, rests):
    peers = len(order)

    def body(where_ref, *refs):
        for i, o_ref in enumerate(refs[peers + columns :]):

            def put(h, tile):
                o_ref[0, :, pl.ds(pl.multiple_of(h * HD, HD), HD)] = tile

            for n, d in enumerate(order):
                for s in range(full):
                    put(s * peers + (where_ref[2] ^ d), refs[n][2 * s + i])
            for s in range(columns):
                put(full * peers + (where_ref[0] ^ s), refs[peers + s][i])

    width = (full * peers + columns) * HD
    return pl.pallas_call(
        body,
        in_specs=[SMEM] + [VMEM] * (peers + columns),
        out_specs=[VMEM] * 2,
        out_shape=[jax.ShapeDtypeStruct((1, TOK, width), jnp.bfloat16)] * 2,
        compiler_params=LOCAL,
        cost_estimate=cost(0, 1, 4 * width // HD),
    )(where, *slots, *rests)


def by_slots_and_columns(tensors, peers, full, rest, first, clips):
    here = lax.axis_index("tm")
    where = jnp.stack([here // 2, here % 2, here]).astype(jnp.int32)

    def swapped(x, by):
        return lax.ppermute(x, "tm", [(i, i ^ by) for i in range(peers)]) if by else x

    far = sorted(range(rest, peers), key=lambda d: (d % 2, d))
    near = sorted(range(1, rest), key=lambda d: (d % 2, d))
    there = [d for d in near if d != 1] + far + [1, 0]
    home = near[:2] + far + near[2:] + [0]

    pieces = rest_pack(full * peers, rest, where[:1], tensors)
    own = [swapped(x, 2 * s) for s, x in enumerate(pieces)]
    packed = dict(zip(there, slots_pack(full, there, where, tensors)))
    arrived = {d: swapped(packed[d], d) for d in there if d != 1}
    across = jnp.concatenate([packed[1], *own])
    across, _ = lax.optimization_barrier((across, [arrived[d] for d in near if d != 1]))
    arrived[1] = swapped(across, 1)
    pieces = rest_kernel(rest, 5 * full, first, clips, where, own, arrived[1])
    arrived, pieces = lax.optimization_barrier(([arrived[d] for d in there], pieces))
    rests = [swapped(x, 2 * s) for s, x in enumerate(pieces)]
    results = slots_kernel(full, there, home, first, clips, where, arrived)
    results, rests = lax.optimization_barrier((results, rests))
    slots = [swapped(x, d) for x, d in zip(results, home)]
    return tuple(join(full, home, rest, where, slots, rests))


def by_roles(tensors, peers, heads, first, clips):
    here = lax.axis_index("tm")
    role = jnp.where(here < 2 * heads, 1 + here % 2, 0).astype(jnp.int32)[None]
    plan = [
        [(t, min(p // 2, heads - 1)) for t in ((3, 4, 4) if p % 2 else (0, 1, 2))]
        for p in range(peers)
    ]
    arrived = lax.all_to_all(pack(plan, [(0, heads)], tensors), "tm", 0, 0)
    gen = student_kernel(peers, first, role, arrived)
    shared = lax.ppermute(gen, "tm", [(2 * r, 2 * r + 1) for r in range(heads)])
    results = rest_teacher(peers, clips, role, arrived, 0, gen, shared)
    back = lax.all_to_all(results, "tm", 0, 0)
    return tuple(unpack([[(2 * r + i, 0) for r in range(heads)] for i in (0, 1)], back))


def per_device(student_q, student_k, student_v, teacher_q, teacher_k, stagger, clip_lengths):
    heads = student_q.shape[2] // HD
    peers = lax.axis_size("tm")
    full, rest = divmod(heads, peers)
    running = jnp.cumsum(clip_lengths[0])
    block = jnp.arange(peers, dtype=jnp.int32)
    before = running[None, :] <= block[:, None]
    low = jnp.max(jnp.where(before, running[None, :], 0), axis=1)
    high = jnp.min(jnp.where(before, peers, running[None, :]), axis=1)
    large = jnp.where(clip_lengths[0] == peers // 2 + 1, running - clip_lengths[0], 0)
    large = jnp.broadcast_to(jnp.max(large), (peers,))
    clips = jnp.stack([low, high, large]).astype(jnp.int32)
    tensors = (student_q, student_k, student_v, teacher_q, teacher_k)
    if full == 0:
        assert 2 * rest <= peers
        return by_roles(tensors, peers, rest, stagger, clips)
    assert peers == 2 * rest and rest & (rest - 1) == 0
    return by_slots_and_columns(tensors, peers, full, rest, stagger, clips)


def solution(mesh):
    spec = P("seq", "tm", "mp")
    return jax.shard_map(
        per_device,
        mesh=mesh,
        in_specs=(spec,) * 5 + (P("seq"), P("seq", None)),
        out_specs=(spec, spec),
        check_vma=False,
    )
```

```python
import functools
import math

import jax
import jax.numpy as jnp
from jax import lax
from jax.experimental import pallas as pl
from jax.experimental.pallas import tpu as pltpu
from jax.sharding import PartitionSpec as P

HD = 128
TOK = 128
NEG = -1e30
RATE = math.log2(math.e) / math.sqrt(HD)
MIB = 2**20
VMEM = pl.BlockSpec(memory_space=pltpu.VMEM)
SMEM = pl.BlockSpec(memory_space=pltpu.SMEM)
WHOLE = pltpu.CompilerParams(vmem_limit_bytes=60 * MIB)
LOCAL = pltpu.CompilerParams(vmem_limit_bytes=24 * MIB)


def attend(q, k, v, bias):
    g = q.shape[0]
    scores = lax.dot_general(
        q.reshape(g * TOK, HD), k, (((1,), (1,)), ((), ())), preferred_element_type=jnp.float32
    )
    scores = scores.reshape(g, TOK, -1)
    if bias is not None:
        scores = scores + bias
    top = jnp.max(scores, axis=-1, keepdims=True)
    weights = jnp.exp2((scores - top) * RATE)
    total = jnp.sum(weights, axis=-1, keepdims=True)
    weights = weights.astype(jnp.bfloat16).reshape(g * TOK, -1)
    mixed = jnp.dot(weights, v, preferred_element_type=jnp.float32)
    return mixed.reshape(g, TOK, HD) / total


def student_head(pairs, first, sources, o_ref, o_at):
    (q_ref, q_at), (k_ref, k_at), (v_ref, v_at) = sources
    for i in pairs:
        width = (i + 2) * TOK
        block = lax.broadcasted_iota(jnp.int32, (2, 1, width), 2) // TOK
        own = lax.broadcasted_iota(jnp.int32, (2, 1, width), 0) + i
        bias = jnp.where((block == own) | (block >= first) & (block < own), 0.0, NEG)
        k = k_ref[0 : i + 2, k_at].reshape(width, HD)
        v = v_ref[0 : i + 2, v_at].reshape(width, HD)
        o_ref[i : i + 2, o_at] = attend(q_ref[i : i + 2, q_at], k, v, bias).astype(jnp.bfloat16)


def teacher_head(blocks, rows, clip_ref, sources, gen, o_ref, o_at):
    (q_ref, q_at), (k_ref, k_at) = sources
    reach = blocks // 2 + 1
    width = reach * TOK
    offset = lax.broadcasted_iota(jnp.int32, (1, 1, width), 2) // TOK
    for i in rows:
        low = clip_ref[0, i]
        high = clip_ref[1, i]
        start = jnp.minimum(low, blocks - reach)
        block = offset + start
        bias = jnp.where((block >= low) & (block < high), 0.0, NEG)
        k = k_ref[pl.ds(start, reach), k_at].reshape(width, HD)
        v = gen(pl.ds(start, reach)).reshape(width, HD)
        out = attend(q_ref[pl.ds(i, 1), q_at], k, v, bias)
        score = (out[0] - gen(i).astype(jnp.float32)).astype(jnp.bfloat16)
        if o_at is None:
            o_ref[1] = score
        else:
            o_ref[i, o_at] = score


def teacher_whole_head(blocks, clip_ref, sources, gen, o_ref, o_at):
    (q_ref, q_at), (k_ref, k_at) = sources
    reach = blocks // 2 + 1

    def put(at, out):
        score = out - gen(at).astype(jnp.float32)
        o_ref[at, o_at] = score.astype(jnp.bfloat16)

    large = clip_ref[2, 0]
    k = k_ref[pl.ds(large, reach), k_at].reshape(reach * TOK, HD)
    v = gen(pl.ds(large, reach)).reshape(reach * TOK, HD)
    for i in range(0, reach, 2):
        at = pl.ds(large + i, min(2, reach - i))
        put(at, attend(q_ref[at, q_at], k, v, None))
    span = blocks - reach - 1
    offset = lax.broadcasted_iota(jnp.int32, (1, 1, span * TOK), 2) // TOK
    for j in range(blocks - reach):
        i = jnp.where(j < large, j, j + reach)
        low, high = clip_ref[0, i], clip_ref[1, i]
        start = jnp.minimum(low, blocks - span)
        block = offset + start
        bias = jnp.where((block >= low) & (block < high), 0.0, NEG)
        k = k_ref[pl.ds(start, span), k_at].reshape(span * TOK, HD)
        v = gen(pl.ds(start, span)).reshape(span * TOK, HD)
        put(pl.ds(i, 1), attend(q_ref[pl.ds(i, 1), q_at], k, v, bias))


def cost(heads, blocks, units):
    return pl.CostEstimate(
        flops=heads * blocks * blocks * 4 * TOK * TOK * HD,
        bytes_accessed=units * blocks * TOK * HD * 2,
        transcendentals=heads * blocks * blocks * TOK * TOK,
    )


def pack(plan, ranges, tensors):
    peers, units = len(plan), len(plan[0])
    widths = [count * HD for _, count in ranges]
    starts = [sum(widths[:r]) for r in range(len(ranges))]

    def place(h):
        for r, (head, count) in enumerate(ranges):
            if head <= h < head + count:
                return r, starts[r] + (h - head) * HD

    need = []
    for u in range(units):
        need.append(list(dict.fromkeys((plan[p][u][0], place(plan[p][u][1])[0]) for p in range(peers))))
    order = sorted(range(units), key=lambda u: (len(need[u]), u))
    fetch = list(dict.fromkeys(piece for u in order for piece in need[u]))

    def body(*refs):
        o_ref, rows, tiles, in_sem, out_sem = refs[len(tensors) :]
        copies = {}
        for n, (t, r) in enumerate(fetch):
            source = refs[t].at[0, :, pl.ds(ranges[r][0] * HD, widths[r])]
            target = rows.at[t, :, pl.ds(starts[r], widths[r])]
            copies[t, r] = pltpu.make_async_copy(source, target, in_sem.at[n])
            copies[t, r].start()
        sent = []
        for u in order:
            for piece in need[u]:
                if piece in copies:
                    copies.pop(piece).wait()
            for p in range(peers):
                t, h = plan[p][u]
                at = place(h)[1]
                tiles[p, u] = rows[t, :, at : at + HD]
            sent.append(pltpu.make_async_copy(tiles.at[:, u], o_ref.at[:, u], out_sem.at[u]))
            sent[-1].start()
        for copy in sent:
            copy.wait()

    return pl.pallas_call(
        body,
        in_specs=[pl.BlockSpec(memory_space=pl.ANY)] * len(tensors),
        out_specs=pl.BlockSpec(memory_space=pl.ANY),
        out_shape=jax.ShapeDtypeStruct((peers, units, TOK, HD), jnp.bfloat16),
        scratch_shapes=[
            pltpu.VMEM((len(tensors), TOK, sum(widths)), jnp.bfloat16),
            pltpu.VMEM((peers, units, TOK, HD), jnp.bfloat16),
            pltpu.SemaphoreType.DMA((len(fetch),)),
            pltpu.SemaphoreType.DMA((units,)),
        ],
        compiler_params=WHOLE,
        cost_estimate=cost(0, peers, 2 * units),
    )(*tensors)


def unpack(places, back):
    def body(x_ref, *o_refs):
        for o_ref, place in zip(o_refs, places):
            for h, (p, u) in enumerate(place):
                o_ref[0, :, h * HD : (h + 1) * HD] = x_ref[p, u]

    width = len(places[0]) * HD
    return pl.pallas_call(
        body,
        out_shape=[jax.ShapeDtypeStruct((1, TOK, width), jnp.bfloat16) for _ in places],
        compiler_params=LOCAL,
        cost_estimate=cost(0, 1, 4 * len(places[0])),
    )(back)


def student_kernel(blocks, first, role, arrived):
    def body(first_ref, role_ref, x_ref, o_ref):
        @pl.when(role_ref[0] == 1)
        def _():
            sources = [(x_ref, t) for t in range(3)]
            student_head(range(0, blocks, 2), first_ref[0], sources, o_ref, 0)

    return pl.pallas_call(
        body,
        in_specs=[SMEM, SMEM, VMEM],
        out_specs=VMEM,
        out_shape=jax.ShapeDtypeStruct((blocks, 1, TOK, HD), jnp.bfloat16),
        compiler_params=LOCAL,
        cost_estimate=cost(1, blocks, 4),
    )(first, role, arrived)


def rest_teacher(blocks, clips, role, arrived, offset, gen, shared):
    def body(clip_ref, role_ref, x_ref, gen_ref, shared_ref, o_ref):
        @pl.when(role_ref[0] == 1)
        def _():
            o_ref[...] = gen_ref[...]

        @pl.when(role_ref[0] == 2)
        def _():
            sources = [(x_ref, offset + t) for t in range(2)]
            teacher_head(
                blocks, range(blocks), clip_ref, sources, lambda at: shared_ref[at, 0], o_ref, 0
            )

    return pl.pallas_call(
        body,
        in_specs=[SMEM, SMEM, VMEM, VMEM, VMEM],
        out_specs=VMEM,
        out_shape=jax.ShapeDtypeStruct((blocks, 1, TOK, HD), jnp.bfloat16),
        compiler_params=LOCAL,
        cost_estimate=cost(1, blocks, 5),
    )(clips, role, arrived, gen, shared)


def slots_kernel(full, order, home, first, clips, where, arrived):
    blocks = len(order)

    def body(first_ref, clip_ref, where_ref, *refs):
        x_refs, o_refs, (x, y) = refs[:blocks], refs[blocks : 2 * blocks], refs[2 * blocks :]
        at = [where_ref[2] ^ d for d in order]
        for i in range(blocks):
            x[at[i]] = x_refs[i][...]

        def head(s, carry):
            sources = [(x, 5 * s + t) for t in range(5)]
            student_head(range(0, blocks, 2), first_ref[0], sources[:3], y, 2 * s)
            gen = lambda at: y[at, 2 * s]
            teacher_whole_head(blocks, clip_ref, sources[3:], gen, y, 2 * s + 1)

        lax.fori_loop(0, full, head, None)
        for i, d in enumerate(home):
            o_refs[i][...] = y[where_ref[2] ^ d]

    return pl.pallas_call(
        body,
        in_specs=[SMEM] * 3 + [VMEM] * blocks,
        out_specs=[VMEM] * blocks,
        out_shape=[jax.ShapeDtypeStruct((2 * full, TOK, HD), jnp.bfloat16)] * blocks,
        scratch_shapes=[
            pltpu.VMEM((blocks, 5 * full, TOK, HD), jnp.bfloat16),
            pltpu.VMEM((blocks, 2 * full, TOK, HD), jnp.bfloat16),
        ],
        compiler_params=LOCAL,
        cost_estimate=cost(2 * full, blocks, 7 * full),
    )(first, clips, where, *arrived)


def slots_pack(full, order, where, tensors):
    peers = len(order)

    def body(where_ref, *refs):
        o_refs, (rows, sems) = refs[5 : 5 + peers], refs[5 + peers :]
        copies = []
        for t in range(5):
            source = refs[t].at[0, :, pl.ds(0, full * peers * HD)]
            copies.append(pltpu.make_async_copy(source, rows.at[t], sems.at[t]))
            copies[-1].start()
        for t in range(5):
            copies[t].wait()
            for s in range(full):
                for i, d in enumerate(order):
                    at = pl.multiple_of((s * peers + (where_ref[2] ^ d)) * HD, HD)
                    o_refs[i][5 * s + t] = rows[t, :, pl.ds(at, HD)]

    return pl.pallas_call(
        body,
        in_specs=[SMEM] + [pl.BlockSpec(memory_space=pl.ANY)] * 5,
        out_specs=[VMEM] * peers,
        out_shape=[jax.ShapeDtypeStruct((5 * full, TOK, HD), jnp.bfloat16)] * peers,
        scratch_shapes=[
            pltpu.VMEM((5, TOK, full * peers * HD), jnp.bfloat16),
            pltpu.SemaphoreType.DMA((5,)),
        ],
        compiler_params=WHOLE,
        cost_estimate=cost(0, peers, 10 * full),
    )(where, *tensors)


def rest_pack(base, columns, column, tensors):
    def body(column_ref, *refs):
        rows, sems = refs[-2:]
        copies = []
        for t in range(5):
            source = refs[t].at[0, :, pl.ds(base * HD, columns * HD)]
            copies.append(pltpu.make_async_copy(source, rows.at[t], sems.at[t]))
            copies[-1].start()
        for t in range(5):
            copies[t].wait()
            for s in range(columns):
                at = pl.multiple_of((column_ref[0] ^ s) * HD, HD)
                refs[5 + s][t] = rows[t, :, pl.ds(at, HD)]

    return pl.pallas_call(
        body,
        in_specs=[SMEM] + [pl.BlockSpec(memory_space=pl.ANY)] * 5,
        out_specs=[VMEM] * columns,
        out_shape=[jax.ShapeDtypeStruct((5, TOK, HD), jnp.bfloat16)] * columns,
        scratch_shapes=[
            pltpu.VMEM((5, TOK, columns * HD), jnp.bfloat16),
            pltpu.SemaphoreType.DMA((5,)),
        ],
        compiler_params=WHOLE,
        cost_estimate=cost(0, 1, 10 * columns),
    )(column, *tensors)


def rest_kernel(columns, first, clips, where, own, other):
    blocks = 2 * columns

    def body(first_ref, clip_ref, where_ref, *refs):
        x, gen = refs[-2:]
        column, side = where_ref[0], where_ref[1]
        mine = [2 * (column ^ s) + side for s in range(columns)]
        for s in range(columns):
            x[mine[s]] = refs[s][...]
            x[mine[s] ^ 1] = refs[columns + s][...]
        sources = [(x, t) for t in range(5)]
        student_head(range(0, blocks, 2), first_ref[0], sources[:3], gen, 0)
        at_gen = lambda at: gen[at, 0]
        for s in range(columns):
            o_ref = refs[2 * columns + s]
            o_ref[0:1] = gen[mine[s]]
            teacher_head(blocks, [mine[s]], clip_ref, sources[3:], at_gen, o_ref, None)

    return pl.pallas_call(
        body,
        in_specs=[SMEM] * 3 + [VMEM] * (2 * columns),
        out_specs=[VMEM] * columns,
        out_shape=[jax.ShapeDtypeStruct((2, TOK, HD), jnp.bfloat16)] * columns,
        scratch_shapes=[
            pltpu.VMEM((blocks, 5, TOK, HD), jnp.bfloat16),
            pltpu.VMEM((blocks, 1, TOK, HD), jnp.bfloat16),
        ],
        compiler_params=LOCAL,
        cost_estimate=cost(0, 1, 1),
    )(first, clips, where, *own, *other)


def join(full, order, columns, where, slots, rests):
    peers = len(order)

    def body(where_ref, *refs):
        for i, o_ref in enumerate(refs[peers + columns :]):

            def put(h, tile):
                o_ref[0, :, pl.ds(pl.multiple_of(h * HD, HD), HD)] = tile

            for n, d in enumerate(order):
                for s in range(full):
                    put(s * peers + (where_ref[2] ^ d), refs[n][2 * s + i])
            for s in range(columns):
                put(full * peers + (where_ref[0] ^ s), refs[peers + s][i])

    width = (full * peers + columns) * HD
    return pl.pallas_call(
        body,
        in_specs=[SMEM] + [VMEM] * (peers + columns),
        out_specs=[VMEM] * 2,
        out_shape=[jax.ShapeDtypeStruct((1, TOK, width), jnp.bfloat16)] * 2,
        compiler_params=LOCAL,
        cost_estimate=cost(0, 1, 4 * width // HD),
    )(where, *slots, *rests)


def by_slots_and_columns(tensors, peers, full, rest, first, clips):
    here = lax.axis_index("tm")
    where = jnp.stack([here // 2, here % 2, here]).astype(jnp.int32)

    def swapped(x, by):
        return lax.ppermute(x, "tm", [(i, i ^ by) for i in range(peers)]) if by else x

    far = list(range(rest, peers))
    near = sorted(range(1, rest), key=lambda d: (d % 2, d))
    there = [far[0], near[0], far[1], *near[1:], *far[2:], 0]
    home = [*range(1, peers), 0]

    pieces = rest_pack(full * peers, rest, where[:1], tensors)
    own = [swapped(x, 2 * s) for s, x in enumerate(pieces)]
    packed = slots_pack(full, there, where, tensors)
    arrived = [swapped(x, d) for x, d in zip(packed, there)]
    other = [swapped(x, 1) for x in own]
    pieces = rest_kernel(rest, first, clips, where, own, other)
    arrived, pieces = lax.optimization_barrier((arrived, pieces))
    rests = [swapped(x, 2 * s) for s, x in enumerate(pieces)]
    results = slots_kernel(full, there, home, first, clips, where, arrived)
    results, rests = lax.optimization_barrier((results, rests))
    slots = [swapped(x, d) for x, d in zip(results, home)]
    return tuple(join(full, home, rest, where, slots, rests))


def by_roles(tensors, peers, heads, first, clips):
    here = lax.axis_index("tm")
    role = jnp.where(here < 2 * heads, 1 + here % 2, 0).astype(jnp.int32)[None]
    plan = [
        [(t, min(p // 2, heads - 1)) for t in ((3, 4, 4) if p % 2 else (0, 1, 2))]
        for p in range(peers)
    ]
    arrived = lax.all_to_all(pack(plan, [(0, heads)], tensors), "tm", 0, 0)
    gen = student_kernel(peers, first, role, arrived)
    shared = lax.ppermute(gen, "tm", [(2 * r, 2 * r + 1) for r in range(heads)])
    results = rest_teacher(peers, clips, role, arrived, 0, gen, shared)
    back = lax.all_to_all(results, "tm", 0, 0)
    return tuple(unpack([[(2 * r + i, 0) for r in range(heads)] for i in (0, 1)], back))


def per_device(student_q, student_k, student_v, teacher_q, teacher_k, stagger, clip_lengths):
    heads = student_q.shape[2] // HD
    peers = lax.axis_size("tm")
    full, rest = divmod(heads, peers)
    running = jnp.cumsum(clip_lengths[0])
    block = jnp.arange(peers, dtype=jnp.int32)
    before = running[None, :] <= block[:, None]
    low = jnp.max(jnp.where(before, running[None, :], 0), axis=1)
    high = jnp.min(jnp.where(before, peers, running[None, :]), axis=1)
    large = jnp.where(clip_lengths[0] == peers // 2 + 1, running - clip_lengths[0], 0)
    large = jnp.broadcast_to(jnp.max(large), (peers,))
    clips = jnp.stack([low, high, large]).astype(jnp.int32)
    tensors = (student_q, student_k, student_v, teacher_q, teacher_k)
    if full == 0:
        assert 2 * rest <= peers
        return by_roles(tensors, peers, rest, stagger, clips)
    assert peers == 2 * rest and rest & (rest - 1) == 0
    return by_slots_and_columns(tensors, peers, full, rest, stagger, clips)


def solution(mesh):
    spec = P("seq", "tm", "mp")
    return jax.shard_map(
        per_device,
        mesh=mesh,
        in_specs=(spec,) * 5 + (P("seq"), P("seq", None)),
        out_specs=(spec, spec),
        check_vma=False,
    )
```

```python
import functools
import math

import jax
import jax.numpy as jnp
from jax import lax
from jax.experimental import pallas as pl
from jax.experimental.pallas import tpu as pltpu
from jax.sharding import PartitionSpec as P

HD = 128
TOK = 128
NEG = -1e30
RATE = math.log2(math.e) / math.sqrt(HD)
MIB = 2**20
VMEM = pl.BlockSpec(memory_space=pltpu.VMEM)
SMEM = pl.BlockSpec(memory_space=pltpu.SMEM)
WHOLE = pltpu.CompilerParams(vmem_limit_bytes=60 * MIB)
LOCAL = pltpu.CompilerParams(vmem_limit_bytes=24 * MIB)


def attend(q, k, v, bias):
    g = q.shape[0]
    scores = lax.dot_general(
        q.reshape(g * TOK, HD), k, (((1,), (1,)), ((), ())), preferred_element_type=jnp.float32
    )
    scores = scores.reshape(g, TOK, -1)
    if bias is not None:
        scores = scores + bias
    top = jnp.max(scores, axis=-1, keepdims=True)
    weights = jnp.exp2((scores - top) * RATE)
    total = jnp.sum(weights, axis=-1, keepdims=True)
    weights = weights.astype(jnp.bfloat16).reshape(g * TOK, -1)
    mixed = jnp.dot(weights, v, preferred_element_type=jnp.float32)
    return mixed.reshape(g, TOK, HD) / total


def student_head(pairs, first, sources, o_ref, o_at):
    (q_ref, q_at), (k_ref, k_at), (v_ref, v_at) = sources
    for i in pairs:
        width = (i + 2) * TOK
        block = lax.broadcasted_iota(jnp.int32, (2, 1, width), 2) // TOK
        own = lax.broadcasted_iota(jnp.int32, (2, 1, width), 0) + i
        bias = jnp.where((block == own) | (block >= first) & (block < own), 0.0, NEG)
        k = k_ref[0 : i + 2, k_at].reshape(width, HD)
        v = v_ref[0 : i + 2, v_at].reshape(width, HD)
        o_ref[i : i + 2, o_at] = attend(q_ref[i : i + 2, q_at], k, v, bias).astype(jnp.bfloat16)


def teacher_head(blocks, rows, clip_ref, sources, gen, o_ref, o_at):
    (q_ref, q_at), (k_ref, k_at) = sources
    reach = blocks // 2 + 1
    width = reach * TOK
    offset = lax.broadcasted_iota(jnp.int32, (1, 1, width), 2) // TOK
    for i in rows:
        low = clip_ref[0, i]
        high = clip_ref[1, i]
        start = jnp.minimum(low, blocks - reach)
        block = offset + start
        bias = jnp.where((block >= low) & (block < high), 0.0, NEG)
        k = k_ref[pl.ds(start, reach), k_at].reshape(width, HD)
        v = gen(pl.ds(start, reach)).reshape(width, HD)
        out = attend(q_ref[pl.ds(i, 1), q_at], k, v, bias)
        score = (out[0] - gen(i).astype(jnp.float32)).astype(jnp.bfloat16)
        if o_at is None:
            o_ref[1] = score
        else:
            o_ref[i, o_at] = score


def teacher_whole_head(blocks, clip_ref, sources, gen, o_ref, o_at):
    (q_ref, q_at), (k_ref, k_at) = sources
    reach = blocks // 2 + 1

    def put(at, out):
        score = out - gen(at).astype(jnp.float32)
        o_ref[at, o_at] = score.astype(jnp.bfloat16)

    large = clip_ref[2, 0]
    k = k_ref[pl.ds(large, reach), k_at].reshape(reach * TOK, HD)
    v = gen(pl.ds(large, reach)).reshape(reach * TOK, HD)
    for i in range(0, reach, 2):
        at = pl.ds(large + i, min(2, reach - i))
        put(at, attend(q_ref[at, q_at], k, v, None))
    span = blocks - reach - 1
    offset = lax.broadcasted_iota(jnp.int32, (1, 1, span * TOK), 2) // TOK
    for j in range(blocks - reach):
        i = jnp.where(j < large, j, j + reach)
        low, high = clip_ref[0, i], clip_ref[1, i]
        start = jnp.minimum(low, blocks - span)
        block = offset + start
        bias = jnp.where((block >= low) & (block < high), 0.0, NEG)
        k = k_ref[pl.ds(start, span), k_at].reshape(span * TOK, HD)
        v = gen(pl.ds(start, span)).reshape(span * TOK, HD)
        put(pl.ds(i, 1), attend(q_ref[pl.ds(i, 1), q_at], k, v, bias))


def cost(heads, blocks, units):
    return pl.CostEstimate(
        flops=heads * blocks * blocks * 4 * TOK * TOK * HD,
        bytes_accessed=units * blocks * TOK * HD * 2,
        transcendentals=heads * blocks * blocks * TOK * TOK,
    )


def pack(plan, ranges, tensors):
    peers, units = len(plan), len(plan[0])
    widths = [count * HD for _, count in ranges]
    starts = [sum(widths[:r]) for r in range(len(ranges))]

    def place(h):
        for r, (head, count) in enumerate(ranges):
            if head <= h < head + count:
                return r, starts[r] + (h - head) * HD

    need = []
    for u in range(units):
        need.append(list(dict.fromkeys((plan[p][u][0], place(plan[p][u][1])[0]) for p in range(peers))))
    order = sorted(range(units), key=lambda u: (len(need[u]), u))
    fetch = list(dict.fromkeys(piece for u in order for piece in need[u]))

    def body(*refs):
        o_ref, rows, tiles, in_sem, out_sem = refs[len(tensors) :]
        copies = {}
        for n, (t, r) in enumerate(fetch):
            source = refs[t].at[0, :, pl.ds(ranges[r][0] * HD, widths[r])]
            target = rows.at[t, :, pl.ds(starts[r], widths[r])]
            copies[t, r] = pltpu.make_async_copy(source, target, in_sem.at[n])
            copies[t, r].start()
        sent = []
        for u in order:
            for piece in need[u]:
                if piece in copies:
                    copies.pop(piece).wait()
            for p in range(peers):
                t, h = plan[p][u]
                at = place(h)[1]
                tiles[p, u] = rows[t, :, at : at + HD]
            sent.append(pltpu.make_async_copy(tiles.at[:, u], o_ref.at[:, u], out_sem.at[u]))
            sent[-1].start()
        for copy in sent:
            copy.wait()

    return pl.pallas_call(
        body,
        in_specs=[pl.BlockSpec(memory_space=pl.ANY)] * len(tensors),
        out_specs=pl.BlockSpec(memory_space=pl.ANY),
        out_shape=jax.ShapeDtypeStruct((peers, units, TOK, HD), jnp.bfloat16),
        scratch_shapes=[
            pltpu.VMEM((len(tensors), TOK, sum(widths)), jnp.bfloat16),
            pltpu.VMEM((peers, units, TOK, HD), jnp.bfloat16),
            pltpu.SemaphoreType.DMA((len(fetch),)),
            pltpu.SemaphoreType.DMA((units,)),
        ],
        compiler_params=WHOLE,
        cost_estimate=cost(0, peers, 2 * units),
    )(*tensors)


def unpack(places, back):
    def body(x_ref, *o_refs):
        for o_ref, place in zip(o_refs, places):
            for h, (p, u) in enumerate(place):
                o_ref[0, :, h * HD : (h + 1) * HD] = x_ref[p, u]

    width = len(places[0]) * HD
    return pl.pallas_call(
        body,
        out_shape=[jax.ShapeDtypeStruct((1, TOK, width), jnp.bfloat16) for _ in places],
        compiler_params=LOCAL,
        cost_estimate=cost(0, 1, 4 * len(places[0])),
    )(back)


def student_kernel(blocks, first, role, arrived):
    def body(first_ref, role_ref, x_ref, o_ref):
        @pl.when(role_ref[0] == 1)
        def _():
            sources = [(x_ref, t) for t in range(3)]
            student_head(range(0, blocks, 2), first_ref[0], sources, o_ref, 0)

    return pl.pallas_call(
        body,
        in_specs=[SMEM, SMEM, VMEM],
        out_specs=VMEM,
        out_shape=jax.ShapeDtypeStruct((blocks, 1, TOK, HD), jnp.bfloat16),
        compiler_params=LOCAL,
        cost_estimate=cost(1, blocks, 4),
    )(first, role, arrived)


def rest_teacher(blocks, clips, role, arrived, offset, gen, shared):
    def body(clip_ref, role_ref, x_ref, gen_ref, shared_ref, o_ref):
        @pl.when(role_ref[0] == 1)
        def _():
            o_ref[...] = gen_ref[...]

        @pl.when(role_ref[0] == 2)
        def _():
            sources = [(x_ref, offset + t) for t in range(2)]
            teacher_head(
                blocks, range(blocks), clip_ref, sources, lambda at: shared_ref[at, 0], o_ref, 0
            )

    return pl.pallas_call(
        body,
        in_specs=[SMEM, SMEM, VMEM, VMEM, VMEM],
        out_specs=VMEM,
        out_shape=jax.ShapeDtypeStruct((blocks, 1, TOK, HD), jnp.bfloat16),
        compiler_params=LOCAL,
        cost_estimate=cost(1, blocks, 5),
    )(clips, role, arrived, gen, shared)


def slots_kernel(full, order, home, first, clips, where, arrived, pieces):
    blocks = len(order)

    def body(first_ref, clip_ref, where_ref, *refs):
        x_refs, refs = refs[:blocks], refs[blocks:]
        piece_refs, refs = refs[: len(pieces)], refs[len(pieces) :]
        o_refs, (x, y) = refs[:blocks], refs[blocks:]
        at = [where_ref[2] ^ d for d in order]
        for i in range(blocks):
            x[at[i]] = x_refs[i][...]

        def head(s, carry):
            sources = [(x, 5 * s + t) for t in range(5)]
            student_head(range(0, blocks, 2), first_ref[0], sources[:3], y, 2 * s)
            gen = lambda at: y[at, 2 * s]
            teacher_whole_head(blocks, clip_ref, sources[3:], gen, y, 2 * s + 1)

        lax.fori_loop(0, full, head, None)
        for i, d in enumerate(home):
            o_refs[i][0 : 2 * full] = y[where_ref[2] ^ d]
            if d % 2 == 0:
                o_refs[i][2 * full : 2 * full + 2] = piece_refs[d // 2][...]

    return pl.pallas_call(
        body,
        in_specs=[SMEM] * 3 + [VMEM] * (blocks + len(pieces)),
        out_specs=[VMEM] * blocks,
        out_shape=[
            jax.ShapeDtypeStruct((2 * full + 2 * (d % 2 == 0), TOK, HD), jnp.bfloat16)
            for d in home
        ],
        scratch_shapes=[
            pltpu.VMEM((blocks, 5 * full, TOK, HD), jnp.bfloat16),
            pltpu.VMEM((blocks, 2 * full, TOK, HD), jnp.bfloat16),
        ],
        compiler_params=LOCAL,
        cost_estimate=cost(2 * full, blocks, 7 * full),
    )(first, clips, where, *arrived, *pieces)


def slots_pack(full, order, where, tensors):
    peers = len(order)

    def body(where_ref, *refs):
        o_refs, (rows, sems) = refs[5 : 5 + peers], refs[5 + peers :]
        copies = []
        for t in range(5):
            source = refs[t].at[0, :, pl.ds(0, full * peers * HD)]
            copies.append(pltpu.make_async_copy(source, rows.at[t], sems.at[t]))
            copies[-1].start()
        for t in range(5):
            copies[t].wait()
            for s in range(full):
                for i, d in enumerate(order):
                    at = pl.multiple_of((s * peers + (where_ref[2] ^ d)) * HD, HD)
                    o_refs[i][5 * s + t] = rows[t, :, pl.ds(at, HD)]

    return pl.pallas_call(
        body,
        in_specs=[SMEM] + [pl.BlockSpec(memory_space=pl.ANY)] * 5,
        out_specs=[VMEM] * peers,
        out_shape=[jax.ShapeDtypeStruct((5 * full, TOK, HD), jnp.bfloat16)] * peers,
        scratch_shapes=[
            pltpu.VMEM((5, TOK, full * peers * HD), jnp.bfloat16),
            pltpu.SemaphoreType.DMA((5,)),
        ],
        compiler_params=WHOLE,
        cost_estimate=cost(0, peers, 10 * full),
    )(where, *tensors)


def rest_pack(base, columns, column, tensors):
    def body(column_ref, *refs):
        rows, sems = refs[-2:]
        copies = []
        for t in range(5):
            source = refs[t].at[0, :, pl.ds(base * HD, columns * HD)]
            copies.append(pltpu.make_async_copy(source, rows.at[t], sems.at[t]))
            copies[-1].start()
        for t in range(5):
            copies[t].wait()
            for s in range(columns):
                at = pl.multiple_of((column_ref[0] ^ s) * HD, HD)
                refs[5 + s][t] = rows[t, :, pl.ds(at, HD)]

    return pl.pallas_call(
        body,
        in_specs=[SMEM] + [pl.BlockSpec(memory_space=pl.ANY)] * 5,
        out_specs=[VMEM] * columns,
        out_shape=[jax.ShapeDtypeStruct((5, TOK, HD), jnp.bfloat16)] * columns,
        scratch_shapes=[
            pltpu.VMEM((5, TOK, columns * HD), jnp.bfloat16),
            pltpu.SemaphoreType.DMA((5,)),
        ],
        compiler_params=WHOLE,
        cost_estimate=cost(0, 1, 10 * columns),
    )(column, *tensors)


def rest_kernel(columns, order, first, clips, where, own, other):
    blocks = 2 * columns

    def body(first_ref, clip_ref, where_ref, *refs):
        x, gen = refs[-2:]
        column, side = where_ref[0], where_ref[1]
        mine = [2 * (column ^ s) + side for s in range(columns)]
        for n, s in enumerate(order):
            x[mine[s]] = refs[n][...]
            x[mine[s] ^ 1] = refs[columns + n][...]
        sources = [(x, t) for t in range(5)]
        student_head(range(0, blocks, 2), first_ref[0], sources[:3], gen, 0)
        at_gen = lambda at: gen[at, 0]
        for s in range(columns):
            o_ref = refs[2 * columns + s]
            o_ref[0:1] = gen[mine[s]]
            teacher_head(blocks, [mine[s]], clip_ref, sources[3:], at_gen, o_ref, None)

    return pl.pallas_call(
        body,
        in_specs=[SMEM] * 3 + [VMEM] * (2 * columns),
        out_specs=[VMEM] * columns,
        out_shape=[jax.ShapeDtypeStruct((2, TOK, HD), jnp.bfloat16)] * columns,
        scratch_shapes=[
            pltpu.VMEM((blocks, 5, TOK, HD), jnp.bfloat16),
            pltpu.VMEM((blocks, 1, TOK, HD), jnp.bfloat16),
        ],
        compiler_params=LOCAL,
        cost_estimate=cost(0, 1, 1),
    )(first, clips, where, *own, *other)


def join(full, order, columns, where, slots):
    peers = len(order)

    def body(where_ref, *refs):
        for i, o_ref in enumerate(refs[peers:]):

            def put(h, tile):
                o_ref[0, :, pl.ds(pl.multiple_of(h * HD, HD), HD)] = tile

            for n, d in enumerate(order):
                for s in range(full):
                    put(s * peers + (where_ref[2] ^ d), refs[n][2 * s + i])
            for s in range(columns):
                ref = refs[order.index(2 * s)]
                put(full * peers + (where_ref[0] ^ s), ref[2 * full + i])

    width = (full * peers + columns) * HD
    return pl.pallas_call(
        body,
        in_specs=[SMEM] + [VMEM] * peers,
        out_specs=[VMEM] * 2,
        out_shape=[jax.ShapeDtypeStruct((1, TOK, width), jnp.bfloat16)] * 2,
        compiler_params=LOCAL,
        cost_estimate=cost(0, 1, 4 * width // HD),
    )(where, *slots)


def by_slots_and_columns(tensors, peers, full, rest, first, clips):
    here = lax.axis_index("tm")
    where = jnp.stack([here // 2, here % 2, here]).astype(jnp.int32)

    def swapped(x, by):
        return lax.ppermute(x, "tm", [(i, i ^ by) for i in range(peers)]) if by else x

    far = list(range(rest, peers))
    near = sorted(range(1, rest), key=lambda d: (d % 2, d))
    there = [far[0], near[0], far[1], *near[1:], *far[2:], 0]
    home = [far[0]] + [d for pair in zip(range(1, rest), far[1:]) for d in pair] + [0]
    across = [*range(rest // 2, rest), *range(1, rest // 2), 0]

    pieces = rest_pack(full * peers, rest, where[:1], tensors)
    own = [swapped(pieces[s], 2 * s) for s in across]
    packed = slots_pack(full, there, where, tensors)
    arrived = [swapped(x, d) for x, d in zip(packed, there)]
    other = [swapped(x, 1) for x in own]
    pieces = rest_kernel(rest, across, first, clips, where, own, other)
    arrived, pieces = lax.optimization_barrier((arrived, pieces))
    results = slots_kernel(full, there, home, first, clips, where, arrived, pieces)
    slots = [swapped(x, d) for x, d in zip(results, home)]
    return tuple(join(full, home, rest, where, slots))


def by_roles(tensors, peers, heads, first, clips):
    here = lax.axis_index("tm")
    role = jnp.where(here < 2 * heads, 1 + here % 2, 0).astype(jnp.int32)[None]
    plan = [
        [(t, min(p // 2, heads - 1)) for t in ((3, 4, 4) if p % 2 else (0, 1, 2))]
        for p in range(peers)
    ]
    arrived = lax.all_to_all(pack(plan, [(0, heads)], tensors), "tm", 0, 0)
    gen = student_kernel(peers, first, role, arrived)
    shared = lax.ppermute(gen, "tm", [(2 * r, 2 * r + 1) for r in range(heads)])
    results = rest_teacher(peers, clips, role, arrived, 0, gen, shared)
    back = lax.all_to_all(results, "tm", 0, 0)
    return tuple(unpack([[(2 * r + i, 0) for r in range(heads)] for i in (0, 1)], back))


def per_device(student_q, student_k, student_v, teacher_q, teacher_k, stagger, clip_lengths):
    heads = student_q.shape[2] // HD
    peers = lax.axis_size("tm")
    full, rest = divmod(heads, peers)
    running = jnp.cumsum(clip_lengths[0])
    block = jnp.arange(peers, dtype=jnp.int32)
    before = running[None, :] <= block[:, None]
    low = jnp.max(jnp.where(before, running[None, :], 0), axis=1)
    high = jnp.min(jnp.where(before, peers, running[None, :]), axis=1)
    large = jnp.where(clip_lengths[0] == peers // 2 + 1, running - clip_lengths[0], 0)
    large = jnp.broadcast_to(jnp.max(large), (peers,))
    clips = jnp.stack([low, high, large]).astype(jnp.int32)
    tensors = (student_q, student_k, student_v, teacher_q, teacher_k)
    if full == 0:
        assert 2 * rest <= peers
        return by_roles(tensors, peers, rest, stagger, clips)
    assert peers == 2 * rest and rest & (rest - 1) == 0
    return by_slots_and_columns(tensors, peers, full, rest, stagger, clips)


def solution(mesh):
    spec = P("seq", "tm", "mp")
    return jax.shard_map(
        per_device,
        mesh=mesh,
        in_specs=(spec,) * 5 + (P("seq"), P("seq", None)),
        out_specs=(spec, spec),
        check_vma=False,
    )
```

```python
import functools
import math

import jax
import jax.numpy as jnp
from jax import lax
from jax.experimental import pallas as pl
from jax.experimental.pallas import tpu as pltpu
from jax.sharding import PartitionSpec as P

HD = 128
TOK = 128
NEG = -1e30
RATE = math.log2(math.e) / math.sqrt(HD)
MIB = 2**20
VMEM = pl.BlockSpec(memory_space=pltpu.VMEM)
SMEM = pl.BlockSpec(memory_space=pltpu.SMEM)
WHOLE = pltpu.CompilerParams(vmem_limit_bytes=60 * MIB)
LOCAL = pltpu.CompilerParams(vmem_limit_bytes=24 * MIB)


def attend(q, k, v, bias):
    g = q.shape[0]
    scores = lax.dot_general(
        q.reshape(g * TOK, HD), k, (((1,), (1,)), ((), ())), preferred_element_type=jnp.float32
    )
    scores = scores.reshape(g, TOK, -1)
    if bias is not None:
        scores = scores + bias
    top = jnp.max(scores, axis=-1, keepdims=True)
    weights = jnp.exp2((scores - top) * RATE)
    total = jnp.sum(weights, axis=-1, keepdims=True)
    weights = weights.astype(jnp.bfloat16).reshape(g * TOK, -1)
    mixed = jnp.dot(weights, v, preferred_element_type=jnp.float32)
    return mixed.reshape(g, TOK, HD) / total


def student_head(pairs, first, sources, o_ref, o_at):
    (q_ref, q_at), (k_ref, k_at), (v_ref, v_at) = sources
    for i in pairs:
        width = (i + 2) * TOK
        block = lax.broadcasted_iota(jnp.int32, (2, 1, width), 2) // TOK
        own = lax.broadcasted_iota(jnp.int32, (2, 1, width), 0) + i
        bias = jnp.where((block == own) | (block >= first) & (block < own), 0.0, NEG)
        k = k_ref[0 : i + 2, k_at].reshape(width, HD)
        v = v_ref[0 : i + 2, v_at].reshape(width, HD)
        o_ref[i : i + 2, o_at] = attend(q_ref[i : i + 2, q_at], k, v, bias).astype(jnp.bfloat16)


def teacher_head(blocks, rows, clip_ref, sources, gen, o_ref, o_at):
    (q_ref, q_at), (k_ref, k_at) = sources
    reach = blocks // 2 + 1
    width = reach * TOK
    offset = lax.broadcasted_iota(jnp.int32, (1, 1, width), 2) // TOK
    for i in rows:
        low = clip_ref[0, i]
        high = clip_ref[1, i]
        start = jnp.minimum(low, blocks - reach)
        block = offset + start
        bias = jnp.where((block >= low) & (block < high), 0.0, NEG)
        k = k_ref[pl.ds(start, reach), k_at].reshape(width, HD)
        v = gen(pl.ds(start, reach)).reshape(width, HD)
        out = attend(q_ref[pl.ds(i, 1), q_at], k, v, bias)
        score = (out[0] - gen(i).astype(jnp.float32)).astype(jnp.bfloat16)
        if o_at is None:
            o_ref[1] = score
        else:
            o_ref[i, o_at] = score


def teacher_whole_head(blocks, clip_ref, sources, gen, o_ref, o_at):
    (q_ref, q_at), (k_ref, k_at) = sources
    reach = blocks // 2 + 1

    def put(at, out):
        score = out - gen(at).astype(jnp.float32)
        o_ref[at, o_at] = score.astype(jnp.bfloat16)

    large = clip_ref[2, 0]
    k = k_ref[pl.ds(large, reach), k_at].reshape(reach * TOK, HD)
    v = gen(pl.ds(large, reach)).reshape(reach * TOK, HD)
    for i in range(0, reach, 2):
        at = pl.ds(large + i, min(2, reach - i))
        put(at, attend(q_ref[at, q_at], k, v, None))
    span = blocks - reach - 1
    offset = lax.broadcasted_iota(jnp.int32, (1, 1, span * TOK), 2) // TOK
    for j in range(blocks - reach):
        i = jnp.where(j < large, j, j + reach)
        low, high = clip_ref[0, i], clip_ref[1, i]
        start = jnp.minimum(low, blocks - span)
        block = offset + start
        bias = jnp.where((block >= low) & (block < high), 0.0, NEG)
        k = k_ref[pl.ds(start, span), k_at].reshape(span * TOK, HD)
        v = gen(pl.ds(start, span)).reshape(span * TOK, HD)
        put(pl.ds(i, 1), attend(q_ref[pl.ds(i, 1), q_at], k, v, bias))


def cost(heads, blocks, units):
    return pl.CostEstimate(
        flops=heads * blocks * blocks * 4 * TOK * TOK * HD,
        bytes_accessed=units * blocks * TOK * HD * 2,
        transcendentals=heads * blocks * blocks * TOK * TOK,
    )


def pack(plan, ranges, tensors):
    peers, units = len(plan), len(plan[0])
    widths = [count * HD for _, count in ranges]
    starts = [sum(widths[:r]) for r in range(len(ranges))]

    def place(h):
        for r, (head, count) in enumerate(ranges):
            if head <= h < head + count:
                return r, starts[r] + (h - head) * HD

    need = []
    for u in range(units):
        need.append(list(dict.fromkeys((plan[p][u][0], place(plan[p][u][1])[0]) for p in range(peers))))
    order = sorted(range(units), key=lambda u: (len(need[u]), u))
    fetch = list(dict.fromkeys(piece for u in order for piece in need[u]))

    def body(*refs):
        o_ref, rows, tiles, in_sem, out_sem = refs[len(tensors) :]
        copies = {}
        for n, (t, r) in enumerate(fetch):
            source = refs[t].at[0, :, pl.ds(ranges[r][0] * HD, widths[r])]
            target = rows.at[t, :, pl.ds(starts[r], widths[r])]
            copies[t, r] = pltpu.make_async_copy(source, target, in_sem.at[n])
            copies[t, r].start()
        sent = []
        for u in order:
            for piece in need[u]:
                if piece in copies:
                    copies.pop(piece).wait()
            for p in range(peers):
                t, h = plan[p][u]
                at = place(h)[1]
                tiles[p, u] = rows[t, :, at : at + HD]
            sent.append(pltpu.make_async_copy(tiles.at[:, u], o_ref.at[:, u], out_sem.at[u]))
            sent[-1].start()
        for copy in sent:
            copy.wait()

    return pl.pallas_call(
        body,
        in_specs=[pl.BlockSpec(memory_space=pl.ANY)] * len(tensors),
        out_specs=pl.BlockSpec(memory_space=pl.ANY),
        out_shape=jax.ShapeDtypeStruct((peers, units, TOK, HD), jnp.bfloat16),
        scratch_shapes=[
            pltpu.VMEM((len(tensors), TOK, sum(widths)), jnp.bfloat16),
            pltpu.VMEM((peers, units, TOK, HD), jnp.bfloat16),
            pltpu.SemaphoreType.DMA((len(fetch),)),
            pltpu.SemaphoreType.DMA((units,)),
        ],
        compiler_params=WHOLE,
        cost_estimate=cost(0, peers, 2 * units),
    )(*tensors)


def unpack(places, back):
    def body(x_ref, *o_refs):
        for o_ref, place in zip(o_refs, places):
            for h, (p, u) in enumerate(place):
                o_ref[0, :, h * HD : (h + 1) * HD] = x_ref[p, u]

    width = len(places[0]) * HD
    return pl.pallas_call(
        body,
        out_shape=[jax.ShapeDtypeStruct((1, TOK, width), jnp.bfloat16) for _ in places],
        compiler_params=LOCAL,
        cost_estimate=cost(0, 1, 4 * len(places[0])),
    )(back)


def student_kernel(blocks, first, role, arrived):
    def body(first_ref, role_ref, x_ref, o_ref):
        @pl.when(role_ref[0] == 1)
        def _():
            sources = [(x_ref, t) for t in range(3)]
            student_head(range(0, blocks, 2), first_ref[0], sources, o_ref, 0)

    return pl.pallas_call(
        body,
        in_specs=[SMEM, SMEM, VMEM],
        out_specs=VMEM,
        out_shape=jax.ShapeDtypeStruct((blocks, 1, TOK, HD), jnp.bfloat16),
        compiler_params=LOCAL,
        cost_estimate=cost(1, blocks, 4),
    )(first, role, arrived)


def rest_teacher(blocks, clips, role, arrived, offset, gen, shared):
    def body(clip_ref, role_ref, x_ref, gen_ref, shared_ref, o_ref):
        @pl.when(role_ref[0] == 1)
        def _():
            o_ref[...] = gen_ref[...]

        @pl.when(role_ref[0] == 2)
        def _():
            sources = [(x_ref, offset + t) for t in range(2)]
            teacher_head(
                blocks, range(blocks), clip_ref, sources, lambda at: shared_ref[at, 0], o_ref, 0
            )

    return pl.pallas_call(
        body,
        in_specs=[SMEM, SMEM, VMEM, VMEM, VMEM],
        out_specs=VMEM,
        out_shape=jax.ShapeDtypeStruct((blocks, 1, TOK, HD), jnp.bfloat16),
        compiler_params=LOCAL,
        cost_estimate=cost(1, blocks, 5),
    )(clips, role, arrived, gen, shared)


def slots_kernel(full, order, home, first, clips, where, arrived, pieces):
    blocks = len(order)

    def body(first_ref, clip_ref, where_ref, *refs):
        x_refs, refs = refs[:blocks], refs[blocks:]
        piece_refs, refs = refs[: len(pieces)], refs[len(pieces) :]
        o_refs, (x, y) = refs[:blocks], refs[blocks:]
        at = [where_ref[2] ^ d for d in order]
        for i in range(blocks):
            x[at[i]] = x_refs[i][...]

        def head(s, carry):
            sources = [(x, 5 * s + t) for t in range(5)]
            student_head(range(0, blocks, 2), first_ref[0], sources[:3], y, 2 * s)
            gen = lambda at: y[at, 2 * s]
            teacher_whole_head(blocks, clip_ref, sources[3:], gen, y, 2 * s + 1)

        lax.fori_loop(0, full, head, None)
        for i, d in enumerate(home):
            o_refs[i][0 : 2 * full] = y[where_ref[2] ^ d]
            if d % 2 == 0:
                o_refs[i][2 * full : 2 * full + 2] = piece_refs[d // 2][...]

    return pl.pallas_call(
        body,
        in_specs=[SMEM] * 3 + [VMEM] * (blocks + len(pieces)),
        out_specs=[VMEM] * blocks,
        out_shape=[
            jax.ShapeDtypeStruct((2 * full + 2 * (d % 2 == 0), TOK, HD), jnp.bfloat16)
            for d in home
        ],
        scratch_shapes=[
            pltpu.VMEM((blocks, 5 * full, TOK, HD), jnp.bfloat16),
            pltpu.VMEM((blocks, 2 * full, TOK, HD), jnp.bfloat16),
        ],
        compiler_params=LOCAL,
        cost_estimate=cost(2 * full, blocks, 7 * full),
    )(first, clips, where, *arrived, *pieces)


def slots_pack(full, order, where, tensors):
    peers = len(order)

    def body(where_ref, *refs):
        o_refs, (rows, sems) = refs[5 : 5 + peers], refs[5 + peers :]
        copies = []
        for t in range(5):
            source = refs[t].at[0, :, pl.ds(0, full * peers * HD)]
            copies.append(pltpu.make_async_copy(source, rows.at[t], sems.at[t]))
            copies[-1].start()
        for t in range(5):
            copies[t].wait()
            for s in range(full):
                for i, d in enumerate(order):
                    at = pl.multiple_of((s * peers + (where_ref[2] ^ d)) * HD, HD)
                    o_refs[i][5 * s + t] = rows[t, :, pl.ds(at, HD)]

    return pl.pallas_call(
        body,
        in_specs=[SMEM] + [pl.BlockSpec(memory_space=pl.ANY)] * 5,
        out_specs=[VMEM] * peers,
        out_shape=[jax.ShapeDtypeStruct((5 * full, TOK, HD), jnp.bfloat16)] * peers,
        scratch_shapes=[
            pltpu.VMEM((5, TOK, full * peers * HD), jnp.bfloat16),
            pltpu.SemaphoreType.DMA((5,)),
        ],
        compiler_params=WHOLE,
        cost_estimate=cost(0, peers, 10 * full),
    )(where, *tensors)


def rest_pack(base, columns, column, tensors):
    def body(column_ref, *refs):
        rows, sems = refs[-2:]
        copies = []
        for t in range(5):
            source = refs[t].at[0, :, pl.ds(base * HD, columns * HD)]
            copies.append(pltpu.make_async_copy(source, rows.at[t], sems.at[t]))
            copies[-1].start()
        for t in range(5):
            copies[t].wait()
            for s in range(columns):
                at = pl.multiple_of((column_ref[0] ^ s) * HD, HD)
                refs[5 + s][t] = rows[t, :, pl.ds(at, HD)]

    return pl.pallas_call(
        body,
        in_specs=[SMEM] + [pl.BlockSpec(memory_space=pl.ANY)] * 5,
        out_specs=[VMEM] * columns,
        out_shape=[jax.ShapeDtypeStruct((5, TOK, HD), jnp.bfloat16)] * columns,
        scratch_shapes=[
            pltpu.VMEM((5, TOK, columns * HD), jnp.bfloat16),
            pltpu.SemaphoreType.DMA((5,)),
        ],
        compiler_params=WHOLE,
        cost_estimate=cost(0, 1, 10 * columns),
    )(column, *tensors)


def rest_kernel(columns, order, first, clips, where, own, other):
    blocks = 2 * columns

    def body(first_ref, clip_ref, where_ref, *refs):
        x, gen = refs[-2:]
        column, side = where_ref[0], where_ref[1]
        mine = [2 * (column ^ s) + side for s in range(columns)]
        for n, s in enumerate(order):
            x[mine[s]] = refs[n][...]
            x[mine[s] ^ 1] = refs[columns + n][...]
        sources = [(x, t) for t in range(5)]
        student_head(range(0, blocks, 2), first_ref[0], sources[:3], gen, 0)
        at_gen = lambda at: gen[at, 0]
        for s in range(columns):
            o_ref = refs[2 * columns + s]
            o_ref[0:1] = gen[mine[s]]
            teacher_head(blocks, [mine[s]], clip_ref, sources[3:], at_gen, o_ref, None)

    return pl.pallas_call(
        body,
        in_specs=[SMEM] * 3 + [VMEM] * (2 * columns),
        out_specs=[VMEM] * columns,
        out_shape=[jax.ShapeDtypeStruct((2, TOK, HD), jnp.bfloat16)] * columns,
        scratch_shapes=[
            pltpu.VMEM((blocks, 5, TOK, HD), jnp.bfloat16),
            pltpu.VMEM((blocks, 1, TOK, HD), jnp.bfloat16),
        ],
        compiler_params=LOCAL,
        cost_estimate=cost(0, 1, 1),
    )(first, clips, where, *own, *other)


def join(full, order, columns, where, slots):
    peers = len(order)

    def body(where_ref, *refs):
        for i, o_ref in enumerate(refs[peers:]):

            def put(h, tile):
                o_ref[0, :, pl.ds(pl.multiple_of(h * HD, HD), HD)] = tile

            for n, d in enumerate(order):
                for s in range(full):
                    put(s * peers + (where_ref[2] ^ d), refs[n][2 * s + i])
            for s in range(columns):
                ref = refs[order.index(2 * s)]
                put(full * peers + (where_ref[0] ^ s), ref[2 * full + i])

    width = (full * peers + columns) * HD
    return pl.pallas_call(
        body,
        in_specs=[SMEM] + [VMEM] * peers,
        out_specs=[VMEM] * 2,
        out_shape=[jax.ShapeDtypeStruct((1, TOK, width), jnp.bfloat16)] * 2,
        compiler_params=LOCAL,
        cost_estimate=cost(0, 1, 4 * width // HD),
    )(where, *slots)


def by_slots_and_columns(tensors, peers, full, rest, first, clips):
    here = lax.axis_index("tm")
    where = jnp.stack([here // 2, here % 2, here]).astype(jnp.int32)

    def swapped(x, by):
        return lax.ppermute(x, "tm", [(i, i ^ by) for i in range(peers)]) if by else x

    far = list(range(rest, peers))
    near = sorted(range(1, rest), key=lambda d: (d % 2, d))
    there = [far[0]] + [d for pair in zip(far[1:], near) for d in pair] + [0]
    home = [far[0]] + [d for pair in zip(range(1, rest), far[1:]) for d in pair] + [0]
    across = [*range(rest // 2, rest), *range(1, rest // 2), 0]

    pieces = rest_pack(full * peers, rest, where[:1], tensors)
    own = [swapped(pieces[s], 2 * s) for s in across]
    packed = slots_pack(full, there, where, tensors)
    arrived = [swapped(x, d) for x, d in zip(packed, there)]
    other = [swapped(x, 1) for x in own]
    pieces = rest_kernel(rest, across, first, clips, where, own, other)
    arrived, pieces = lax.optimization_barrier((arrived, pieces))
    results = slots_kernel(full, there, home, first, clips, where, arrived, pieces)
    slots = [swapped(x, d) for x, d in zip(results, home)]
    return tuple(join(full, home, rest, where, slots))


def by_roles(tensors, peers, heads, first, clips):
    here = lax.axis_index("tm")
    role = jnp.where(here < 2 * heads, 1 + here % 2, 0).astype(jnp.int32)[None]
    plan = [
        [(t, min(p // 2, heads - 1)) for t in ((3, 4, 4) if p % 2 else (0, 1, 2))]
        for p in range(peers)
    ]
    arrived = lax.all_to_all(pack(plan, [(0, heads)], tensors), "tm", 0, 0)
    gen = student_kernel(peers, first, role, arrived)
    shared = lax.ppermute(gen, "tm", [(2 * r, 2 * r + 1) for r in range(heads)])
    results = rest_teacher(peers, clips, role, arrived, 0, gen, shared)
    back = lax.all_to_all(results, "tm", 0, 0)
    return tuple(unpack([[(2 * r + i, 0) for r in range(heads)] for i in (0, 1)], back))


def per_device(student_q, student_k, student_v, teacher_q, teacher_k, stagger, clip_lengths):
    heads = student_q.shape[2] // HD
    peers = lax.axis_size("tm")
    full, rest = divmod(heads, peers)
    running = jnp.cumsum(clip_lengths[0])
    block = jnp.arange(peers, dtype=jnp.int32)
    before = running[None, :] <= block[:, None]
    low = jnp.max(jnp.where(before, running[None, :], 0), axis=1)
    high = jnp.min(jnp.where(before, peers, running[None, :]), axis=1)
    large = jnp.where(clip_lengths[0] == peers // 2 + 1, running - clip_lengths[0], 0)
    large = jnp.broadcast_to(jnp.max(large), (peers,))
    clips = jnp.stack([low, high, large]).astype(jnp.int32)
    tensors = (student_q, student_k, student_v, teacher_q, teacher_k)
    if full == 0:
        assert 2 * rest <= peers
        return by_roles(tensors, peers, rest, stagger, clips)
    assert peers == 2 * rest and rest & (rest - 1) == 0
    return by_slots_and_columns(tensors, peers, full, rest, stagger, clips)


def solution(mesh):
    spec = P("seq", "tm", "mp")
    return jax.shard_map(
        per_device,
        mesh=mesh,
        in_specs=(spec,) * 5 + (P("seq"), P("seq", None)),
        out_specs=(spec, spec),
        check_vma=False,
    )
```

```python
import functools
import math

import jax
import jax.numpy as jnp
from jax import lax
from jax.experimental import pallas as pl
from jax.experimental.pallas import tpu as pltpu
from jax.sharding import PartitionSpec as P

HD = 128
TOK = 128
NEG = -1e30
RATE = math.log2(math.e) / math.sqrt(HD)
MIB = 2**20
VMEM = pl.BlockSpec(memory_space=pltpu.VMEM)
SMEM = pl.BlockSpec(memory_space=pltpu.SMEM)
WHOLE = pltpu.CompilerParams(vmem_limit_bytes=60 * MIB)
LOCAL = pltpu.CompilerParams(vmem_limit_bytes=24 * MIB)


def attend(q, k, v, bias):
    g = q.shape[0]
    scores = lax.dot_general(
        q.reshape(g * TOK, HD), k, (((1,), (1,)), ((), ())), preferred_element_type=jnp.float32
    )
    scores = scores.reshape(g, TOK, -1)
    if bias is not None:
        scores = scores + bias
    top = jnp.max(scores, axis=-1, keepdims=True)
    weights = jnp.exp2((scores - top) * RATE)
    total = jnp.sum(weights, axis=-1, keepdims=True)
    weights = weights.astype(jnp.bfloat16).reshape(g * TOK, -1)
    mixed = jnp.dot(weights, v, preferred_element_type=jnp.float32)
    return mixed.reshape(g, TOK, HD) / total


def student_head(pairs, first, sources, o_ref, o_at):
    (q_ref, q_at), (k_ref, k_at), (v_ref, v_at) = sources
    for i in pairs:
        width = (i + 2) * TOK
        block = lax.broadcasted_iota(jnp.int32, (2, 1, width), 2) // TOK
        own = lax.broadcasted_iota(jnp.int32, (2, 1, width), 0) + i
        bias = jnp.where((block == own) | (block >= first) & (block < own), 0.0, NEG)
        k = k_ref[0 : i + 2, k_at].reshape(width, HD)
        v = v_ref[0 : i + 2, v_at].reshape(width, HD)
        o_ref[i : i + 2, o_at] = attend(q_ref[i : i + 2, q_at], k, v, bias).astype(jnp.bfloat16)


def teacher_head(blocks, rows, clip_ref, sources, gen, o_ref, o_at):
    (q_ref, q_at), (k_ref, k_at) = sources
    reach = blocks // 2 + 1
    width = reach * TOK
    offset = lax.broadcasted_iota(jnp.int32, (1, 1, width), 2) // TOK
    for i in rows:
        low = clip_ref[0, i]
        high = clip_ref[1, i]
        start = jnp.minimum(low, blocks - reach)
        block = offset + start
        bias = jnp.where((block >= low) & (block < high), 0.0, NEG)
        k = k_ref[pl.ds(start, reach), k_at].reshape(width, HD)
        v = gen(pl.ds(start, reach)).reshape(width, HD)
        out = attend(q_ref[pl.ds(i, 1), q_at], k, v, bias)
        score = (out[0] - gen(i).astype(jnp.float32)).astype(jnp.bfloat16)
        if o_at is None:
            o_ref[1] = score
        else:
            o_ref[i, o_at] = score


def teacher_whole_head(blocks, clip_ref, sources, gen, o_ref, o_at):
    (q_ref, q_at), (k_ref, k_at) = sources
    reach = blocks // 2 + 1

    def put(at, out):
        score = out - gen(at).astype(jnp.float32)
        o_ref[at, o_at] = score.astype(jnp.bfloat16)

    large = clip_ref[2, 0]
    k = k_ref[pl.ds(large, reach), k_at].reshape(reach * TOK, HD)
    v = gen(pl.ds(large, reach)).reshape(reach * TOK, HD)
    for i in range(0, reach, 2):
        at = pl.ds(large + i, min(2, reach - i))
        put(at, attend(q_ref[at, q_at], k, v, None))
    span = blocks - reach - 1
    offset = lax.broadcasted_iota(jnp.int32, (1, 1, span * TOK), 2) // TOK
    for j in range(blocks - reach):
        i = jnp.where(j < large, j, j + reach)
        low, high = clip_ref[0, i], clip_ref[1, i]
        start = jnp.minimum(low, blocks - span)
        block = offset + start
        bias = jnp.where((block >= low) & (block < high), 0.0, NEG)
        k = k_ref[pl.ds(start, span), k_at].reshape(span * TOK, HD)
        v = gen(pl.ds(start, span)).reshape(span * TOK, HD)
        put(pl.ds(i, 1), attend(q_ref[pl.ds(i, 1), q_at], k, v, bias))


def cost(heads, blocks, units):
    return pl.CostEstimate(
        flops=heads * blocks * blocks * 4 * TOK * TOK * HD,
        bytes_accessed=units * blocks * TOK * HD * 2,
        transcendentals=heads * blocks * blocks * TOK * TOK,
    )


def pack(plan, ranges, tensors):
    peers, units = len(plan), len(plan[0])
    widths = [count * HD for _, count in ranges]
    starts = [sum(widths[:r]) for r in range(len(ranges))]

    def place(h):
        for r, (head, count) in enumerate(ranges):
            if head <= h < head + count:
                return r, starts[r] + (h - head) * HD

    need = []
    for u in range(units):
        need.append(list(dict.fromkeys((plan[p][u][0], place(plan[p][u][1])[0]) for p in range(peers))))
    order = sorted(range(units), key=lambda u: (len(need[u]), u))
    fetch = list(dict.fromkeys(piece for u in order for piece in need[u]))

    def body(*refs):
        o_ref, rows, tiles, in_sem, out_sem = refs[len(tensors) :]
        copies = {}
        for n, (t, r) in enumerate(fetch):
            source = refs[t].at[0, :, pl.ds(ranges[r][0] * HD, widths[r])]
            target = rows.at[t, :, pl.ds(starts[r], widths[r])]
            copies[t, r] = pltpu.make_async_copy(source, target, in_sem.at[n])
            copies[t, r].start()
        sent = []
        for u in order:
            for piece in need[u]:
                if piece in copies:
                    copies.pop(piece).wait()
            for p in range(peers):
                t, h = plan[p][u]
                at = place(h)[1]
                tiles[p, u] = rows[t, :, at : at + HD]
            sent.append(pltpu.make_async_copy(tiles.at[:, u], o_ref.at[:, u], out_sem.at[u]))
            sent[-1].start()
        for copy in sent:
            copy.wait()

    return pl.pallas_call(
        body,
        in_specs=[pl.BlockSpec(memory_space=pl.ANY)] * len(tensors),
        out_specs=pl.BlockSpec(memory_space=pl.ANY),
        out_shape=jax.ShapeDtypeStruct((peers, units, TOK, HD), jnp.bfloat16),
        scratch_shapes=[
            pltpu.VMEM((len(tensors), TOK, sum(widths)), jnp.bfloat16),
            pltpu.VMEM((peers, units, TOK, HD), jnp.bfloat16),
            pltpu.SemaphoreType.DMA((len(fetch),)),
            pltpu.SemaphoreType.DMA((units,)),
        ],
        compiler_params=WHOLE,
        cost_estimate=cost(0, peers, 2 * units),
    )(*tensors)


def unpack(places, back):
    def body(x_ref, *o_refs):
        for o_ref, place in zip(o_refs, places):
            for h, (p, u) in enumerate(place):
                o_ref[0, :, h * HD : (h + 1) * HD] = x_ref[p, u]

    width = len(places[0]) * HD
    return pl.pallas_call(
        body,
        out_shape=[jax.ShapeDtypeStruct((1, TOK, width), jnp.bfloat16) for _ in places],
        compiler_params=LOCAL,
        cost_estimate=cost(0, 1, 4 * len(places[0])),
    )(back)


def student_kernel(blocks, first, role, arrived):
    def body(first_ref, role_ref, x_ref, o_ref):
        @pl.when(role_ref[0] == 1)
        def _():
            sources = [(x_ref, t) for t in range(3)]
            student_head(range(0, blocks, 2), first_ref[0], sources, o_ref, 0)

    return pl.pallas_call(
        body,
        in_specs=[SMEM, SMEM, VMEM],
        out_specs=VMEM,
        out_shape=jax.ShapeDtypeStruct((blocks, 1, TOK, HD), jnp.bfloat16),
        compiler_params=LOCAL,
        cost_estimate=cost(1, blocks, 4),
    )(first, role, arrived)


def rest_teacher(blocks, clips, role, arrived, offset, gen, shared):
    def body(clip_ref, role_ref, x_ref, gen_ref, shared_ref, o_ref):
        @pl.when(role_ref[0] == 1)
        def _():
            o_ref[...] = gen_ref[...]

        @pl.when(role_ref[0] == 2)
        def _():
            sources = [(x_ref, offset + t) for t in range(2)]
            teacher_head(
                blocks, range(blocks), clip_ref, sources, lambda at: shared_ref[at, 0], o_ref, 0
            )

    return pl.pallas_call(
        body,
        in_specs=[SMEM, SMEM, VMEM, VMEM, VMEM],
        out_specs=VMEM,
        out_shape=jax.ShapeDtypeStruct((blocks, 1, TOK, HD), jnp.bfloat16),
        compiler_params=LOCAL,
        cost_estimate=cost(1, blocks, 5),
    )(clips, role, arrived, gen, shared)


def slot_kernel(order, home, first, clips, where, arrived, pieces):
    blocks = len(order)

    def body(first_ref, clip_ref, where_ref, *refs):
        x_refs, refs = refs[:blocks], refs[blocks:]
        piece_refs, refs = refs[: len(pieces)], refs[len(pieces) :]
        o_refs, (x, y) = refs[:blocks], refs[blocks:]
        at = [where_ref[2] ^ d for d in order]
        for i in range(blocks):
            x[at[i]] = x_refs[i][...]

        sources = [(x, t) for t in range(5)]
        student_head(range(0, blocks, 2), first_ref[0], sources[:3], y, 0)
        gen = lambda at: y[at, 0]
        teacher_whole_head(blocks, clip_ref, sources[3:], gen, y, 1)
        for i, d in enumerate(home):
            o_refs[i][0:2] = y[where_ref[2] ^ d]
            if pieces and d % 2 == 0:
                o_refs[i][2:4] = piece_refs[d // 2][...]

    return pl.pallas_call(
        body,
        in_specs=[SMEM] * 3 + [VMEM] * (blocks + len(pieces)),
        out_specs=[VMEM] * blocks,
        out_shape=[
            jax.ShapeDtypeStruct((4 if pieces and d % 2 == 0 else 2, TOK, HD), jnp.bfloat16)
            for d in home
        ],
        scratch_shapes=[
            pltpu.VMEM((blocks, 5, TOK, HD), jnp.bfloat16),
            pltpu.VMEM((blocks, 2, TOK, HD), jnp.bfloat16),
        ],
        compiler_params=LOCAL,
        cost_estimate=cost(2, blocks, 7),
    )(first, clips, where, *arrived, *pieces)


def slots_pack(full, order, where, tensors):
    peers = len(order)

    def body(where_ref, *refs):
        o_refs, (rows, sems) = refs[5 : 5 + full * peers], refs[5 + full * peers :]
        copies = []
        for t in range(5):
            source = refs[t].at[0, :, pl.ds(0, full * peers * HD)]
            copies.append(pltpu.make_async_copy(source, rows.at[t], sems.at[t]))
            copies[-1].start()
        for t in range(5):
            copies[t].wait()
            for s in range(full):
                for i, d in enumerate(order):
                    at = pl.multiple_of((s * peers + (where_ref[2] ^ d)) * HD, HD)
                    o_refs[s * peers + i][t] = rows[t, :, pl.ds(at, HD)]

    packed = pl.pallas_call(
        body,
        in_specs=[SMEM] + [pl.BlockSpec(memory_space=pl.ANY)] * 5,
        out_specs=[VMEM] * (full * peers),
        out_shape=[jax.ShapeDtypeStruct((5, TOK, HD), jnp.bfloat16)] * (full * peers),
        scratch_shapes=[
            pltpu.VMEM((5, TOK, full * peers * HD), jnp.bfloat16),
            pltpu.SemaphoreType.DMA((5,)),
        ],
        compiler_params=WHOLE,
        cost_estimate=cost(0, peers, 10 * full),
    )(where, *tensors)
    return [packed[s * peers : (s + 1) * peers] for s in range(full)]


def rest_pack(base, columns, column, tensors):
    def body(column_ref, *refs):
        rows, sems = refs[-2:]
        copies = []
        for t in range(5):
            source = refs[t].at[0, :, pl.ds(base * HD, columns * HD)]
            copies.append(pltpu.make_async_copy(source, rows.at[t], sems.at[t]))
            copies[-1].start()
        for t in range(5):
            copies[t].wait()
            for s in range(columns):
                at = pl.multiple_of((column_ref[0] ^ s) * HD, HD)
                refs[5 + s][t] = rows[t, :, pl.ds(at, HD)]

    return pl.pallas_call(
        body,
        in_specs=[SMEM] + [pl.BlockSpec(memory_space=pl.ANY)] * 5,
        out_specs=[VMEM] * columns,
        out_shape=[jax.ShapeDtypeStruct((5, TOK, HD), jnp.bfloat16)] * columns,
        scratch_shapes=[
            pltpu.VMEM((5, TOK, columns * HD), jnp.bfloat16),
            pltpu.SemaphoreType.DMA((5,)),
        ],
        compiler_params=WHOLE,
        cost_estimate=cost(0, 1, 10 * columns),
    )(column, *tensors)


def rest_kernel(columns, order, first, clips, where, own, other):
    blocks = 2 * columns

    def body(first_ref, clip_ref, where_ref, *refs):
        x, gen = refs[-2:]
        column, side = where_ref[0], where_ref[1]
        mine = [2 * (column ^ s) + side for s in range(columns)]
        for n, s in enumerate(order):
            x[mine[s]] = refs[n][...]
            x[mine[s] ^ 1] = refs[columns + n][...]
        sources = [(x, t) for t in range(5)]
        student_head(range(0, blocks, 2), first_ref[0], sources[:3], gen, 0)
        at_gen = lambda at: gen[at, 0]
        for s in range(columns):
            o_ref = refs[2 * columns + s]
            o_ref[0:1] = gen[mine[s]]
            teacher_head(blocks, [mine[s]], clip_ref, sources[3:], at_gen, o_ref, None)

    return pl.pallas_call(
        body,
        in_specs=[SMEM] * 3 + [VMEM] * (2 * columns),
        out_specs=[VMEM] * columns,
        out_shape=[jax.ShapeDtypeStruct((2, TOK, HD), jnp.bfloat16)] * columns,
        scratch_shapes=[
            pltpu.VMEM((blocks, 5, TOK, HD), jnp.bfloat16),
            pltpu.VMEM((blocks, 1, TOK, HD), jnp.bfloat16),
        ],
        compiler_params=LOCAL,
        cost_estimate=cost(0, 1, 1),
    )(first, clips, where, *own, *other)


def join(full, order, columns, where, slots):
    peers = len(order)

    def body(where_ref, *refs):
        for i, o_ref in enumerate(refs[full * peers :]):

            def put(h, tile):
                o_ref[0, :, pl.ds(pl.multiple_of(h * HD, HD), HD)] = tile

            for n, d in enumerate(order):
                for s in range(full):
                    put(s * peers + (where_ref[2] ^ d), refs[s * peers + n][i])
            for s in range(columns):
                ref = refs[order.index(2 * s)]
                put(full * peers + (where_ref[0] ^ s), ref[2 + i])

    width = (full * peers + columns) * HD
    return pl.pallas_call(
        body,
        in_specs=[SMEM] + [VMEM] * (full * peers),
        out_specs=[VMEM] * 2,
        out_shape=[jax.ShapeDtypeStruct((1, TOK, width), jnp.bfloat16)] * 2,
        compiler_params=LOCAL,
        cost_estimate=cost(0, 1, 4 * width // HD),
    )(where, *slots)


def by_slots_and_columns(tensors, peers, full, rest, first, clips):
    here = lax.axis_index("tm")
    where = jnp.stack([here // 2, here % 2, here]).astype(jnp.int32)

    def swapped(x, by):
        return lax.ppermute(x, "tm", [(i, i ^ by) for i in range(peers)]) if by else x

    far = list(range(rest, peers))
    near = sorted(range(1, rest), key=lambda d: (d % 2, d))
    there = [far[0], near[0], far[1], *near[1:], *far[2:], 0]
    home = [far[0]] + [d for pair in zip(range(1, rest), far[1:]) for d in pair] + [0]
    across = [*range(rest // 2, rest), *range(1, rest // 2), 0]

    pieces = rest_pack(full * peers, rest, where[:1], tensors)
    own = [swapped(pieces[s], 2 * s) for s in across]
    packed = slots_pack(full, there, where, tensors)
    arrived = [[swapped(x, d) for x, d in zip(xs, there)] for xs in packed]
    other = [swapped(x, 1) for x in own]
    pieces = rest_kernel(rest, across, first, clips, where, own, other)
    slots = []
    for xs in arrived:
        results = slot_kernel(there, home, first, clips, where, xs, pieces)
        slots += [swapped(x, d) for x, d in zip(results, home)]
        pieces = ()
    return tuple(join(full, home, rest, where, slots))


def by_roles(tensors, peers, heads, first, clips):
    here = lax.axis_index("tm")
    role = jnp.where(here < 2 * heads, 1 + here % 2, 0).astype(jnp.int32)[None]
    plan = [
        [(t, min(p // 2, heads - 1)) for t in ((3, 4, 4) if p % 2 else (0, 1, 2))]
        for p in range(peers)
    ]
    arrived = lax.all_to_all(pack(plan, [(0, heads)], tensors), "tm", 0, 0)
    gen = student_kernel(peers, first, role, arrived)
    shared = lax.ppermute(gen, "tm", [(2 * r, 2 * r + 1) for r in range(heads)])
    results = rest_teacher(peers, clips, role, arrived, 0, gen, shared)
    back = lax.all_to_all(results, "tm", 0, 0)
    return tuple(unpack([[(2 * r + i, 0) for r in range(heads)] for i in (0, 1)], back))


def per_device(student_q, student_k, student_v, teacher_q, teacher_k, stagger, clip_lengths):
    heads = student_q.shape[2] // HD
    peers = lax.axis_size("tm")
    full, rest = divmod(heads, peers)
    running = jnp.cumsum(clip_lengths[0])
    block = jnp.arange(peers, dtype=jnp.int32)
    before = running[None, :] <= block[:, None]
    low = jnp.max(jnp.where(before, running[None, :], 0), axis=1)
    high = jnp.min(jnp.where(before, peers, running[None, :]), axis=1)
    large = jnp.where(clip_lengths[0] == peers // 2 + 1, running - clip_lengths[0], 0)
    large = jnp.broadcast_to(jnp.max(large), (peers,))
    clips = jnp.stack([low, high, large]).astype(jnp.int32)
    tensors = (student_q, student_k, student_v, teacher_q, teacher_k)
    if full == 0:
        assert 2 * rest <= peers
        return by_roles(tensors, peers, rest, stagger, clips)
    assert peers == 2 * rest and rest & (rest - 1) == 0
    return by_slots_and_columns(tensors, peers, full, rest, stagger, clips)


def solution(mesh):
    spec = P("seq", "tm", "mp")
    return jax.shard_map(
        per_device,
        mesh=mesh,
        in_specs=(spec,) * 5 + (P("seq"), P("seq", None)),
        out_specs=(spec, spec),
        check_vma=False,
    )
```

```python
import functools
import math

import jax
import jax.numpy as jnp
from jax import lax
from jax.experimental import pallas as pl
from jax.experimental.pallas import tpu as pltpu
from jax.sharding import PartitionSpec as P

HD = 128
TOK = 128
NEG = -1e30
RATE = math.log2(math.e) / math.sqrt(HD)
MIB = 2**20
VMEM = pl.BlockSpec(memory_space=pltpu.VMEM)
SMEM = pl.BlockSpec(memory_space=pltpu.SMEM)
WHOLE = pltpu.CompilerParams(vmem_limit_bytes=60 * MIB)
LOCAL = pltpu.CompilerParams(vmem_limit_bytes=24 * MIB)


def attend(q, k, v, bias):
    g = q.shape[0]
    scores = lax.dot_general(
        q.reshape(g * TOK, HD), k, (((1,), (1,)), ((), ())), preferred_element_type=jnp.float32
    )
    scores = scores.reshape(g, TOK, -1)
    if bias is not None:
        scores = scores + bias
    top = jnp.max(scores, axis=-1, keepdims=True)
    weights = jnp.exp2((scores - top) * RATE)
    total = jnp.sum(weights, axis=-1, keepdims=True)
    weights = weights.astype(jnp.bfloat16).reshape(g * TOK, -1)
    mixed = jnp.dot(weights, v, preferred_element_type=jnp.float32)
    return mixed.reshape(g, TOK, HD) / total


def student_head(pairs, first, sources, o_ref, o_at):
    (q_ref, q_at), (k_ref, k_at), (v_ref, v_at) = sources
    for i in pairs:
        width = (i + 2) * TOK
        block = lax.broadcasted_iota(jnp.int32, (2, 1, width), 2) // TOK
        own = lax.broadcasted_iota(jnp.int32, (2, 1, width), 0) + i
        bias = jnp.where((block == own) | (block >= first) & (block < own), 0.0, NEG)
        k = k_ref[0 : i + 2, k_at].reshape(width, HD)
        v = v_ref[0 : i + 2, v_at].reshape(width, HD)
        o_ref[i : i + 2, o_at] = attend(q_ref[i : i + 2, q_at], k, v, bias).astype(jnp.bfloat16)


def teacher_head(blocks, rows, clip_ref, sources, gen, o_ref, o_at):
    (q_ref, q_at), (k_ref, k_at) = sources
    reach = blocks // 2 + 1
    width = reach * TOK
    offset = lax.broadcasted_iota(jnp.int32, (1, 1, width), 2) // TOK
    for i in rows:
        low = clip_ref[0, i]
        high = clip_ref[1, i]
        start = jnp.minimum(low, blocks - reach)
        block = offset + start
        bias = jnp.where((block >= low) & (block < high), 0.0, NEG)
        k = k_ref[pl.ds(start, reach), k_at].reshape(width, HD)
        v = gen(pl.ds(start, reach)).reshape(width, HD)
        out = attend(q_ref[pl.ds(i, 1), q_at], k, v, bias)
        score = (out[0] - gen(i).astype(jnp.float32)).astype(jnp.bfloat16)
        if o_at is None:
            o_ref[1] = score
        else:
            o_ref[i, o_at] = score


def teacher_whole_head(blocks, clip_ref, sources, gen, o_ref, o_at):
    (q_ref, q_at), (k_ref, k_at) = sources
    reach = blocks // 2 + 1

    def put(at, out):
        score = out - gen(at).astype(jnp.float32)
        o_ref[at, o_at] = score.astype(jnp.bfloat16)

    large = clip_ref[2, 0]
    k = k_ref[pl.ds(large, reach), k_at].reshape(reach * TOK, HD)
    v = gen(pl.ds(large, reach)).reshape(reach * TOK, HD)
    for i in range(0, reach, 2):
        at = pl.ds(large + i, min(2, reach - i))
        put(at, attend(q_ref[at, q_at], k, v, None))
    span = blocks - reach - 1
    offset = lax.broadcasted_iota(jnp.int32, (1, 1, span * TOK), 2) // TOK
    for j in range(blocks - reach):
        i = jnp.where(j < large, j, j + reach)
        low, high = clip_ref[0, i], clip_ref[1, i]
        start = jnp.minimum(low, blocks - span)
        block = offset + start
        bias = jnp.where((block >= low) & (block < high), 0.0, NEG)
        k = k_ref[pl.ds(start, span), k_at].reshape(span * TOK, HD)
        v = gen(pl.ds(start, span)).reshape(span * TOK, HD)
        put(pl.ds(i, 1), attend(q_ref[pl.ds(i, 1), q_at], k, v, bias))


def cost(heads, blocks, units):
    return pl.CostEstimate(
        flops=heads * blocks * blocks * 4 * TOK * TOK * HD,
        bytes_accessed=units * blocks * TOK * HD * 2,
        transcendentals=heads * blocks * blocks * TOK * TOK,
    )


def pack(plan, ranges, tensors):
    peers, units = len(plan), len(plan[0])
    widths = [count * HD for _, count in ranges]
    starts = [sum(widths[:r]) for r in range(len(ranges))]

    def place(h):
        for r, (head, count) in enumerate(ranges):
            if head <= h < head + count:
                return r, starts[r] + (h - head) * HD

    need = []
    for u in range(units):
        need.append(list(dict.fromkeys((plan[p][u][0], place(plan[p][u][1])[0]) for p in range(peers))))
    order = sorted(range(units), key=lambda u: (len(need[u]), u))
    fetch = list(dict.fromkeys(piece for u in order for piece in need[u]))

    def body(*refs):
        o_ref, rows, tiles, in_sem, out_sem = refs[len(tensors) :]
        copies = {}
        for n, (t, r) in enumerate(fetch):
            source = refs[t].at[0, :, pl.ds(ranges[r][0] * HD, widths[r])]
            target = rows.at[t, :, pl.ds(starts[r], widths[r])]
            copies[t, r] = pltpu.make_async_copy(source, target, in_sem.at[n])
            copies[t, r].start()
        sent = []
        for u in order:
            for piece in need[u]:
                if piece in copies:
                    copies.pop(piece).wait()
            for p in range(peers):
                t, h = plan[p][u]
                at = place(h)[1]
                tiles[p, u] = rows[t, :, at : at + HD]
            sent.append(pltpu.make_async_copy(tiles.at[:, u], o_ref.at[:, u], out_sem.at[u]))
            sent[-1].start()
        for copy in sent:
            copy.wait()

    return pl.pallas_call(
        body,
        in_specs=[pl.BlockSpec(memory_space=pl.ANY)] * len(tensors),
        out_specs=pl.BlockSpec(memory_space=pl.ANY),
        out_shape=jax.ShapeDtypeStruct((peers, units, TOK, HD), jnp.bfloat16),
        scratch_shapes=[
            pltpu.VMEM((len(tensors), TOK, sum(widths)), jnp.bfloat16),
            pltpu.VMEM((peers, units, TOK, HD), jnp.bfloat16),
            pltpu.SemaphoreType.DMA((len(fetch),)),
            pltpu.SemaphoreType.DMA((units,)),
        ],
        compiler_params=WHOLE,
        cost_estimate=cost(0, peers, 2 * units),
    )(*tensors)


def unpack(places, back):
    def body(x_ref, *o_refs):
        for o_ref, place in zip(o_refs, places):
            for h, (p, u) in enumerate(place):
                o_ref[0, :, h * HD : (h + 1) * HD] = x_ref[p, u]

    width = len(places[0]) * HD
    return pl.pallas_call(
        body,
        out_shape=[jax.ShapeDtypeStruct((1, TOK, width), jnp.bfloat16) for _ in places],
        compiler_params=LOCAL,
        cost_estimate=cost(0, 1, 4 * len(places[0])),
    )(back)


def student_kernel(blocks, first, role, arrived):
    def body(first_ref, role_ref, x_ref, o_ref):
        @pl.when(role_ref[0] == 1)
        def _():
            sources = [(x_ref, t) for t in range(3)]
            student_head(range(0, blocks, 2), first_ref[0], sources, o_ref, 0)

    return pl.pallas_call(
        body,
        in_specs=[SMEM, SMEM, VMEM],
        out_specs=VMEM,
        out_shape=jax.ShapeDtypeStruct((blocks, 1, TOK, HD), jnp.bfloat16),
        compiler_params=LOCAL,
        cost_estimate=cost(1, blocks, 4),
    )(first, role, arrived)


def rest_teacher(blocks, clips, role, arrived, offset, gen, shared):
    def body(clip_ref, role_ref, x_ref, gen_ref, shared_ref, o_ref):
        @pl.when(role_ref[0] == 1)
        def _():
            o_ref[...] = gen_ref[...]

        @pl.when(role_ref[0] == 2)
        def _():
            sources = [(x_ref, offset + t) for t in range(2)]
            teacher_head(
                blocks, range(blocks), clip_ref, sources, lambda at: shared_ref[at, 0], o_ref, 0
            )

    return pl.pallas_call(
        body,
        in_specs=[SMEM, SMEM, VMEM, VMEM, VMEM],
        out_specs=VMEM,
        out_shape=jax.ShapeDtypeStruct((blocks, 1, TOK, HD), jnp.bfloat16),
        compiler_params=LOCAL,
        cost_estimate=cost(1, blocks, 5),
    )(clips, role, arrived, gen, shared)


def slot_kernel(order, home, first, clips, where, arrived, pieces):
    blocks = len(order)

    def body(first_ref, clip_ref, where_ref, *refs):
        x_refs, refs = refs[:blocks], refs[blocks:]
        piece_refs, refs = refs[: len(pieces)], refs[len(pieces) :]
        o_refs, (x, y) = refs[:blocks], refs[blocks:]
        at = [where_ref[2] ^ d for d in order]
        for i in range(blocks):
            x[at[i]] = x_refs[i][...]

        sources = [(x, t) for t in range(5)]
        student_head(range(0, blocks, 2), first_ref[0], sources[:3], y, 0)
        gen = lambda at: y[at, 0]
        teacher_whole_head(blocks, clip_ref, sources[3:], gen, y, 1)
        for i, d in enumerate(home):
            o_refs[i][0:2] = y[where_ref[2] ^ d]
            if pieces and d % 2 == 0:
                o_refs[i][2:4] = piece_refs[d // 2][...]

    return pl.pallas_call(
        body,
        in_specs=[SMEM] * 3 + [VMEM] * (blocks + len(pieces)),
        out_specs=[VMEM] * blocks,
        out_shape=[
            jax.ShapeDtypeStruct((4 if pieces and d % 2 == 0 else 2, TOK, HD), jnp.bfloat16)
            for d in home
        ],
        scratch_shapes=[
            pltpu.VMEM((blocks, 5, TOK, HD), jnp.bfloat16),
            pltpu.VMEM((blocks, 2, TOK, HD), jnp.bfloat16),
        ],
        compiler_params=LOCAL,
        cost_estimate=cost(2, blocks, 7),
    )(first, clips, where, *arrived, *pieces)


def slots_pack(full, order, where, tensors):
    peers = len(order)

    def body(where_ref, *refs):
        o_refs, (rows, sems) = refs[5 : 5 + full * peers], refs[5 + full * peers :]
        copies = []
        for t in range(5):
            source = refs[t].at[0, :, pl.ds(0, full * peers * HD)]
            copies.append(pltpu.make_async_copy(source, rows.at[t], sems.at[t]))
            copies[-1].start()
        for t in range(5):
            copies[t].wait()
            for s in range(full):
                for i, d in enumerate(order):
                    at = pl.multiple_of((s * peers + (where_ref[2] ^ d)) * HD, HD)
                    o_refs[s * peers + i][t] = rows[t, :, pl.ds(at, HD)]

    packed = pl.pallas_call(
        body,
        in_specs=[SMEM] + [pl.BlockSpec(memory_space=pl.ANY)] * 5,
        out_specs=[VMEM] * (full * peers),
        out_shape=[jax.ShapeDtypeStruct((5, TOK, HD), jnp.bfloat16)] * (full * peers),
        scratch_shapes=[
            pltpu.VMEM((5, TOK, full * peers * HD), jnp.bfloat16),
            pltpu.SemaphoreType.DMA((5,)),
        ],
        compiler_params=WHOLE,
        cost_estimate=cost(0, peers, 10 * full),
    )(where, *tensors)
    return [packed[s * peers : (s + 1) * peers] for s in range(full)]


def rest_pack(base, columns, column, tensors):
    def body(column_ref, *refs):
        rows, sems = refs[-2:]
        copies = []
        for t in range(5):
            source = refs[t].at[0, :, pl.ds(base * HD, columns * HD)]
            copies.append(pltpu.make_async_copy(source, rows.at[t], sems.at[t]))
            copies[-1].start()
        for t in range(5):
            copies[t].wait()
            for s in range(columns):
                at = pl.multiple_of((column_ref[0] ^ s) * HD, HD)
                refs[5 + s][t] = rows[t, :, pl.ds(at, HD)]

    return pl.pallas_call(
        body,
        in_specs=[SMEM] + [pl.BlockSpec(memory_space=pl.ANY)] * 5,
        out_specs=[VMEM] * columns,
        out_shape=[jax.ShapeDtypeStruct((5, TOK, HD), jnp.bfloat16)] * columns,
        scratch_shapes=[
            pltpu.VMEM((5, TOK, columns * HD), jnp.bfloat16),
            pltpu.SemaphoreType.DMA((5,)),
        ],
        compiler_params=WHOLE,
        cost_estimate=cost(0, 1, 10 * columns),
    )(column, *tensors)


def rest_kernel(columns, order, first, clips, where, own, other):
    blocks = 2 * columns

    def body(first_ref, clip_ref, where_ref, *refs):
        x, gen = refs[-2:]
        column, side = where_ref[0], where_ref[1]
        mine = [2 * (column ^ s) + side for s in range(columns)]
        for n, s in enumerate(order):
            x[mine[s]] = refs[n][...]
            x[mine[s] ^ 1] = refs[columns + n][...]
        sources = [(x, t) for t in range(5)]
        student_head(range(0, blocks, 2), first_ref[0], sources[:3], gen, 0)
        at_gen = lambda at: gen[at, 0]
        for s in range(columns):
            o_ref = refs[2 * columns + s]
            o_ref[0:1] = gen[mine[s]]
            teacher_head(blocks, [mine[s]], clip_ref, sources[3:], at_gen, o_ref, None)

    return pl.pallas_call(
        body,
        in_specs=[SMEM] * 3 + [VMEM] * (2 * columns),
        out_specs=[VMEM] * columns,
        out_shape=[jax.ShapeDtypeStruct((2, TOK, HD), jnp.bfloat16)] * columns,
        scratch_shapes=[
            pltpu.VMEM((blocks, 5, TOK, HD), jnp.bfloat16),
            pltpu.VMEM((blocks, 1, TOK, HD), jnp.bfloat16),
        ],
        compiler_params=LOCAL,
        cost_estimate=cost(0, 1, 1),
    )(first, clips, where, *own, *other)


def join(full, order, columns, where, slots):
    peers = len(order)

    def body(where_ref, *refs):
        for i, o_ref in enumerate(refs[full * peers :]):

            def put(h, tile):
                o_ref[0, :, pl.ds(pl.multiple_of(h * HD, HD), HD)] = tile

            for n, d in enumerate(order):
                for s in range(full):
                    put(s * peers + (where_ref[2] ^ d), refs[s * peers + n][i])
            for s in range(columns):
                ref = refs[order.index(2 * s)]
                put(full * peers + (where_ref[0] ^ s), ref[2 + i])

    width = (full * peers + columns) * HD
    return pl.pallas_call(
        body,
        in_specs=[SMEM] + [VMEM] * (full * peers),
        out_specs=[VMEM] * 2,
        out_shape=[jax.ShapeDtypeStruct((1, TOK, width), jnp.bfloat16)] * 2,
        compiler_params=LOCAL,
        cost_estimate=cost(0, 1, 4 * width // HD),
    )(where, *slots)


def by_slots_and_columns(tensors, peers, full, rest, first, clips):
    here = lax.axis_index("tm")
    where = jnp.stack([here // 2, here % 2, here]).astype(jnp.int32)

    def swapped(x, by):
        return lax.ppermute(x, "tm", [(i, i ^ by) for i in range(peers)]) if by else x

    far = list(range(rest, peers))
    near = sorted(range(1, rest), key=lambda d: (d % 2, d))
    there = [far[0], near[0], far[1], *near[1:], *far[2:], 0]
    home = [far[0]] + [d for pair in zip(range(1, rest), far[1:]) for d in pair] + [0]
    across = [*range(rest // 2, rest), *range(1, rest // 2), 0]

    pieces = rest_pack(full * peers, rest, where[:1], tensors)
    own = [swapped(pieces[s], 2 * s) for s in across]
    packed = slots_pack(full, there, where, tensors)
    arrived = [[swapped(x, d) for x, d in zip(xs, there)] for xs in packed]

    def work(xs, pieces):
        return slot_kernel(there, home, first, clips, where, xs, pieces)

    results = [work(xs, ()) for xs in arrived[1:]]
    results, own = lax.optimization_barrier((results, own))
    other = [swapped(x, 1) for x in own]
    pieces = rest_kernel(rest, across, first, clips, where, own, other)
    results = [work(arrived[0], pieces), *results]
    slots = [swapped(x, d) for xs in results for x, d in zip(xs, home)]
    return tuple(join(full, home, rest, where, slots))


def by_roles(tensors, peers, heads, first, clips):
    here = lax.axis_index("tm")
    role = jnp.where(here < 2 * heads, 1 + here % 2, 0).astype(jnp.int32)[None]
    plan = [
        [(t, min(p // 2, heads - 1)) for t in ((3, 4, 4) if p % 2 else (0, 1, 2))]
        for p in range(peers)
    ]
    arrived = lax.all_to_all(pack(plan, [(0, heads)], tensors), "tm", 0, 0)
    gen = student_kernel(peers, first, role, arrived)
    shared = lax.ppermute(gen, "tm", [(2 * r, 2 * r + 1) for r in range(heads)])
    results = rest_teacher(peers, clips, role, arrived, 0, gen, shared)
    back = lax.all_to_all(results, "tm", 0, 0)
    return tuple(unpack([[(2 * r + i, 0) for r in range(heads)] for i in (0, 1)], back))


def per_device(student_q, student_k, student_v, teacher_q, teacher_k, stagger, clip_lengths):
    heads = student_q.shape[2] // HD
    peers = lax.axis_size("tm")
    full, rest = divmod(heads, peers)
    running = jnp.cumsum(clip_lengths[0])
    block = jnp.arange(peers, dtype=jnp.int32)
    before = running[None, :] <= block[:, None]
    low = jnp.max(jnp.where(before, running[None, :], 0), axis=1)
    high = jnp.min(jnp.where(before, peers, running[None, :]), axis=1)
    large = jnp.where(clip_lengths[0] == peers // 2 + 1, running - clip_lengths[0], 0)
    large = jnp.broadcast_to(jnp.max(large), (peers,))
    clips = jnp.stack([low, high, large]).astype(jnp.int32)
    tensors = (student_q, student_k, student_v, teacher_q, teacher_k)
    if full == 0:
        assert 2 * rest <= peers
        return by_roles(tensors, peers, rest, stagger, clips)
    assert peers == 2 * rest and rest & (rest - 1) == 0
    return by_slots_and_columns(tensors, peers, full, rest, stagger, clips)


def solution(mesh):
    spec = P("seq", "tm", "mp")
    return jax.shard_map(
        per_device,
        mesh=mesh,
        in_specs=(spec,) * 5 + (P("seq"), P("seq", None)),
        out_specs=(spec, spec),
        check_vma=False,
    )
```

```python
import functools
import math

import jax
import jax.numpy as jnp
from jax import lax
from jax.experimental import pallas as pl
from jax.experimental.pallas import tpu as pltpu
from jax.sharding import PartitionSpec as P

HD = 128
TOK = 128
NEG = -1e30
RATE = math.log2(math.e) / math.sqrt(HD)
MIB = 2**20
VMEM = pl.BlockSpec(memory_space=pltpu.VMEM)
SMEM = pl.BlockSpec(memory_space=pltpu.SMEM)
WHOLE = pltpu.CompilerParams(vmem_limit_bytes=60 * MIB)
LOCAL = pltpu.CompilerParams(vmem_limit_bytes=24 * MIB)


def attend(q, k, v, bias):
    g = q.shape[0]
    scores = lax.dot_general(
        q.reshape(g * TOK, HD), k, (((1,), (1,)), ((), ())), preferred_element_type=jnp.float32
    )
    scores = scores.reshape(g, TOK, -1)
    if bias is not None:
        scores = scores + bias
    top = jnp.max(scores, axis=-1, keepdims=True)
    weights = jnp.exp2((scores - top) * RATE)
    total = jnp.sum(weights, axis=-1, keepdims=True)
    weights = weights.astype(jnp.bfloat16).reshape(g * TOK, -1)
    mixed = jnp.dot(weights, v, preferred_element_type=jnp.float32)
    return mixed.reshape(g, TOK, HD) / total


def student_head(pairs, first, sources, o_ref, o_at):
    (q_ref, q_at), (k_ref, k_at), (v_ref, v_at) = sources
    for i in pairs:
        width = (i + 2) * TOK
        block = lax.broadcasted_iota(jnp.int32, (2, 1, width), 2) // TOK
        own = lax.broadcasted_iota(jnp.int32, (2, 1, width), 0) + i
        bias = jnp.where((block == own) | (block >= first) & (block < own), 0.0, NEG)
        k = k_ref[0 : i + 2, k_at].reshape(width, HD)
        v = v_ref[0 : i + 2, v_at].reshape(width, HD)
        o_ref[i : i + 2, o_at] = attend(q_ref[i : i + 2, q_at], k, v, bias).astype(jnp.bfloat16)


def teacher_head(blocks, rows, clip_ref, sources, gen, o_ref, o_at):
    (q_ref, q_at), (k_ref, k_at) = sources
    reach = blocks // 2 + 1
    width = reach * TOK
    offset = lax.broadcasted_iota(jnp.int32, (1, 1, width), 2) // TOK
    for i in rows:
        low = clip_ref[0, i]
        high = clip_ref[1, i]
        start = jnp.minimum(low, blocks - reach)
        block = offset + start
        bias = jnp.where((block >= low) & (block < high), 0.0, NEG)
        k = k_ref[pl.ds(start, reach), k_at].reshape(width, HD)
        v = gen(pl.ds(start, reach)).reshape(width, HD)
        out = attend(q_ref[pl.ds(i, 1), q_at], k, v, bias)
        score = (out[0] - gen(i).astype(jnp.float32)).astype(jnp.bfloat16)
        if o_at is None:
            o_ref[1] = score
        else:
            o_ref[i, o_at] = score


def teacher_whole_head(blocks, clip_ref, sources, gen, o_ref, o_at):
    (q_ref, q_at), (k_ref, k_at) = sources
    reach = blocks // 2 + 1

    def put(at, out):
        score = out - gen(at).astype(jnp.float32)
        o_ref[at, o_at] = score.astype(jnp.bfloat16)

    large = clip_ref[2, 0]
    k = k_ref[pl.ds(large, reach), k_at].reshape(reach * TOK, HD)
    v = gen(pl.ds(large, reach)).reshape(reach * TOK, HD)
    for i in range(0, reach, 2):
        at = pl.ds(large + i, min(2, reach - i))
        put(at, attend(q_ref[at, q_at], k, v, None))
    span = blocks - reach - 1
    offset = lax.broadcasted_iota(jnp.int32, (1, 1, span * TOK), 2) // TOK
    for j in range(blocks - reach):
        i = jnp.where(j < large, j, j + reach)
        low, high = clip_ref[0, i], clip_ref[1, i]
        start = jnp.minimum(low, blocks - span)
        block = offset + start
        bias = jnp.where((block >= low) & (block < high), 0.0, NEG)
        k = k_ref[pl.ds(start, span), k_at].reshape(span * TOK, HD)
        v = gen(pl.ds(start, span)).reshape(span * TOK, HD)
        put(pl.ds(i, 1), attend(q_ref[pl.ds(i, 1), q_at], k, v, bias))


def cost(heads, blocks, units):
    return pl.CostEstimate(
        flops=heads * blocks * blocks * 4 * TOK * TOK * HD,
        bytes_accessed=units * blocks * TOK * HD * 2,
        transcendentals=heads * blocks * blocks * TOK * TOK,
    )


def pack(plan, ranges, tensors):
    peers, units = len(plan), len(plan[0])
    widths = [count * HD for _, count in ranges]
    starts = [sum(widths[:r]) for r in range(len(ranges))]

    def place(h):
        for r, (head, count) in enumerate(ranges):
            if head <= h < head + count:
                return r, starts[r] + (h - head) * HD

    need = []
    for u in range(units):
        need.append(list(dict.fromkeys((plan[p][u][0], place(plan[p][u][1])[0]) for p in range(peers))))
    order = sorted(range(units), key=lambda u: (len(need[u]), u))
    fetch = list(dict.fromkeys(piece for u in order for piece in need[u]))

    def body(*refs):
        o_ref, rows, tiles, in_sem, out_sem = refs[len(tensors) :]
        copies = {}
        for n, (t, r) in enumerate(fetch):
            source = refs[t].at[0, :, pl.ds(ranges[r][0] * HD, widths[r])]
            target = rows.at[t, :, pl.ds(starts[r], widths[r])]
            copies[t, r] = pltpu.make_async_copy(source, target, in_sem.at[n])
            copies[t, r].start()
        sent = []
        for u in order:
            for piece in need[u]:
                if piece in copies:
                    copies.pop(piece).wait()
            for p in range(peers):
                t, h = plan[p][u]
                at = place(h)[1]
                tiles[p, u] = rows[t, :, at : at + HD]
            sent.append(pltpu.make_async_copy(tiles.at[:, u], o_ref.at[:, u], out_sem.at[u]))
            sent[-1].start()
        for copy in sent:
            copy.wait()

    return pl.pallas_call(
        body,
        in_specs=[pl.BlockSpec(memory_space=pl.ANY)] * len(tensors),
        out_specs=pl.BlockSpec(memory_space=pl.ANY),
        out_shape=jax.ShapeDtypeStruct((peers, units, TOK, HD), jnp.bfloat16),
        scratch_shapes=[
            pltpu.VMEM((len(tensors), TOK, sum(widths)), jnp.bfloat16),
            pltpu.VMEM((peers, units, TOK, HD), jnp.bfloat16),
            pltpu.SemaphoreType.DMA((len(fetch),)),
            pltpu.SemaphoreType.DMA((units,)),
        ],
        compiler_params=WHOLE,
        cost_estimate=cost(0, peers, 2 * units),
    )(*tensors)


def unpack(places, back):
    def body(x_ref, *o_refs):
        for o_ref, place in zip(o_refs, places):
            for h, (p, u) in enumerate(place):
                o_ref[0, :, h * HD : (h + 1) * HD] = x_ref[p, u]

    width = len(places[0]) * HD
    return pl.pallas_call(
        body,
        out_shape=[jax.ShapeDtypeStruct((1, TOK, width), jnp.bfloat16) for _ in places],
        compiler_params=LOCAL,
        cost_estimate=cost(0, 1, 4 * len(places[0])),
    )(back)


def student_kernel(blocks, first, role, arrived):
    def body(first_ref, role_ref, x_ref, o_ref):
        @pl.when(role_ref[0] == 1)
        def _():
            sources = [(x_ref, t) for t in range(3)]
            student_head(range(0, blocks, 2), first_ref[0], sources, o_ref, 0)

    return pl.pallas_call(
        body,
        in_specs=[SMEM, SMEM, VMEM],
        out_specs=VMEM,
        out_shape=jax.ShapeDtypeStruct((blocks, 1, TOK, HD), jnp.bfloat16),
        compiler_params=LOCAL,
        cost_estimate=cost(1, blocks, 4),
    )(first, role, arrived)


def rest_teacher(blocks, clips, role, arrived, offset, gen, shared):
    def body(clip_ref, role_ref, x_ref, gen_ref, shared_ref, o_ref):
        @pl.when(role_ref[0] == 1)
        def _():
            o_ref[...] = gen_ref[...]

        @pl.when(role_ref[0] == 2)
        def _():
            sources = [(x_ref, offset + t) for t in range(2)]
            teacher_head(
                blocks, range(blocks), clip_ref, sources, lambda at: shared_ref[at, 0], o_ref, 0
            )

    return pl.pallas_call(
        body,
        in_specs=[SMEM, SMEM, VMEM, VMEM, VMEM],
        out_specs=VMEM,
        out_shape=jax.ShapeDtypeStruct((blocks, 1, TOK, HD), jnp.bfloat16),
        compiler_params=LOCAL,
        cost_estimate=cost(1, blocks, 5),
    )(clips, role, arrived, gen, shared)


def slots_kernel(full, order, home, first, clips, where, arrived):
    blocks = len(order)

    def body(first_ref, clip_ref, where_ref, *refs):
        x_refs, o_refs, (x, y) = refs[:blocks], refs[blocks : 2 * blocks], refs[2 * blocks :]
        at = [where_ref[2] ^ d for d in order]
        for i in range(blocks):
            x[at[i]] = x_refs[i][...]

        for s in range(full):
            sources = [(x, 5 * s + t) for t in range(5)]
            student_head(range(0, blocks, 2), first_ref[0], sources[:3], y, 2 * s)
            gen = functools.partial(lambda u, at: y[at, u], 2 * s)
            teacher_whole_head(blocks, clip_ref, sources[3:], gen, y, 2 * s + 1)

        for i, d in enumerate(home):
            o_refs[i][...] = y[where_ref[2] ^ d]

    return pl.pallas_call(
        body,
        in_specs=[SMEM] * 3 + [VMEM] * blocks,
        out_specs=[VMEM] * blocks,
        out_shape=[jax.ShapeDtypeStruct((2 * full, TOK, HD), jnp.bfloat16)] * blocks,
        scratch_shapes=[
            pltpu.VMEM((blocks, 5 * full, TOK, HD), jnp.bfloat16),
            pltpu.VMEM((blocks, 2 * full, TOK, HD), jnp.bfloat16),
        ],
        compiler_params=LOCAL,
        cost_estimate=cost(2 * full, blocks, 7 * full),
    )(first, clips, where, *arrived)


def slots_pack(full, order, where, tensors):
    peers = len(order)

    def body(where_ref, *refs):
        o_refs, (rows, sems) = refs[5 : 5 + peers], refs[5 + peers :]
        copies = []
        for t in range(5):
            source = refs[t].at[0, :, pl.ds(0, full * peers * HD)]
            copies.append(pltpu.make_async_copy(source, rows.at[t], sems.at[t]))
            copies[-1].start()
        for t in range(5):
            copies[t].wait()
            for s in range(full):
                for i, d in enumerate(order):
                    at = pl.multiple_of((s * peers + (where_ref[2] ^ d)) * HD, HD)
                    o_refs[i][5 * s + t] = rows[t, :, pl.ds(at, HD)]

    return pl.pallas_call(
        body,
        in_specs=[SMEM] + [pl.BlockSpec(memory_space=pl.ANY)] * 5,
        out_specs=[VMEM] * peers,
        out_shape=[jax.ShapeDtypeStruct((5 * full, TOK, HD), jnp.bfloat16)] * peers,
        scratch_shapes=[
            pltpu.VMEM((5, TOK, full * peers * HD), jnp.bfloat16),
            pltpu.SemaphoreType.DMA((5,)),
        ],
        compiler_params=WHOLE,
        cost_estimate=cost(0, peers, 10 * full),
    )(where, *tensors)


def rest_pack(base, columns, column, tensors):
    def body(column_ref, *refs):
        rows, sems = refs[-2:]
        copies = []
        for t in range(5):
            source = refs[t].at[0, :, pl.ds(base * HD, columns * HD)]
            copies.append(pltpu.make_async_copy(source, rows.at[t], sems.at[t]))
            copies[-1].start()
        for t in range(5):
            copies[t].wait()
            for s in range(columns):
                at = pl.multiple_of((column_ref[0] ^ s) * HD, HD)
                refs[5 + s][t] = rows[t, :, pl.ds(at, HD)]

    return pl.pallas_call(
        body,
        in_specs=[SMEM] + [pl.BlockSpec(memory_space=pl.ANY)] * 5,
        out_specs=[VMEM] * columns,
        out_shape=[jax.ShapeDtypeStruct((5, TOK, HD), jnp.bfloat16)] * columns,
        scratch_shapes=[
            pltpu.VMEM((5, TOK, columns * HD), jnp.bfloat16),
            pltpu.SemaphoreType.DMA((5,)),
        ],
        compiler_params=WHOLE,
        cost_estimate=cost(0, 1, 10 * columns),
    )(column, *tensors)


def rest_kernel(columns, first, clips, where, own, other):
    blocks = 2 * columns

    def body(first_ref, clip_ref, where_ref, *refs):
        x, gen = refs[-2:]
        column, side = where_ref[0], where_ref[1]
        mine = [2 * (column ^ s) + side for s in range(columns)]
        for s in range(columns):
            x[mine[s]] = refs[s][...]
            x[mine[s] ^ 1] = refs[columns + s][...]
        sources = [(x, t) for t in range(5)]
        student_head(range(0, blocks, 2), first_ref[0], sources[:3], gen, 0)
        at_gen = lambda at: gen[at, 0]
        for s in range(columns):
            o_ref = refs[2 * columns + s]
            o_ref[0:1] = gen[mine[s]]
            teacher_head(blocks, [mine[s]], clip_ref, sources[3:], at_gen, o_ref, None)

    return pl.pallas_call(
        body,
        in_specs=[SMEM] * 3 + [VMEM] * (2 * columns),
        out_specs=[VMEM] * columns,
        out_shape=[jax.ShapeDtypeStruct((2, TOK, HD), jnp.bfloat16)] * columns,
        scratch_shapes=[
            pltpu.VMEM((blocks, 5, TOK, HD), jnp.bfloat16),
            pltpu.VMEM((blocks, 1, TOK, HD), jnp.bfloat16),
        ],
        compiler_params=LOCAL,
        cost_estimate=cost(0, 1, 1),
    )(first, clips, where, *own, *other)


def join(full, order, columns, where, slots, rests):
    peers = len(order)

    def body(where_ref, *refs):
        for i, o_ref in enumerate(refs[peers + columns :]):

            def put(h, tile):
                o_ref[0, :, pl.ds(pl.multiple_of(h * HD, HD), HD)] = tile

            for n, d in enumerate(order):
                for s in range(full):
                    put(s * peers + (where_ref[2] ^ d), refs[n][2 * s + i])
            for s in range(columns):
                put(full * peers + (where_ref[0] ^ s), refs[peers + s][i])

    width = (full * peers + columns) * HD
    return pl.pallas_call(
        body,
        in_specs=[SMEM] + [VMEM] * (peers + columns),
        out_specs=[VMEM] * 2,
        out_shape=[jax.ShapeDtypeStruct((1, TOK, width), jnp.bfloat16)] * 2,
        compiler_params=LOCAL,
        cost_estimate=cost(0, 1, 4 * width // HD),
    )(where, *slots, *rests)


def by_slots_and_columns(tensors, peers, full, rest, first, clips):
    here = lax.axis_index("tm")
    where = jnp.stack([here // 2, here % 2, here]).astype(jnp.int32)

    def swapped(x, by):
        return lax.ppermute(x, "tm", [(i, i ^ by) for i in range(peers)]) if by else x

    far = list(range(rest, peers))
    near = sorted(range(1, rest), key=lambda d: (d % 2, d))
    there = [far[0], near[0], far[1], *near[1:], *far[2:], 0]
    home = [*range(1, peers), 0]

    pieces = rest_pack(full * peers, rest, where[:1], tensors)
    own = [swapped(x, 2 * s) for s, x in enumerate(pieces)]
    packed = slots_pack(full, there, where, tensors)
    arrived = [swapped(x, d) for x, d in zip(packed, there)]
    other = [swapped(x, 1) for x in own]
    pieces = rest_kernel(rest, first, clips, where, own, other)
    arrived, pieces = lax.optimization_barrier((arrived, pieces))
    rests = [swapped(x, 2 * s) for s, x in enumerate(pieces)]
    results = slots_kernel(full, there, home, first, clips, where, arrived)
    results, rests = lax.optimization_barrier((results, rests))
    slots = [swapped(x, d) for x, d in zip(results, home)]
    return tuple(join(full, home, rest, where, slots, rests))


def by_roles(tensors, peers, heads, first, clips):
    here = lax.axis_index("tm")
    role = jnp.where(here < 2 * heads, 1 + here % 2, 0).astype(jnp.int32)[None]
    plan = [
        [(t, min(p // 2, heads - 1)) for t in ((3, 4, 4) if p % 2 else (0, 1, 2))]
        for p in range(peers)
    ]
    arrived = lax.all_to_all(pack(plan, [(0, heads)], tensors), "tm", 0, 0)
    gen = student_kernel(peers, first, role, arrived)
    shared = lax.ppermute(gen, "tm", [(2 * r, 2 * r + 1) for r in range(heads)])
    results = rest_teacher(peers, clips, role, arrived, 0, gen, shared)
    back = lax.all_to_all(results, "tm", 0, 0)
    return tuple(unpack([[(2 * r + i, 0) for r in range(heads)] for i in (0, 1)], back))


def per_device(student_q, student_k, student_v, teacher_q, teacher_k, stagger, clip_lengths):
    heads = student_q.shape[2] // HD
    peers = lax.axis_size("tm")
    full, rest = divmod(heads, peers)
    running = jnp.cumsum(clip_lengths[0])
    block = jnp.arange(peers, dtype=jnp.int32)
    before = running[None, :] <= block[:, None]
    low = jnp.max(jnp.where(before, running[None, :], 0), axis=1)
    high = jnp.min(jnp.where(before, peers, running[None, :]), axis=1)
    large = jnp.where(clip_lengths[0] == peers // 2 + 1, running - clip_lengths[0], 0)
    large = jnp.broadcast_to(jnp.max(large), (peers,))
    clips = jnp.stack([low, high, large]).astype(jnp.int32)
    tensors = (student_q, student_k, student_v, teacher_q, teacher_k)
    if full == 0:
        assert 2 * rest <= peers
        return by_roles(tensors, peers, rest, stagger, clips)
    assert peers == 2 * rest and rest & (rest - 1) == 0
    return by_slots_and_columns(tensors, peers, full, rest, stagger, clips)


def solution(mesh):
    spec = P("seq", "tm", "mp")
    return jax.shard_map(
        per_device,
        mesh=mesh,
        in_specs=(spec,) * 5 + (P("seq"), P("seq", None)),
        out_specs=(spec, spec),
        check_vma=False,
    )
```

```python
import functools
import math

import jax
import jax.numpy as jnp
from jax import lax
from jax.experimental import pallas as pl
from jax.experimental.pallas import tpu as pltpu
from jax.sharding import PartitionSpec as P

HD = 128
TOK = 128
NEG = -1e30
RATE = math.log2(math.e) / math.sqrt(HD)
MIB = 2**20
VMEM = pl.BlockSpec(memory_space=pltpu.VMEM)
SMEM = pl.BlockSpec(memory_space=pltpu.SMEM)
WHOLE = pltpu.CompilerParams(vmem_limit_bytes=60 * MIB)
LOCAL = pltpu.CompilerParams(vmem_limit_bytes=24 * MIB)


def attend(q, k, v, bias):
    g = q.shape[0]
    scores = lax.dot_general(
        q.reshape(g * TOK, HD), k, (((1,), (1,)), ((), ())), preferred_element_type=jnp.float32
    )
    scores = scores.reshape(g, TOK, -1)
    if bias is not None:
        scores = scores + bias
    top = jnp.max(scores, axis=-1, keepdims=True)
    weights = jnp.exp2((scores - top) * RATE)
    total = jnp.sum(weights, axis=-1, keepdims=True)
    weights = weights.astype(jnp.bfloat16).reshape(g * TOK, -1)
    mixed = jnp.dot(weights, v, preferred_element_type=jnp.float32)
    return mixed.reshape(g, TOK, HD) / total


def student_head(pairs, first, sources, o_ref, o_at):
    (q_ref, q_at), (k_ref, k_at), (v_ref, v_at) = sources
    for i in pairs:
        width = (i + 2) * TOK
        block = lax.broadcasted_iota(jnp.int32, (2, 1, width), 2) // TOK
        own = lax.broadcasted_iota(jnp.int32, (2, 1, width), 0) + i
        bias = jnp.where((block == own) | (block >= first) & (block < own), 0.0, NEG)
        k = k_ref[0 : i + 2, k_at].reshape(width, HD)
        v = v_ref[0 : i + 2, v_at].reshape(width, HD)
        o_ref[i : i + 2, o_at] = attend(q_ref[i : i + 2, q_at], k, v, bias).astype(jnp.bfloat16)


def teacher_head(blocks, rows, clip_ref, sources, gen, o_ref, o_at):
    (q_ref, q_at), (k_ref, k_at) = sources
    reach = blocks // 2 + 1
    width = reach * TOK
    offset = lax.broadcasted_iota(jnp.int32, (1, 1, width), 2) // TOK
    for i in rows:
        low = clip_ref[0, i]
        high = clip_ref[1, i]
        start = jnp.minimum(low, blocks - reach)
        block = offset + start
        bias = jnp.where((block >= low) & (block < high), 0.0, NEG)
        k = k_ref[pl.ds(start, reach), k_at].reshape(width, HD)
        v = gen(pl.ds(start, reach)).reshape(width, HD)
        out = attend(q_ref[pl.ds(i, 1), q_at], k, v, bias)
        score = (out[0] - gen(i).astype(jnp.float32)).astype(jnp.bfloat16)
        if o_at is None:
            o_ref[1] = score
        else:
            o_ref[i, o_at] = score


def teacher_whole_head(blocks, clip_ref, sources, gen, o_ref, o_at):
    (q_ref, q_at), (k_ref, k_at) = sources
    reach = blocks // 2 + 1

    def put(at, out):
        score = out - gen(at).astype(jnp.float32)
        o_ref[at, o_at] = score.astype(jnp.bfloat16)

    large = clip_ref[2, 0]
    k = k_ref[pl.ds(large, reach), k_at].reshape(reach * TOK, HD)
    v = gen(pl.ds(large, reach)).reshape(reach * TOK, HD)
    for i in range(0, reach, 2):
        at = pl.ds(large + i, min(2, reach - i))
        put(at, attend(q_ref[at, q_at], k, v, None))
    span = blocks - reach - 1
    offset = lax.broadcasted_iota(jnp.int32, (1, 1, span * TOK), 2) // TOK
    for j in range(blocks - reach):
        i = jnp.where(j < large, j, j + reach)
        low, high = clip_ref[0, i], clip_ref[1, i]
        start = jnp.minimum(low, blocks - span)
        block = offset + start
        bias = jnp.where((block >= low) & (block < high), 0.0, NEG)
        k = k_ref[pl.ds(start, span), k_at].reshape(span * TOK, HD)
        v = gen(pl.ds(start, span)).reshape(span * TOK, HD)
        put(pl.ds(i, 1), attend(q_ref[pl.ds(i, 1), q_at], k, v, bias))


def cost(heads, blocks, units):
    return pl.CostEstimate(
        flops=heads * blocks * blocks * 4 * TOK * TOK * HD,
        bytes_accessed=units * blocks * TOK * HD * 2,
        transcendentals=heads * blocks * blocks * TOK * TOK,
    )


def pack(plan, ranges, tensors):
    peers, units = len(plan), len(plan[0])
    widths = [count * HD for _, count in ranges]
    starts = [sum(widths[:r]) for r in range(len(ranges))]

    def place(h):
        for r, (head, count) in enumerate(ranges):
            if head <= h < head + count:
                return r, starts[r] + (h - head) * HD

    need = []
    for u in range(units):
        need.append(list(dict.fromkeys((plan[p][u][0], place(plan[p][u][1])[0]) for p in range(peers))))
    order = sorted(range(units), key=lambda u: (len(need[u]), u))
    fetch = list(dict.fromkeys(piece for u in order for piece in need[u]))

    def body(*refs):
        o_ref, rows, tiles, in_sem, out_sem = refs[len(tensors) :]
        copies = {}
        for n, (t, r) in enumerate(fetch):
            source = refs[t].at[0, :, pl.ds(ranges[r][0] * HD, widths[r])]
            target = rows.at[t, :, pl.ds(starts[r], widths[r])]
            copies[t, r] = pltpu.make_async_copy(source, target, in_sem.at[n])
            copies[t, r].start()
        sent = []
        for u in order:
            for piece in need[u]:
                if piece in copies:
                    copies.pop(piece).wait()
            for p in range(peers):
                t, h = plan[p][u]
                at = place(h)[1]
                tiles[p, u] = rows[t, :, at : at + HD]
            sent.append(pltpu.make_async_copy(tiles.at[:, u], o_ref.at[:, u], out_sem.at[u]))
            sent[-1].start()
        for copy in sent:
            copy.wait()

    return pl.pallas_call(
        body,
        in_specs=[pl.BlockSpec(memory_space=pl.ANY)] * len(tensors),
        out_specs=pl.BlockSpec(memory_space=pl.ANY),
        out_shape=jax.ShapeDtypeStruct((peers, units, TOK, HD), jnp.bfloat16),
        scratch_shapes=[
            pltpu.VMEM((len(tensors), TOK, sum(widths)), jnp.bfloat16),
            pltpu.VMEM((peers, units, TOK, HD), jnp.bfloat16),
            pltpu.SemaphoreType.DMA((len(fetch),)),
            pltpu.SemaphoreType.DMA((units,)),
        ],
        compiler_params=WHOLE,
        cost_estimate=cost(0, peers, 2 * units),
    )(*tensors)


def unpack(places, back):
    def body(x_ref, *o_refs):
        for o_ref, place in zip(o_refs, places):
            for h, (p, u) in enumerate(place):
                o_ref[0, :, h * HD : (h + 1) * HD] = x_ref[p, u]

    width = len(places[0]) * HD
    return pl.pallas_call(
        body,
        out_shape=[jax.ShapeDtypeStruct((1, TOK, width), jnp.bfloat16) for _ in places],
        compiler_params=LOCAL,
        cost_estimate=cost(0, 1, 4 * len(places[0])),
    )(back)


def student_kernel(blocks, first, role, arrived):
    def body(first_ref, role_ref, x_ref, o_ref):
        @pl.when(role_ref[0] == 1)
        def _():
            sources = [(x_ref, t) for t in range(3)]
            student_head(range(0, blocks, 2), first_ref[0], sources, o_ref, 0)

    return pl.pallas_call(
        body,
        in_specs=[SMEM, SMEM, VMEM],
        out_specs=VMEM,
        out_shape=jax.ShapeDtypeStruct((blocks, 1, TOK, HD), jnp.bfloat16),
        compiler_params=LOCAL,
        cost_estimate=cost(1, blocks, 4),
    )(first, role, arrived)


def rest_teacher(blocks, clips, role, arrived, offset, gen, shared):
    def body(clip_ref, role_ref, x_ref, gen_ref, shared_ref, o_ref):
        @pl.when(role_ref[0] == 1)
        def _():
            o_ref[...] = gen_ref[...]

        @pl.when(role_ref[0] == 2)
        def _():
            sources = [(x_ref, offset + t) for t in range(2)]
            teacher_head(
                blocks, range(blocks), clip_ref, sources, lambda at: shared_ref[at, 0], o_ref, 0
            )

    return pl.pallas_call(
        body,
        in_specs=[SMEM, SMEM, VMEM, VMEM, VMEM],
        out_specs=VMEM,
        out_shape=jax.ShapeDtypeStruct((blocks, 1, TOK, HD), jnp.bfloat16),
        compiler_params=LOCAL,
        cost_estimate=cost(1, blocks, 5),
    )(clips, role, arrived, gen, shared)


def slots_kernel(full, order, home, first, clips, where, arrived):
    blocks = len(order)

    def body(first_ref, clip_ref, where_ref, *refs):
        x_refs, o_refs, (x, y) = refs[:blocks], refs[blocks : 2 * blocks], refs[2 * blocks :]
        at = [where_ref[2] ^ d for d in order]
        for i in range(blocks):
            x[at[i]] = x_refs[i][...]

        for s in range(full):
            sources = [(x, 5 * s + t) for t in range(5)]
            student_head(range(0, blocks, 2), first_ref[0], sources[:3], y, 2 * s)
            gen = functools.partial(lambda u, at: y[at, u], 2 * s)
            teacher_whole_head(blocks, clip_ref, sources[3:], gen, y, 2 * s + 1)

        for i, d in enumerate(home):
            o_refs[i][...] = y[where_ref[2] ^ d]

    return pl.pallas_call(
        body,
        in_specs=[SMEM] * 3 + [VMEM] * blocks,
        out_specs=[VMEM] * blocks,
        out_shape=[jax.ShapeDtypeStruct((2 * full, TOK, HD), jnp.bfloat16)] * blocks,
        scratch_shapes=[
            pltpu.VMEM((blocks, 5 * full, TOK, HD), jnp.bfloat16),
            pltpu.VMEM((blocks, 2 * full, TOK, HD), jnp.bfloat16),
        ],
        compiler_params=LOCAL,
        cost_estimate=cost(2 * full, blocks, 7 * full),
    )(first, clips, where, *arrived)


def slots_pack(full, order, where, tensors):
    peers = len(order)

    def body(where_ref, *refs):
        o_refs, (rows, sems) = refs[5 : 5 + peers], refs[5 + peers :]
        copies = []
        for t in range(5):
            source = refs[t].at[0, :, pl.ds(0, full * peers * HD)]
            copies.append(pltpu.make_async_copy(source, rows.at[t], sems.at[t]))
            copies[-1].start()
        for t in range(5):
            copies[t].wait()
            for s in range(full):
                for i, d in enumerate(order):
                    at = pl.multiple_of((s * peers + (where_ref[2] ^ d)) * HD, HD)
                    o_refs[i][5 * s + t] = rows[t, :, pl.ds(at, HD)]

    return pl.pallas_call(
        body,
        in_specs=[SMEM] + [pl.BlockSpec(memory_space=pl.ANY)] * 5,
        out_specs=[VMEM] * peers,
        out_shape=[jax.ShapeDtypeStruct((5 * full, TOK, HD), jnp.bfloat16)] * peers,
        scratch_shapes=[
            pltpu.VMEM((5, TOK, full * peers * HD), jnp.bfloat16),
            pltpu.SemaphoreType.DMA((5,)),
        ],
        compiler_params=WHOLE,
        cost_estimate=cost(0, peers, 10 * full),
    )(where, *tensors)


def rest_pack(base, columns, column, tensors):
    def body(column_ref, *refs):
        rows, sems = refs[-2:]
        copies = []
        for t in range(5):
            source = refs[t].at[0, :, pl.ds(base * HD, columns * HD)]
            copies.append(pltpu.make_async_copy(source, rows.at[t], sems.at[t]))
            copies[-1].start()
        for t in range(5):
            copies[t].wait()
            for s in range(columns):
                at = pl.multiple_of((column_ref[0] ^ s) * HD, HD)
                refs[5 + s][(0, 1, 2, 4, 3)[t]] = rows[t, :, pl.ds(at, HD)]

    return pl.pallas_call(
        body,
        in_specs=[SMEM] + [pl.BlockSpec(memory_space=pl.ANY)] * 5,
        out_specs=[VMEM] * columns,
        out_shape=[jax.ShapeDtypeStruct((5, TOK, HD), jnp.bfloat16)] * columns,
        scratch_shapes=[
            pltpu.VMEM((5, TOK, columns * HD), jnp.bfloat16),
            pltpu.SemaphoreType.DMA((5,)),
        ],
        compiler_params=WHOLE,
        cost_estimate=cost(0, 1, 10 * columns),
    )(column, *tensors)


def rest_kernel(columns, first, clips, where, own, other):
    blocks = 2 * columns

    def body(first_ref, clip_ref, where_ref, *refs):
        x, gen = refs[-2:]
        column, side = where_ref[0], where_ref[1]
        mine = [2 * (column ^ s) + side for s in range(columns)]
        for s in range(columns):
            x[mine[s]] = refs[s][...]
            x[mine[s] ^ 1, 0:4] = refs[columns + s][...]
        sources = [(x, t) for t in (0, 1, 2, 4, 3)]
        student_head(range(0, blocks, 2), first_ref[0], sources[:3], gen, 0)
        at_gen = lambda at: gen[at, 0]
        for s in range(columns):
            o_ref = refs[2 * columns + s]
            o_ref[0:1] = gen[mine[s]]
            teacher_head(blocks, [mine[s]], clip_ref, sources[3:], at_gen, o_ref, None)

    return pl.pallas_call(
        body,
        in_specs=[SMEM] * 3 + [VMEM] * (2 * columns),
        out_specs=[VMEM] * columns,
        out_shape=[jax.ShapeDtypeStruct((2, TOK, HD), jnp.bfloat16)] * columns,
        scratch_shapes=[
            pltpu.VMEM((blocks, 5, TOK, HD), jnp.bfloat16),
            pltpu.VMEM((blocks, 1, TOK, HD), jnp.bfloat16),
        ],
        compiler_params=LOCAL,
        cost_estimate=cost(0, 1, 1),
    )(first, clips, where, *own, *other)


def join(full, order, columns, where, slots, rests):
    peers = len(order)

    def body(where_ref, *refs):
        for i, o_ref in enumerate(refs[peers + columns :]):

            def put(h, tile):
                o_ref[0, :, pl.ds(pl.multiple_of(h * HD, HD), HD)] = tile

            for n, d in enumerate(order):
                for s in range(full):
                    put(s * peers + (where_ref[2] ^ d), refs[n][2 * s + i])
            for s in range(columns):
                put(full * peers + (where_ref[0] ^ s), refs[peers + s][i])

    width = (full * peers + columns) * HD
    return pl.pallas_call(
        body,
        in_specs=[SMEM] + [VMEM] * (peers + columns),
        out_specs=[VMEM] * 2,
        out_shape=[jax.ShapeDtypeStruct((1, TOK, width), jnp.bfloat16)] * 2,
        compiler_params=LOCAL,
        cost_estimate=cost(0, 1, 4 * width // HD),
    )(where, *slots, *rests)


def by_slots_and_columns(tensors, peers, full, rest, first, clips):
    here = lax.axis_index("tm")
    where = jnp.stack([here // 2, here % 2, here]).astype(jnp.int32)

    def swapped(x, by):
        return lax.ppermute(x, "tm", [(i, i ^ by) for i in range(peers)]) if by else x

    far = list(range(rest, peers))
    near = sorted(range(1, rest), key=lambda d: (d % 2, d))
    there = [far[0], near[0], far[1], *near[1:], *far[2:], 0]
    home = [*range(1, peers), 0]

    pieces = rest_pack(full * peers, rest, where[:1], tensors)
    own = [swapped(x, 2 * s) for s, x in enumerate(pieces)]
    packed = slots_pack(full, there, where, tensors)
    arrived = [swapped(x, d) for x, d in zip(packed, there)]
    other = [swapped(x[:4], 1) for x in own]
    pieces = rest_kernel(rest, first, clips, where, own, other)
    arrived, pieces = lax.optimization_barrier((arrived, pieces))
    rests = [swapped(x, 2 * s) for s, x in enumerate(pieces)]
    results = slots_kernel(full, there, home, first, clips, where, arrived)
    results, rests = lax.optimization_barrier((results, rests))
    slots = [swapped(x, d) for x, d in zip(results, home)]
    return tuple(join(full, home, rest, where, slots, rests))


def by_roles(tensors, peers, heads, first, clips):
    here = lax.axis_index("tm")
    role = jnp.where(here < 2 * heads, 1 + here % 2, 0).astype(jnp.int32)[None]
    plan = [
        [(t, min(p // 2, heads - 1)) for t in ((3, 4, 4) if p % 2 else (0, 1, 2))]
        for p in range(peers)
    ]
    arrived = lax.all_to_all(pack(plan, [(0, heads)], tensors), "tm", 0, 0)
    gen = student_kernel(peers, first, role, arrived)
    shared = lax.ppermute(gen, "tm", [(2 * r, 2 * r + 1) for r in range(heads)])
    results = rest_teacher(peers, clips, role, arrived, 0, gen, shared)
    back = lax.all_to_all(results, "tm", 0, 0)
    return tuple(unpack([[(2 * r + i, 0) for r in range(heads)] for i in (0, 1)], back))


def per_device(student_q, student_k, student_v, teacher_q, teacher_k, stagger, clip_lengths):
    heads = student_q.shape[2] // HD
    peers = lax.axis_size("tm")
    full, rest = divmod(heads, peers)
    running = jnp.cumsum(clip_lengths[0])
    block = jnp.arange(peers, dtype=jnp.int32)
    before = running[None, :] <= block[:, None]
    low = jnp.max(jnp.where(before, running[None, :], 0), axis=1)
    high = jnp.min(jnp.where(before, peers, running[None, :]), axis=1)
    large = jnp.where(clip_lengths[0] == peers // 2 + 1, running - clip_lengths[0], 0)
    large = jnp.broadcast_to(jnp.max(large), (peers,))
    clips = jnp.stack([low, high, large]).astype(jnp.int32)
    tensors = (student_q, student_k, student_v, teacher_q, teacher_k)
    if full == 0:
        assert 2 * rest <= peers
        return by_roles(tensors, peers, rest, stagger, clips)
    assert peers == 2 * rest and rest & (rest - 1) == 0
    return by_slots_and_columns(tensors, peers, full, rest, stagger, clips)


def solution(mesh):
    spec = P("seq", "tm", "mp")
    return jax.shard_map(
        per_device,
        mesh=mesh,
        in_specs=(spec,) * 5 + (P("seq"), P("seq", None)),
        out_specs=(spec, spec),
        check_vma=False,
    )
```
